32 devices in a mesh: dp: 16 (over z, y, x), fsdp: 2 (over core).
Axes of the slice: x: 2, y: 2, z: 4, core: 2. Of those that a mesh axis runs over, the one named last changes fastest.
Arguments:
- tokens: bfloat16 [16, 512, 1024], P('dp', 'fsdp'), may hold values from -6 to 6
- document_index: int32 [16, 512], P('dp'), may hold values from 0 to 3, never falling along the last dimension, each value on 1 to 256 neighbouring positions
- loss_token_mask: int32 [16, 512], P('dp', 'fsdp'), may hold values 0 or 1
- cotangent: bfloat16 [16, 512, 1024], P('dp', 'fsdp'), may hold values from -6 to 6
- first_gain: bfloat16 [1024], P(('dp', 'fsdp')), may hold values from 0.5 to 1.5
- mixer_in: bfloat16 [1024, 3072], P(('dp', 'fsdp')), may hold values from -0.1875 to 0.1875
- conv_kernel: bfloat16 [3, 1024], P(None, ('dp', 'fsdp')), may hold values from -3.5 to 3.5
- mixer_out: bfloat16 [1024, 1024], P(('dp', 'fsdp')), may hold values from -0.1875 to 0.1875
- second_gain: bfloat16 [1024], P(('dp', 'fsdp')), may hold values from 0.5 to 1.5
- gate_weight: bfloat16 [1024, 4608], P(('dp', 'fsdp')), may hold values from -0.1875 to 0.1875
- up_weight: bfloat16 [1024, 4608], P(('dp', 'fsdp')), may hold values from -0.1875 to 0.1875
- down_weight: bfloat16 [4608, 1024], P(('dp', 'fsdp')), may hold values from -0.09375 to 0.09375
Outputs:
- block_out: bfloat16 [16, 512, 1024], P('dp', 'fsdp')
- input_grad: float32 [16, 512, 1024], P('dp', 'fsdp')
- first_gain_grad: float32 [1024], P(('dp', 'fsdp'))
- mixer_in_grad: float32 [1024, 3072], P(('dp', 'fsdp'))
- conv_kernel_grad: float32 [3, 1024], P(None, ('dp', 'fsdp'))
- mixer_out_grad: float32 [1024, 1024], P(('dp', 'fsdp'))
- second_gain_grad: float32 [1024], P(('dp', 'fsdp'))
- gate_grad: float32 [1024, 4608], P(('dp', 'fsdp'))
- up_grad: float32 [1024, 4608], P(('dp', 'fsdp'))
- down_grad: float32 [4608, 1024], P(('dp', 'fsdp'))
The draws below stay inside these ranges and needn't reach their ends.
Inputs may be any that keep to these rules, and one draw needn't show every extreme that they name: `document_index`: within a row the ids never fall and each of 0 to 3 forms one run; the longest run holds 256 tokens.
All inputs are finite; a program needn't handle non-finite values. No bound on the sum of `loss_token_mask` on one device may be relied on, other than what follows from the above.
Results may differ from the reference program's by a relative error of at most 0.0086.
Values may be sent and summed in bfloat16 or wider, within the bound.
A program may use at most 256 MiB of HBM per device.

```python
import math
import jax
import jax.numpy as jnp
import numpy as np
from jax import lax

MODEL_DIMENSION = 1024
FF = 4608
KW = 3
TOTAL_ROWS = 16
ROW_LENGTH = 512
DOCS_PER_ROW = 4
LONGEST_DOC_LEN = 256


def place_ends(entries, stream_key, smallest, top_value):
    index_at = [jax.random.randint(jax.random.fold_in(stream_key, axis), (), 0, length) for axis, length in enumerate(entries.shape)]
    longest = entries.shape.index(max(entries.shape))
    beside = index_at[:longest] + [(index_at[longest] + 1) % entries.shape[longest]] + index_at[longest + 1:]
    return entries.at[tuple(index_at)].set(smallest).at[tuple(beside)].set(top_value)


def block_levels(own_key, shape, cuts, least, largest):
    gain = 1.0
    for position, shards_of in cuts:
        draws = jax.random.uniform(jax.random.fold_in(jax.random.fold_in(own_key, 6), position), (shards_of,), jnp.float32, least / len(cuts), largest / len(cuts))
        gain = gain * jnp.repeat(jnp.exp(draws), shape[position] // shards_of).reshape((-1,) + (1,) * (len(shape) - 1 - position))
    return gain


def length_profile(amount, total, bound, slope):
    portions = [(1 << 20) // math.isqrt(grade ** slope) + 1 for grade in range(2, amount + 1)]
    surplus, given = total - bound - (amount - 1), [1] * (amount - 1)
    while surplus > 0:
        free = [i for i in range(amount - 1) if given[i] < bound]
        pool, left = sum([portions[i] for i in free]), surplus
        for i in free:
            addition = min(bound - given[i], max(1, left * portions[i] // pool), surplus)
            given[i] = given[i] + addition
            surplus = surplus - addition
    return np.array([bound] + given)


def uneven_parts(key, number_of, total, limit, slope):
    if number_of == 2:
        one = jax.random.randint(key, (), max(1, total - limit), min(limit, total - 1) + 1)
        return jnp.stack([one, total - one])
    lengths = jnp.asarray(length_profile(number_of, total, limit, slope), jnp.int32)
    pairs = (number_of - 1) // 2
    donor, sink = lengths[1:1 + 2 * pairs:2], lengths[2:2 + 2 * pairs:2]
    margin = jnp.minimum(donor - 1, limit - sink)
    passed = jax.random.randint(jax.random.fold_in(key, 1), (pairs,), 0, 1 << 20) % (margin + 1)
    lengths = lengths.at[1:1 + 2 * pairs:2].set(donor - passed).at[2:2 + 2 * pairs:2].set(sink + passed)
    return lengths[jax.random.permutation(jax.random.fold_in(key, 2), number_of)]


def centred(rng, dims, scale, reach, cuts=(), kind=jnp.bfloat16):
    values = scale * jax.random.normal(rng, dims, jnp.float32)
    if cuts:
        values = values * block_levels(rng, dims, cuts, -0.22, 0.18)
    return jnp.clip(values, -reach, reach).astype(kind)


def setup_inputs(seed: int = 0) -> dict:
    splits = jax.random.split(jax.random.key(seed), 13)
    return {
        "tokens": centred(splits[0], (TOTAL_ROWS, ROW_LENGTH, MODEL_DIMENSION), 1.0, 6.0, ((0, 16), (1, 2))),
        "document_index": jax.vmap(lambda own: jnp.searchsorted(jnp.cumsum(uneven_parts(own, DOCS_PER_ROW, ROW_LENGTH, LONGEST_DOC_LEN, 2)), jnp.arange(ROW_LENGTH), side="right"))(jax.random.split(splits[1], TOTAL_ROWS)).reshape((TOTAL_ROWS, ROW_LENGTH)).astype(jnp.int32),
        "loss_token_mask": place_ends((jax.random.randint(splits[2], (TOTAL_ROWS, ROW_LENGTH), 0, 8) < 7).astype(jnp.int32), jax.random.fold_in(splits[2], 1), 0, 1),
        "cotangent": centred(splits[3], (TOTAL_ROWS, ROW_LENGTH, MODEL_DIMENSION), 1.0, 6.0, ((0, 16), (1, 2))),
        "first_gain": jnp.clip(1.0 + 0.1 * jax.random.normal(splits[4], (MODEL_DIMENSION,), jnp.float32), 0.5, 1.5).astype(jnp.bfloat16),
        "mixer_in": centred(splits[5], (MODEL_DIMENSION, 3 * MODEL_DIMENSION), MODEL_DIMENSION ** -0.5, 0.1875, ((0, 32),)),
        "conv_kernel": centred(splits[6], (KW, MODEL_DIMENSION), KW ** -0.5, 3.5, ((1, 32),)),
        "mixer_out": centred(splits[7], (MODEL_DIMENSION, MODEL_DIMENSION), MODEL_DIMENSION ** -0.5, 0.1875, ((0, 32),)),
        "second_gain": jnp.clip(1.0 + 0.1 * jax.random.normal(splits[8], (MODEL_DIMENSION,), jnp.float32), 0.5, 1.5).astype(jnp.bfloat16),
        "gate_weight": centred(splits[9], (MODEL_DIMENSION, FF), MODEL_DIMENSION ** -0.5, 0.1875, ((0, 32),)),
        "up_weight": centred(splits[10], (MODEL_DIMENSION, FF), MODEL_DIMENSION ** -0.5, 0.1875, ((0, 32),)),
        "down_weight": centred(splits[11], (FF, MODEL_DIMENSION), FF ** -0.5, 0.09375, ((0, 32),)),
    }


EPSILON = 1e-05

@jax.custom_vjp
def low(v):
    return lax.optimization_barrier(v.astype(jnp.bfloat16)).astype(jnp.float32)

@jax.custom_vjp
def low_back(v):
    return v

def low_keep(v):
    return (low(v), None)

def low_pass(kept, grad):
    return (grad,)

def back_keep(v):
    return (v, None)

def back_low(kept, grad):
    return (low(grad),)
low.defvjp(low_keep, low_pass)
low_back.defvjp(back_keep, back_low)

def matmul(left_side, right_side):
    return jnp.dot(left_side, right_side, precision=lax.Precision.HIGHEST)

def inverse_rms(values):
    return lax.rsqrt(lax.optimization_barrier(jnp.mean(values * values, axis=-1, keepdims=True)) + EPSILON)

def block_forward(stream, same_one, same_two, first_gain, mixer_in, conv_kernel, mixer_out, second_gain, gate_weight, up_weight, down_weight):
    model_width = stream.shape[1]
    normed_one = stream * inverse_rms(stream)
    hidden_one = low(normed_one * first_gain)
    projected = low_back(matmul(hidden_one, mixer_in))
    before_gate = projected[:, :model_width]
    after_gate = projected[:, model_width:2 * model_width]
    mixed_in = projected[:, 2 * model_width:]
    conv_input = before_gate * mixed_in
    zero_row = jnp.zeros((1, model_width), jnp.float32)
    back_one = jnp.concatenate([zero_row, conv_input[:-1]], axis=0)
    back_two = jnp.concatenate([zero_row, zero_row, conv_input[:-2]], axis=0)
    conv_result = conv_kernel[2] * conv_input + conv_kernel[1] * same_one[:, None] * back_one + conv_kernel[0] * same_two[:, None] * back_two
    mixer_act = low(after_gate * conv_result)
    second = stream + low_back(matmul(mixer_act, mixer_out))
    normed_two = second * inverse_rms(second)
    hidden_two = low(normed_two * second_gain)
    gate_pre = low_back(matmul(hidden_two, gate_weight))
    up_pre = low_back(matmul(hidden_two, up_weight))
    inner_act = low(jax.nn.silu(gate_pre) * up_pre)
    return second + low_back(matmul(inner_act, down_weight))

def reference(tokens, document_index, loss_token_mask, cotangent, first_gain, mixer_in, conv_kernel, mixer_out, second_gain, gate_weight, up_weight, down_weight):
    weights = tuple((item.astype(jnp.float32) for item in (first_gain, mixer_in, conv_kernel, mixer_out, second_gain, gate_weight, up_weight, down_weight)))
    all_tokens = tokens.shape[0] * tokens.shape[1]

    def one_row(running, row_data):
        row_tokens, row_segments, row_mask, row_cotangent = row_data
        same_one = jnp.concatenate([jnp.zeros((1,), jnp.float32), (row_segments[1:] == row_segments[:-1]).astype(jnp.float32)])
        same_two = jnp.concatenate([jnp.zeros((2,), jnp.float32), (row_segments[2:] == row_segments[:-2]).astype(jnp.float32)])

        def forward(stream, *params):
            return block_forward(stream, same_one, same_two, *params)
        result, pullback = jax.vjp(forward, row_tokens.astype(jnp.float32), *weights)
        upstream = row_cotangent.astype(jnp.float32) * row_mask.astype(jnp.float32)[:, None]
        gradients = pullback(upstream)
        running = tuple((total_part + grad_part for total_part, grad_part in zip(running, gradients[1:])))
        return (running, (result.astype(jnp.bfloat16), gradients[0]))
    initial = tuple((jnp.zeros_like(item) for item in weights))
    totals, (outputs, input_grads) = lax.scan(one_row, initial, (tokens, document_index, loss_token_mask, cotangent))
    factor = lax.rsqrt(jnp.asarray(all_tokens, jnp.float32))
    scaled = tuple((item * factor for item in totals))
    return (outputs, input_grads, scaled[0], scaled[1], scaled[2], scaled[3], scaled[4], scaled[5], scaled[6], scaled[7])
```

```python
import functools
import math

import jax
import jax.numpy as jnp
from jax import lax
from jax.experimental import pallas as pl
from jax.experimental.pallas import tpu as pltpu
from jax.sharding import PartitionSpec as P

EPSILON = 1e-05
MESH = pl.DeviceIdType.MESH
F32 = jnp.float32
BF16 = jnp.bfloat16
PLACES = 32


def nn(a, b):
    return jnp.dot(a, b, preferred_element_type=F32)


def nt(a, b):
    return lax.dot_general(a, b, (((1,), (1,)), ((), ())), preferred_element_type=F32)


def tn(a, b):
    return lax.dot_general(a, b, (((0,), (0,)), ((), ())), preferred_element_type=F32)


def kernel(
    fsdp_count,
    copies_of_place,
    factor,
    tokens,
    cotangent,
    document,
    loss_mask,
    gain_one,
    gain_two,
    taps,
    mixer_in,
    mixer_out,
    gate,
    up,
    down,
    block_out,
    input_grad,
    small_out,
    mixer_in_grad,
    mixer_out_grad,
    gate_grad,
    up_grad,
    down_grad,
    small_tile,
    small_all,
    small_grad,
    small_in,
    w_mi,
    w_mo,
    w_gu,
    w_dn,
    mi_stage,
    gu_stage,
    xs,
    flags,
    gs,
    hs,
    proj,
    ubuf,
    conv,
    ys,
    dps,
    x2,
    o_send,
    o_recv,
    pre,
    dm_buf,
    ms,
    dabs,
    acc,
    dhp,
    dh_a,
    dh_b,
    dh_x,
    dh_y,
    dos,
    r_gu_c,
    r_gu_0,
    r_gu_1,
    r_dn_c,
    r_dn_0,
    r_dn_1,
    r_mi_c,
    r_mi_y,
    r_mi_0,
    r_mi_1,
    r_mo_c,
    r_mo_y,
    r_mo_0,
    r_mo_1,
    rows_buf,
    send,
    recv,
    load_sem,
    store_sem,
    small_send,
    small_recv,
    back_send,
    back_recv,
    free_x,
    free_y,
):
    toks, width = tokens.shape
    dkbuf = pre
    rows = mixer_in.shape[0]
    half_width = width // 2
    units = w_dn.shape[0] * w_dn.shape[1] * w_dn.shape[2] * w_dn.shape[3]
    part = units // 3
    half = toks // 2
    step = 32

    dp, fs = lax.axis_index("dp"), lax.axis_index("fsdp")
    number = dp * fsdp_count + fs
    v = lax.div(number, copies_of_place)
    rep = lax.rem(number, copies_of_place)
    c = lax.rem(v, 2)
    x = lax.rem(lax.div(v, 2), 2)
    y = lax.rem(lax.div(v, 4), 2)
    z0 = lax.rem(lax.div(v, 8), 2)
    z1 = lax.div(v, 16)
    p = 2 * y + x
    px = 2 * y + (1 - x)
    py = 2 * (1 - y) + x
    pd = 2 * (1 - y) + (1 - x)

    def dev(place):
        whole = place * copies_of_place + rep
        return (lax.div(whole, fsdp_count), lax.rem(whole, fsdp_count))

    cn = dev(v + (1 - 2 * c))
    xn = dev(v + 2 * (1 - 2 * x))
    yn = dev(v + 4 * (1 - 2 * y))
    dn = dev(v + 2 * (1 - 2 * x) + 4 * (1 - 2 * y))
    z0n = dev(v + 8 * (1 - 2 * z0))
    z1n = dev(v + 16 * (1 - 2 * z1))
    following = (dp, lax.rem(fs + 1, fsdp_count))
    preceding = (dp, lax.rem(fs + fsdp_count - 1, fsdp_count))

    counter = [0]
    started = []

    def remote(src, dst, target):
        at = counter[0]
        counter[0] += 1
        return pltpu.make_async_remote_copy(
            src_ref=src, dst_ref=dst, send_sem=send.at[at], recv_sem=recv.at[at],
            device_id=target, device_id_type=MESH,
        )

    def go(copy):
        copy.start()
        started.append(copy)
        return copy

    def same(ref, target):
        return remote(ref, ref, target)

    def sent(copy):
        copy.wait_send()
        started[:] = [other for other in started if other is not copy]

    barrier = pltpu.get_barrier_semaphore()

    def greet(m, _):
        pl.semaphore_signal(
            barrier, inc=1, device_id=dev(lax.rem(v + m, PLACES)), device_id_type=MESH
        )
        return 0

    lax.fori_loop(1, PLACES, greet, 0)
    pl.semaphore_signal(barrier, inc=1, device_id=following, device_id_type=MESH)
    pl.semaphore_signal(barrier, inc=1, device_id=preceding, device_id_type=MESH)

    load_out = pltpu.make_async_copy(mixer_out, w_mo.at[z1, z0, y, c], load_sem.at[0])
    load_down = pltpu.make_async_copy(down, w_dn.at[z1, z0, c], load_sem.at[1])
    load_cot = pltpu.make_async_copy(cotangent, gs.at[p], load_sem.at[2])
    load_out.start()
    load_down.start()
    load_cot.start()

    lane = lax.broadcasted_iota(jnp.int32, (1, 128), 1)
    mine = lax.div(lane, 32) == lax.rem(v, 4)
    small_tile[...] = jnp.zeros_like(small_tile)

    def spread(values):
        wide = jnp.concatenate([values.astype(F32)] * 4, axis=1)
        return jnp.where(mine, wide, 0.0)

    small_tile[0:1, :] = spread(gain_one[...])
    small_tile[1:2, :] = spread(gain_two[...])
    small_tile[2:5, :] = spread(taps[...])

    lanes128 = lax.broadcasted_iota(jnp.int32, (rows, 128), 1)
    low = lanes128 < 64
    for b in range(3):
        for q in range(width // 256):
            at = b * width + 256 * q
            even = mixer_in[:, at : at + 128].astype(F32)
            odd = mixer_in[:, at + 128 : at + 256].astype(F32)
            to = b * half_width + 128 * q
            mi_stage[0, :, to : to + 128] = jnp.where(low, even, pltpu.roll(odd, 64, 1)).astype(BF16)
            mi_stage[1, :, to : to + 128] = jnp.where(low, pltpu.roll(even, 64, 1), odd).astype(BF16)
    w_mi[z1, z0, y, x, c] = mi_stage[x]
    small_all[v] = small_tile[...]

    pl.semaphore_wait(barrier, PLACES + 1)

    mi_swap = go(remote(mi_stage.at[1 - x], w_mi.at[z1, z0, y, x, c], xn))

    def small_copy(src, dst, m, sems=(small_send, small_recv)):
        return pltpu.make_async_remote_copy(
            src_ref=src, dst_ref=dst, send_sem=sems[0].at[m], recv_sem=sems[1].at[m],
            device_id=dev(lax.rem(v + m, PLACES)), device_id_type=MESH,
        )

    def small_start(m, _):
        small_copy(small_tile, small_all.at[v], m).start()
        return 0

    lax.fori_loop(1, PLACES, small_start, 0)
    tok_swap = go(remote(tokens, xs.at[x], xn))

    def mo_at(a, b, yy, cc):
        return w_mo.at[a, b, yy, cc]

    def mi_at(a, b, yy, cc):
        return w_mi.at[a, b, yy, :, cc]

    def mix_gather(at):
        return dict(
            s1=same(at(z1, z0, y, c), z1n),
            s2=same(at(z1, z0, y, c), z0n),
            s3=same(at(1 - z1, z0, y, c), z0n),
            y0=same(at(z1, z0, y, c), yn),
            y1=same(at(1 - z1, z0, y, c), yn),
            y2=same(at(z1, 1 - z0, y, c), yn),
            y3=same(at(1 - z1, 1 - z0, y, c), yn),
        )

    mo_g, mi_g = mix_gather(mo_at), mix_gather(mi_at)
    load_out.wait()
    for name in ("s1", "s2", "y0"):
        go(mo_g[name])
    mi_swap.wait_recv()
    for name in ("s1", "s2", "y0"):
        go(mi_g[name])

    offset = fs * toks
    ids = document[...].astype(F32) + 1.0
    mask_row = loss_mask[...].astype(F32)
    id_lane = lax.broadcasted_iota(jnp.int32, (step, ids.shape[1]), 1)
    id_row = lax.broadcasted_iota(jnp.int32, (step, ids.shape[1]), 0)
    ma_lane = lax.broadcasted_iota(jnp.int32, (step, toks), 1)
    ma_row = lax.broadcasted_iota(jnp.int32, (step, toks), 0)
    fl_lane = lax.broadcasted_iota(jnp.int32, (step, 128), 1)

    def flag_rows(i, _):
        base = i * step
        at = pl.ds(pl.multiple_of(base, step), step)

        def column(shift):
            hit = id_lane == id_row + (offset + base + shift)
            return jnp.sum(jnp.where(hit, ids, 0.0), axis=1, keepdims=True)

        centre = column(0)
        tile = jnp.zeros((step, 128), F32)
        for k, shift in enumerate((-1, -2, 1, 2)):
            tile = jnp.where(
                jnp.logical_and(fl_lane == k, column(shift) == centre), 1.0, tile
            )
        flags[x, at, :] = tile.astype(BF16)
        keep = jnp.sum(
            jnp.where(ma_lane == ma_row + base, mask_row, 0.0), axis=1, keepdims=True
        )
        gs[p, at, :] = (gs[p, at, :].astype(F32) * keep).astype(BF16)
        return 0

    load_cot.wait()
    lax.fori_loop(0, toks // step, flag_rows, 0)
    flag_swap = go(same(flags.at[x], xn))
    xs[x] = tokens[...]

    run = units // 4
    def pick(ref, at_p):
        whole = ref[...].astype(F32)
        return jnp.concatenate(
            [whole[:, run * (4 * z + at_p) : run * (4 * z + at_p) + run] for z in range(4)], axis=1
        ).astype(BF16)

    for at_p in range(4):
        picked_gate, picked_up = pick(gate, at_p), pick(up, at_p)
        for j in range(3):
            gu_stage[at_p, j, :, 0:part] = picked_gate[:, j * part : j * part + part]
            gu_stage[at_p, j, :, part:] = picked_up[:, j * part : j * part + part]
    for j in range(3):
        w_gu[j, z1, z0, p, c] = gu_stage[p, j]

    def forward(g, arrived, names):
        g[arrived].wait_recv()
        for name in names:
            go(g[name])

    for g in (mo_g, mi_g):
        forward(g, "s1", ("s3", "y1"))
        forward(g, "s2", ("y2",))
        forward(g, "s3", ("y3",))

    gu_swap = [
        go(remote(gu_stage.at[px], w_gu.at[:, z1, z0, p, c], xn)),
        go(remote(gu_stage.at[py], w_gu.at[:, z1, z0, p, c], yn)),
        go(remote(gu_stage.at[pd], w_gu.at[:, z1, z0, p, c], dn)),
    ]

    def z_gather(at):
        return dict(
            s1=same(at(z1, z0, c), z1n),
            s2=same(at(z1, z0, c), z0n),
            s3=same(at(1 - z1, z0, c), z0n),
            core=same(at(slice(None), slice(None), c), cn),
        )

    dn_g = z_gather(lambda a, b, cc: w_dn.at[a, b, cc])
    gu_g = [z_gather(lambda a, b, cc, j=j: w_gu.at[j, a, b, :, cc]) for j in range(3)]
    load_down.wait()
    go(dn_g["s1"])
    go(dn_g["s2"])

    def plane_gather(buf):
        lo, hi = pl.ds(0, half), pl.ds(half, half)
        g = dict(
            x0=same(buf.at[p, lo], xn),
            y1=same(buf.at[p, hi], yn),
            x1=same(buf.at[p, hi], xn),
            y0=same(buf.at[p, lo], yn),
            fx=same(buf.at[px, lo], yn),
            fy=same(buf.at[py, hi], xn),
        )
        for name in ("x0", "y1", "x1", "y0"):
            go(g[name])
        return g

    def plane_forward(g):
        forward(g, "x0", ("fx",))
        forward(g, "y1", ("fy",))

    gs_g = plane_gather(gs)

    def small_wait(m, _):
        copy = small_copy(small_tile, small_all.at[v], m)
        copy.wait()
        return 0

    lax.fori_loop(1, PLACES, small_wait, 0)
    natural = []
    for q in range(8):
        natural.append(
            small_all[4 * q] + small_all[4 * q + 1] + small_all[4 * q + 2] + small_all[4 * q + 3]
        )
    for q in range(8):
        rows_buf[:, 128 * q : 128 * q + 128] = natural[q]
    low8 = lax.broadcasted_iota(jnp.int32, (8, 128), 1) < 64
    is_one = x == 1
    for q in range(4):
        even, odd = natural[2 * q], natural[2 * q + 1]
        first = jnp.where(low8, even, pltpu.roll(odd, 64, 1))
        second = jnp.where(low8, pltpu.roll(even, 64, 1), odd)
        rows_buf[:, width + 128 * q : width + 128 * q + 128] = jnp.where(is_one, second, first)
    g1 = rows_buf[0:1, 0:width]
    g2 = rows_buf[1:2, 0:width]
    tap0 = rows_buf[2:3, width : width + half_width]
    tap1 = rows_buf[3:4, width : width + half_width]
    tap2 = rows_buf[4:5, width : width + half_width]

    def inverse_rms(values):
        return lax.rsqrt(jnp.mean(values * values, axis=1, keepdims=True) + EPSILON)

    def loop(count, body):
        def wrapped(i, _):
            body(pl.ds(pl.multiple_of(i * step, step), step))
            return 0

        lax.fori_loop(0, count // step, wrapped, 0)

    def hidden_one(s):
        def body(at):
            values = xs[s, at, :].astype(F32)
            xs[s, at, :] = (values * inverse_rms(values) * g1).astype(BF16)

        loop(toks, body)

    hidden_one(x)
    tok_swap.wait_recv()
    hidden_one(1 - x)

    for g in (mo_g, mi_g):
        for name in ("y0", "y1", "y2", "y3"):
            g[name].wait_recv()
    every = slice(None)
    mo_core = go(same(w_mo.at[:, :, :, c], cn))
    mi_core = go(same(w_mi.at[:, :, :, :, c], cn))
    mi_core.wait_recv()
    h1 = xs[...].reshape(2 * toks, width)
    wide = 3 * half_width
    proj[...] = nn(h1, w_mi[...].reshape(width, wide)).reshape(2, toks, wide)

    for s in range(2):
        def body(at, s=s):
            ubuf[s, pl.ds(pl.multiple_of(at.start + 8, 8), step), :] = (
                proj[s, at, 0:half_width] * proj[s, at, 2 * half_width :]
            )

        loop(toks, body)
    halo = go(remote(ubuf.at[:, pl.ds(toks, 8), :], ubuf.at[:, pl.ds(0, 8), :], following))
    flag_swap.wait_recv()
    halo.wait_recv()
    for s in range(2):
        for i in range(toks // step):
            a = i * step
            fl = flags[s, a : a + step, :].astype(F32)
            value = (
                tap2 * ubuf[s, a + 8 : a + 8 + step, :]
                + tap1 * (fl[:, 0:1] * ubuf[s, a + 7 : a + 7 + step, :])
                + tap0 * (fl[:, 1:2] * ubuf[s, a + 6 : a + 6 + step, :])
            )
            conv[s, a : a + step, :] = value
            ys[s, a : a + step, :] = (
                proj[s, a : a + step, half_width : 2 * half_width] * value
            ).astype(BF16)
    mo_core.wait_recv()
    mo_flat = w_mo[...].reshape(half_width, width)
    o_send[...] = nn(ys[1 - x], mo_flat).astype(BF16)
    o_swap = go(remote(o_send, o_recv, xn))
    x2[...] = nn(ys[x], mo_flat)

    def z_forward(g):
        forward(g, "s1", ("s3",))

    def z_core(g):
        g["s2"].wait_recv()
        g["s3"].wait_recv()
        go(g["core"])

    z_forward(dn_g)
    plane_forward(gs_g)
    for copy in gu_swap:
        copy.wait_recv()
        sent(copy)
    sent(mi_swap)
    go(gu_g[0]["s1"])
    go(gu_g[0]["s2"])
    z_core(dn_g)

    o_swap.wait_recv()

    def second_body(at):
        values = tokens[at, :].astype(F32) + x2[at, :] + o_recv[at, :].astype(F32)
        x2[at, :] = values
        hs[p, at, :] = (values * inverse_rms(values) * g2).astype(BF16)

    loop(toks, second_body)
    hs_g = plane_gather(hs)
    z_forward(gu_g[0])
    go(gu_g[1]["s1"])
    go(gu_g[1]["s2"])
    plane_forward(hs_g)
    z_core(gu_g[0])
    z_forward(gu_g[1])
    go(gu_g[2]["s1"])
    go(gu_g[2]["s2"])

    ya, yb = 2 * y, 2 * (1 - y)

    def plane_pair(g, names):
        for name in names:
            g[name].wait_recv()

    def pair_rows(ref, base):
        return ref[pl.ds(base, 2)].reshape(2 * toks, width)

    def feed(j, base):
        w = w_gu[j].reshape(width, 2 * part)
        pre[:, 0:toks, :] = nn(pair_rows(hs, base), w).reshape(2, toks, 2 * part)
        down_rows = w_dn[...].reshape(units, width)[j * part : j * part + part]
        dm_buf[...] = nt(pair_rows(gs, base), down_rows)

        def body(i, _):
            at = pl.ds(pl.multiple_of(i * step, step), step)
            slot = base + lax.div(i, toks // step)
            inner = pl.ds(pl.multiple_of(lax.rem(i, toks // step) * step, step), step)
            which = lax.div(i, toks // step)
            a = pre[which, inner, 0:part]
            b = pre[which, inner, part:]
            d = dm_buf[at, :]
            sg = jax.nn.sigmoid(a)
            silu = a * sg
            ms[slot, inner, j * part : j * part + part] = (silu * b).astype(BF16)
            dabs[j, slot, inner, 0:part] = (d * b * sg * (1.0 + a * (1.0 - sg))).astype(BF16)
            dabs[j, slot, inner, part:] = (d * silu).astype(BF16)
            return 0

        lax.fori_loop(0, 2 * toks // step, body, 0)
        back = nt(dabs[j, pl.ds(base, 2)].reshape(2 * toks, 2 * part), w)
        back = back.reshape(2, toks, width)
        if j == 0:
            acc[pl.ds(base, 2)] = back
        elif j == 1:
            acc[pl.ds(base, 2)] += back
        else:
            total = acc[pl.ds(base, 2)] + back
            acc[pl.ds(base, 2)] = total
            dhp[pl.ds(base, 2)] = total.astype(BF16)

    def gu_weight_grad(j):
        w_gu[j] = (
            tn(hs[...].reshape(4 * toks, width), dabs[j].reshape(4 * toks, 2 * part))
            .astype(BF16)
            .reshape(w_gu.shape[1:])
        )

    def plane_scatter(buf, r_a, r_b, r_x, r_y):
        lo, hi = pl.ds(0, half), pl.ds(half, half)
        return dict(
            a=remote(buf.at[pd, lo], r_a, xn),
            b=remote(buf.at[pd, hi], r_b, yn),
            x0=remote(buf.at[px, lo], r_x.at[lo], xn),
            y1=remote(buf.at[py, hi], r_y.at[hi], yn),
            x1=remote(buf.at[px, hi], r_x.at[hi], xn),
            y0=remote(buf.at[py, lo], r_y.at[lo], yn),
        )

    def add_rows(buf, slot, start, other):
        def body(at):
            into = pl.ds(pl.multiple_of(at.start + start, step), step)
            buf[slot, into, :] = (
                buf[slot, into, :].astype(F32) + other[at, :].astype(F32)
            ).astype(BF16)

        loop(half, body)

    def scatter_rest(g, buf, r_a, r_b):
        g["b"].wait_recv()
        add_rows(buf, px, half, r_b)
        go(g["x1"])
        g["a"].wait_recv()
        add_rows(buf, py, 0, r_a)
        go(g["y0"])

    dn_g["core"].wait_recv()
    plane_pair(gs_g, ("x1",))
    plane_pair(hs_g, ("x1",))
    gu_g[0]["core"].wait_recv()
    feed(0, ya)
    plane_pair(gs_g, ("y0", "fx", "fy"))
    plane_pair(hs_g, ("y0", "fx", "fy"))
    feed(0, yb)

    def z_reduce(at, r_c, r_0, r_1):
        return dict(
            core=remote(at(every, every, 1 - c), r_c, cn),
            z0=remote(at(every, 1 - z0, c), r_0, z0n),
            z1=remote(at(1 - z1, z0, c), r_1, z1n),
        )

    gu_r = [
        z_reduce(lambda a, b, cc, j=j: w_gu.at[j, a, b, :, cc], r_gu_c.at[j % 2], r_gu_0.at[j], r_gu_1.at[j])
        for j in range(3)
    ]
    dn_r = z_reduce(lambda a, b, cc: w_dn.at[a, b, cc], r_dn_c, r_dn_0, r_dn_1)

    def plus(one, two):
        return (one.astype(F32) + two.astype(F32)).astype(BF16)

    def gu_after_core(j):
        gu_r[j]["core"].wait_recv()
        for a in range(2):
            for b in range(2):
                w_gu[j, a, b, :, c] = plus(w_gu[j, a, b, :, c], r_gu_c[j % 2, a, b])
        go(gu_r[j]["z0"])

    def gu_after_z0(j):
        gu_r[j]["z0"].wait_recv()
        for a in range(2):
            w_gu[j, a, z0, :, c] = plus(w_gu[j, a, z0, :, c], r_gu_0[j, a])
        go(gu_r[j]["z1"])

    def gu_after_z1(j):
        gu_r[j]["z1"].wait_recv()
        w_gu[j, z1, z0, :, c] = plus(w_gu[j, z1, z0, :, c], r_gu_1[j])
        gu_stage[p, j] = w_gu[j, z1, z0, p, c]
        return [
            go(remote(w_gu.at[j, z1, z0, px, c], gu_stage.at[p, j], xn)),
            go(remote(w_gu.at[j, z1, z0, py, c], gu_stage.at[p, j], yn)),
            go(remote(w_gu.at[j, z1, z0, pd, c], gu_stage.at[p, j], dn)),
        ]

    def gathered(g):
        for name in ("s1", "s2", "s3", "core"):
            sent(g[name])

    gathered(gu_g[0])
    gu_weight_grad(0)
    go(gu_r[0]["core"])
    z_core(gu_g[1])
    z_forward(gu_g[2])
    gu_after_core(0)
    gu_g[1]["core"].wait_recv()
    feed(1, ya)
    feed(1, yb)
    gathered(gu_g[1])
    gu_weight_grad(1)
    go(gu_r[1]["core"])
    z_core(gu_g[2])
    gu_after_core(1)
    gu_g[2]["core"].wait_recv()
    feed(2, yb)
    dh_g = plane_scatter(dhp, dh_a, dh_b, dh_x, dh_y)
    go(dh_g["a"])
    go(dh_g["b"])
    go(dh_g["y1"])
    feed(2, ya)
    go(dh_g["x0"])
    gathered(gu_g[2])
    gu_weight_grad(2)
    go(gu_r[2]["core"])
    scatter_rest(dh_g, dhp, dh_a, dh_b)
    gu_after_z0(0)
    gu_after_core(2)

    for name in ("x0", "x1", "y0", "y1", "fx", "fy"):
        sent(hs_g[name])
    dn_flat = w_dn[...].reshape(units, width)
    for base in (ya, yb):
        m = ms[pl.ds(base, 2)].reshape(2 * toks, units)
        hs[pl.ds(base, 2)] = nn(m, dn_flat).astype(BF16).reshape(2, toks, width)
    gathered(dn_g)
    w_dn[...] = (
        tn(ms[...].reshape(4 * toks, units), gs[...].reshape(4 * toks, width))
        .astype(BF16)
        .reshape(w_dn.shape)
    )
    go(dn_r["core"])
    gu_after_z0(1)

    for name in ("x0", "x1", "y0", "y1"):
        dh_g[name].wait_recv()
    small_grad[...] = jnp.zeros_like(small_grad)

    def norm_two(at):
        dh = acc[p, at, :] + dh_x[at, :].astype(F32) + dh_y[at, :].astype(F32)
        values = x2[at, :]
        inverse = inverse_rms(values)
        normed = values * inverse
        small_grad[1:2, :] += jnp.sum(dh * normed, axis=0, keepdims=True)
        q = dh * g2
        grad = gs[p, at, :].astype(F32) + inverse * (
            q - normed * jnp.mean(q * normed, axis=1, keepdims=True)
        )
        input_grad[at, :] = grad
        dos[x, at, :] = grad.astype(BF16)

    loop(toks, norm_two)
    do_swap = go(same(dos.at[x], xn))
    lo, hi = pl.ds(0, half), pl.ds(half, half)
    ou_g = plane_scatter(hs, dhp.at[py, lo], dhp.at[px, hi], dhp.at[p], dhp.at[p])
    for copy in dh_g.values():
        sent(copy)
    pl.semaphore_signal(free_x, inc=1, device_id=xn, device_id_type=MESH)
    pl.semaphore_signal(free_y, inc=1, device_id=yn, device_id_type=MESH)
    pl.semaphore_wait(free_x, 1)
    pl.semaphore_wait(free_y, 1)
    for name in ("a", "b", "x0", "y1"):
        go(ou_g[name])

    mo_flat = w_mo[...].reshape(half_width, width)

    def split_dy(s):
        def body(at):
            dy = dkbuf[s, at, 0:half_width]
            dps[s, at, half_width : 2 * half_width] = (dy * conv[s, at, :]).astype(BF16)
            dkbuf[s, at, 0:half_width] = dy * proj[s, at, half_width : 2 * half_width]

        loop(toks, body)

    dkbuf[x, 0:toks, 0:half_width] = nt(dos[x], mo_flat)
    split_dy(x)
    dn_r["core"].wait_recv()
    for a in range(2):
        for b in range(2):
            w_dn[a, b, c] = plus(w_dn[a, b, c], r_dn_c[a, b])
    go(dn_r["z0"])
    do_swap.wait_recv()
    dkbuf[1 - x, 0:toks, 0:half_width] = nt(dos[1 - x], mo_flat)
    split_dy(1 - x)
    dk_halo = go(
        remote(
            dkbuf.at[:, pl.ds(0, 8), pl.ds(0, half_width)],
            dkbuf.at[:, pl.ds(toks, 8), pl.ds(0, half_width)],
            preceding,
        )
    )
    for name in ("s1", "s2", "s3", "y0", "y1", "y2", "y3"):
        sent(mo_g[name])
        sent(mi_g[name])
    sent(mo_core)
    sent(mi_core)
    w_mo[...] = (
        tn(ys[...].reshape(2 * toks, half_width), dos[...].reshape(2 * toks, width))
        .astype(BF16)
        .reshape(w_mo.shape)
    )

    def mix_reduce(at, r_c, r_y, r_0, r_1):
        return dict(
            core=remote(at(every, every, every, 1 - c), r_c, cn),
            y3=remote(at(1 - z1, 1 - z0, 1 - y, c), r_y.at[1 - z1, 1 - z0], yn),
            y2=remote(at(z1, 1 - z0, 1 - y, c), r_y.at[z1, 1 - z0], yn),
            y1=remote(at(1 - z1, z0, 1 - y, c), r_y.at[1 - z1, z0], yn),
            y0=remote(at(z1, z0, 1 - y, c), r_y.at[z1, z0], yn),
            s3=remote(at(1 - z1, 1 - z0, y, c), r_0.at[1 - z1], z0n),
            s2=remote(at(z1, 1 - z0, y, c), r_0.at[z1], z0n),
            s1=remote(at(1 - z1, z0, y, c), r_1, z1n),
        )

    mo_r = mix_reduce(mo_at, r_mo_c, r_mo_y, r_mo_0, r_mo_1)
    mi_r = mix_reduce(mi_at, r_mi_c, r_mi_y, r_mi_0, r_mi_1)
    go(mo_r["core"])
    dk_halo.wait_recv()
    ek = [jnp.zeros((1, half_width), F32) for _ in range(3)]
    for s in range(2):
        for i in range(toks // step):
            a = i * step
            fl = flags[s, a : a + step, :].astype(F32)
            dk = dkbuf[s, a : a + step, 0:half_width]
            ek[2] += jnp.sum(dk * ubuf[s, a + 8 : a + 8 + step, :], axis=0, keepdims=True)
            ek[1] += jnp.sum(
                dk * (fl[:, 0:1] * ubuf[s, a + 7 : a + 7 + step, :]), axis=0, keepdims=True
            )
            ek[0] += jnp.sum(
                dk * (fl[:, 1:2] * ubuf[s, a + 6 : a + 6 + step, :]), axis=0, keepdims=True
            )
            du = (
                tap2 * dk
                + tap1 * (fl[:, 2:3] * dkbuf[s, a + 1 : a + 1 + step, 0:half_width])
                + tap0 * (fl[:, 3:4] * dkbuf[s, a + 2 : a + 2 + step, 0:half_width])
            )
            dps[s, a : a + step, 0:half_width] = (
                du * proj[s, a : a + step, 2 * half_width :]
            ).astype(BF16)
            dps[s, a : a + step, 2 * half_width :] = (
                du * proj[s, a : a + step, 0:half_width]
            ).astype(BF16)
    for k in range(3):
        for q in range(4):
            chunk = jnp.broadcast_to(ek[k][:, 128 * q : 128 * q + 128], (8, 128))
            turned = pltpu.roll(chunk, 64, 1)
            even = jnp.where(is_one, jnp.where(low8, 0.0, turned), jnp.where(low8, chunk, 0.0))
            odd = jnp.where(is_one, jnp.where(low8, 0.0, chunk), jnp.where(low8, turned, 0.0))
            small_grad[2 + k : 3 + k, 256 * q : 256 * q + 128] = even[0:1]
            small_grad[2 + k : 3 + k, 256 * q + 128 : 256 * q + 256] = odd[0:1]

    mi_flat = w_mi[...].reshape(width, wide)
    sent(o_swap)
    o_send[...] = nt(dps[1 - x], mi_flat).astype(BF16)
    dh1_swap = go(remote(o_send, o_recv, xn))
    acc[p] = nt(dps[x], mi_flat)
    w_mi[...] = (
        tn(xs[...].reshape(2 * toks, width), dps[...].reshape(2 * toks, wide))
        .astype(BF16)
        .reshape(w_mi.shape)
    )
    go(mi_r["core"])
    scatter_rest(ou_g, hs, dhp.at[pd, lo], dhp.at[pd, hi])
    gu_after_z0(2)

    def mix_core(w, r_c, g, with_x):
        g["core"].wait_recv()
        for a in range(2):
            for b in range(2):
                for yy in range(2):
                    if with_x:
                        w[a, b, yy, :, c] = plus(w[a, b, yy, :, c], r_c[a, b, yy])
                    else:
                        w[a, b, yy, c] = plus(w[a, b, yy, c], r_c[a, b, yy])
        for name in ("y3", "y2", "y1", "y0"):
            go(g[name])

    mix_core(w_mo, r_mo_c, mo_r, False)
    mix_core(w_mi, r_mi_c, mi_r, True)

    dn_r["z0"].wait_recv()
    for a in range(2):
        w_dn[a, z0, c] = plus(w_dn[a, z0, c], r_dn_0[a])
    go(dn_r["z1"])

    dh1_swap.wait_recv()

    def norm_one(at):
        dh = acc[p, at, :] + o_recv[at, :].astype(F32)
        values = tokens[at, :].astype(F32)
        inverse = inverse_rms(values)
        normed = values * inverse
        small_grad[0:1, :] += jnp.sum(dh * normed, axis=0, keepdims=True)
        q = dh * g1
        input_grad[at, :] = input_grad[at, :] + inverse * (
            q - normed * jnp.mean(q * normed, axis=1, keepdims=True)
        )

    loop(toks, norm_one)

    for q in range(8):
        small_in[PLACES + q] = small_grad[:, 128 * q : 128 * q + 128]

    def small_back(m):
        target = lax.rem(v + m, PLACES)
        source = small_in.at[PLACES + lax.div(target, 4)]
        return small_copy(source, small_in.at[v], m, (back_send, back_recv))

    def small_back_start(m, _):
        small_back(m).start()
        return 0

    lax.fori_loop(1, PLACES, small_back_start, 0)
    small_in[v] = small_in[PLACES + lax.div(v, 4)]

    gu_back = gu_after_z1(0)
    gu_back += gu_after_z1(1)

    def mo_idx(a, b):
        return (a, b, y, c)

    def mi_idx(a, b):
        return (a, b, y, every, c)

    def mix_rest(w, idx, g, r_y, r_0, r_1):
        def add(a, b, other):
            w[idx(a, b)] = plus(w[idx(a, b)], other)

        g["y3"].wait_recv()
        add(1 - z1, 1 - z0, r_y[1 - z1, 1 - z0])
        go(g["s3"])
        g["y2"].wait_recv()
        add(z1, 1 - z0, r_y[z1, 1 - z0])
        go(g["s2"])
        g["y1"].wait_recv()
        add(1 - z1, z0, r_y[1 - z1, z0])
        g["s3"].wait_recv()
        add(1 - z1, z0, r_0[1 - z1])
        go(g["s1"])
        g["y0"].wait_recv()
        add(z1, z0, r_y[z1, z0])
        g["s2"].wait_recv()
        add(z1, z0, r_0[z1])

    mix_rest(w_mo, mo_idx, mo_r, r_mo_y, r_mo_0, r_mo_1)
    mix_rest(w_mi, mi_idx, mi_r, r_mi_y, r_mi_0, r_mi_1)
    gu_back += gu_after_z1(2)

    for name in ("x0", "x1", "y0", "y1"):
        ou_g[name].wait_recv()

    def out_body(at):
        o_send[at, :] = (
            x2[at, :]
            + hs[p, at, :].astype(F32)
            + dhp[px, at, :].astype(F32)
            + dhp[py, at, :].astype(F32)
        ).astype(BF16)

    sent(dh1_swap)
    loop(toks, out_body)

    stores = []

    def store(src, dst):
        copy = pltpu.make_async_copy(src, dst, store_sem.at[len(stores)])
        copy.start()
        stores.append(copy)

    store(o_send, block_out)
    down_rows = w_dn.shape[3]
    dn_r["z1"].wait_recv()
    acc[3, 0:down_rows] = (w_dn[z1, z0, c].astype(F32) + r_dn_1[...].astype(F32)) * factor
    store(acc.at[3, pl.ds(0, down_rows)], down_grad)
    mo_r["s1"].wait_recv()
    acc[2, 96 : 96 + rows] = (w_mo[z1, z0, y, c].astype(F32) + r_mo_1[...].astype(F32)) * factor
    store(acc.at[2, pl.ds(96, rows)], mixer_out_grad)
    mi_r["s1"].wait_recv()
    w_mi[z1, z0, y, :, c] = plus(w_mi[z1, z0, y, :, c], r_mi_1[...])
    mi_stage[x] = w_mi[z1, z0, y, x, c]
    mi_back = go(remote(w_mi.at[z1, z0, y, 1 - x, c], mi_stage.at[x], xn))

    for copy in gu_back:
        copy.wait_recv()
    for slot, (ref, start) in enumerate(((gate_grad, 0), (up_grad, part))):
        pieces = []
        for at_p in range(4):
            whole = jnp.concatenate(
                [gu_stage[at_p, j, :, start : start + part] for j in range(3)], axis=1
            ).astype(F32)
            pieces.append(whole * factor)
        whole = jnp.concatenate(
            [pieces[q % 4][:, run * (q // 4) : run * (q // 4) + run] for q in range(16)], axis=1
        )
        for k, first in enumerate(range(0, whole.shape[1], width)):
            count = min(width, whole.shape[1] - first)
            acc[slot, k * rows : k * rows + rows, 0:count] = whole[:, first : first + count]
            store(
                acc.at[slot, pl.ds(k * rows, rows), pl.ds(0, count)],
                ref.at[:, pl.ds(first, count)],
            )
    mi_back.wait_recv()
    for b in range(3):
        for q in range(width // 256):
            at = b * half_width + 128 * q
            first = mi_stage[0, :, at : at + 128].astype(F32) * factor
            second = mi_stage[1, :, at : at + 128].astype(F32) * factor
            to, block = 256 * q, pl.ds(b * rows, rows)
            acc[2, block, to : to + 128] = jnp.where(low, first, pltpu.roll(second, 64, 1))
            acc[2, block, to + 128 : to + 256] = jnp.where(low, pltpu.roll(first, 64, 1), second)
        store(acc.at[2, pl.ds(b * rows, rows)], mixer_in_grad.at[:, pl.ds(b * width, width)])

    def small_back_wait(m, _):
        small_back(m).wait()
        return 0

    lax.fori_loop(1, PLACES, small_back_wait, 0)
    total = small_in[0]
    for q in range(1, PLACES):
        total = total + small_in[q]
    total = total * factor
    small_out[...] = total

    for copy in stores:
        copy.wait()
    for copy in list(started):
        sent(copy)


COPIES = 160


def per_device(
    fsdp_count,
    device_count,
    tokens,
    document_index,
    loss_token_mask,
    cotangent,
    first_gain,
    mixer_in,
    conv_kernel,
    mixer_out,
    second_gain,
    gate_weight,
    up_weight,
    down_weight,
):
    row_count, seq_here, width = tokens.shape
    toks = row_count * seq_here
    spare = device_count // PLACES
    groups = [[place * spare + k for k in range(spare)] for place in range(PLACES)]
    axes = ("dp", "fsdp")

    def joined(shard, axis=0):
        if spare == 1:
            return shard
        return lax.all_gather(shard, axes, axis=axis, tiled=True, axis_index_groups=groups)

    first_gain, second_gain = joined(first_gain), joined(second_gain)
    conv_kernel = joined(conv_kernel, 1)
    mixer_in, mixer_out = joined(mixer_in), joined(mixer_out)
    gate_weight, up_weight, down_weight = joined(gate_weight), joined(up_weight), joined(down_weight)
    rows = mixer_in.shape[0]
    down_rows = down_weight.shape[0]
    ff = gate_weight.shape[1]
    part = ff // 12
    half_width = width // 2
    wide = 3 * half_width
    factor = 1.0 / math.sqrt(toks * device_count)

    def vm(shape, dtype=BF16):
        return pltpu.VMEM(shape, dtype)

    half = toks // 2
    scratch = [
        vm((8, 128), F32),
        vm((PLACES, 8, 128), F32),
        vm((8, width), F32),
        vm((PLACES + 8, 8, 128), F32),
        vm((2, 2, 2, 2, 2, rows, wide)),
        vm((2, 2, 2, 2, rows, width)),
        vm((3, 2, 2, 4, 2, rows, 2 * part)),
        vm((2, 2, 2, down_rows, width)),
        vm((2, rows, wide)),
        vm((4, 3, rows, 2 * part)),
        vm((2, toks, width)),
        vm((2, toks, 128)),
        vm((4, toks, width)),
        vm((4, toks, width)),
        vm((2, toks, wide), F32),
        vm((2, toks + 8, half_width), F32),
        vm((2, toks, half_width), F32),
        vm((2, toks, half_width)),
        vm((2, toks, wide)),
        vm((toks, width), F32),
        vm((toks, width)),
        vm((toks, width)),
        vm((2, toks + 8, 2 * part), F32),
        vm((2 * toks, part), F32),
        vm((4, toks, 3 * part)),
        vm((3, 4, toks, 2 * part)),
        vm((4, toks, width), F32),
        vm((4, toks, width)),
        vm((half, width)),
        vm((half, width)),
        vm((toks, width)),
        vm((toks, width)),
        vm((2, toks, width)),
        vm((2, 2, 2, 4, rows, 2 * part)),
        vm((3, 2, 4, rows, 2 * part)),
        vm((3, 4, rows, 2 * part)),
        vm((2, 2, down_rows, width)),
        vm((2, down_rows, width)),
        vm((down_rows, width)),
        vm((2, 2, 2, 2, rows, wide)),
        vm((2, 2, 2, rows, wide)),
        vm((2, 2, rows, wide)),
        vm((2, rows, wide)),
        vm((2, 2, 2, rows, width)),
        vm((2, 2, rows, width)),
        vm((2, rows, width)),
        vm((rows, width)),
        vm((8, width + half_width), F32),
        pltpu.SemaphoreType.DMA((COPIES,)),
        pltpu.SemaphoreType.DMA((COPIES,)),
        pltpu.SemaphoreType.DMA((3,)),
        pltpu.SemaphoreType.DMA((20,)),
        pltpu.SemaphoreType.DMA((PLACES,)),
        pltpu.SemaphoreType.DMA((PLACES,)),
        pltpu.SemaphoreType.DMA((PLACES,)),
        pltpu.SemaphoreType.DMA((PLACES,)),
        pltpu.SemaphoreType.REGULAR,
        pltpu.SemaphoreType.REGULAR,
    ]
    outs = [
        jax.ShapeDtypeStruct((toks, width), BF16),
        jax.ShapeDtypeStruct((toks, width), F32),
        jax.ShapeDtypeStruct((8, 128), F32),
        jax.ShapeDtypeStruct((rows, 3 * width), F32),
        jax.ShapeDtypeStruct((rows, width), F32),
        jax.ShapeDtypeStruct((rows, ff), F32),
        jax.ShapeDtypeStruct((rows, ff), F32),
        jax.ShapeDtypeStruct((down_rows, width), F32),
    ]
    vmem = pl.BlockSpec(memory_space=pltpu.VMEM)
    hbm = pl.BlockSpec(memory_space=pl.ANY)
    result = pl.pallas_call(
        functools.partial(kernel, fsdp_count, spare, factor),
        out_shape=outs,
        in_specs=[vmem, hbm] + [vmem] * 6 + [hbm] + [vmem] * 2 + [hbm],
        out_specs=[hbm] + [vmem] * 2 + [hbm] * 5,
        scratch_shapes=scratch,
        compiler_params=pltpu.CompilerParams(
            collective_id=0, has_side_effects=True, vmem_limit_bytes=60 << 20
        ),
    )(
        tokens.reshape(toks, width),
        cotangent.reshape(toks, width),
        document_index,
        loss_token_mask,
        first_gain.reshape(1, rows),
        second_gain.reshape(1, rows),
        conv_kernel,
        mixer_in,
        mixer_out,
        gate_weight,
        up_weight,
        down_weight,
    )
    block_out, input_grad, small, g_mi, g_mo, g_gate, g_up, g_down = result
    number = lax.axis_index("dp") * fsdp_count + lax.axis_index("fsdp")
    place = number // spare
    own = lax.dynamic_slice_in_dim(small, (place % 4) * rows, rows, 1)

    def shared(item, axis=0):
        if spare == 1:
            return item
        return lax.psum_scatter(
            item, axes, scatter_dimension=axis, axis_index_groups=groups, tiled=True
        )

    return (
        block_out.reshape(row_count, seq_here, width),
        input_grad.reshape(row_count, seq_here, width),
        shared(own[0]),
        shared(g_mi),
        shared(own[2:5], 1),
        shared(g_mo),
        shared(own[1]),
        shared(g_gate),
        shared(g_up),
        shared(g_down),
    )


def solution(mesh):
    fsdp_count = mesh.shape["fsdp"]
    device_count = mesh.shape["dp"] * fsdp_count
    return jax.shard_map(
        functools.partial(per_device, fsdp_count, device_count),
        mesh=mesh,
        in_specs=(
            P("dp", "fsdp", None),
            P("dp", None),
            P("dp", "fsdp"),
            P("dp", "fsdp", None),
            P(("dp", "fsdp")),
            P(("dp", "fsdp"), None),
            P(None, ("dp", "fsdp")),
            P(("dp", "fsdp"), None),
            P(("dp", "fsdp")),
            P(("dp", "fsdp"), None),
            P(("dp", "fsdp"), None),
            P(("dp", "fsdp"), None),
        ),
        out_specs=(
            P("dp", "fsdp", None),
            P("dp", "fsdp", None),
            P(("dp", "fsdp")),
            P(("dp", "fsdp"), None),
            P(None, ("dp", "fsdp")),
            P(("dp", "fsdp"), None),
            P(("dp", "fsdp")),
            P(("dp", "fsdp"), None),
            P(("dp", "fsdp"), None),
            P(("dp", "fsdp"), None),
        ),
        check_vma=False,
    )
```

```python
import functools
import math

import jax
import jax.numpy as jnp
from jax import lax
from jax.experimental import pallas as pl
from jax.experimental.pallas import tpu as pltpu
from jax.sharding import PartitionSpec as P

EPSILON = 1e-05
MESH = pl.DeviceIdType.MESH
F32 = jnp.float32
BF16 = jnp.bfloat16
PLACES = 32


def nn(a, b):
    return jnp.dot(a, b, preferred_element_type=F32)


def nt(a, b):
    return lax.dot_general(a, b, (((1,), (1,)), ((), ())), preferred_element_type=F32)


def tn(a, b):
    return lax.dot_general(a, b, (((0,), (0,)), ((), ())), preferred_element_type=F32)


def kernel(
    fsdp_count,
    copies_of_place,
    factor,
    tokens,
    cotangent,
    document,
    loss_mask,
    gain_one,
    gain_two,
    taps,
    mixer_in,
    mixer_out,
    gate,
    up,
    down,
    block_out,
    input_grad,
    small_out,
    mi_sum,
    mo_sum,
    gu_sum,
    dn_sum,
    small_tile,
    small_all,
    small_grad,
    small_in,
    w_mi,
    w_mo,
    w_gu,
    w_dn,
    mi_stage,
    gu_stage,
    xs,
    flags,
    gs,
    hs,
    proj,
    ubuf,
    conv,
    ys,
    dps,
    x2,
    o_send,
    o_recv,
    pre,
    dm_buf,
    ms,
    dabs,
    acc,
    dhp,
    dh_a,
    dh_b,
    dh_x,
    dh_y,
    dos,
    r_gu_c,
    r_gu_0,
    r_gu_1,
    r_dn_c,
    r_dn_0,
    r_dn_1,
    r_mi_c,
    r_mi_y,
    r_mi_0,
    r_mi_1,
    r_mo_c,
    r_mo_y,
    r_mo_0,
    r_mo_1,
    rows_buf,
    send,
    recv,
    load_sem,
    store_sem,
    small_send,
    small_recv,
    back_send,
    back_recv,
    free_x,
    free_y,
):
    toks, width = tokens.shape
    dkbuf = pre
    rows = mixer_in.shape[0]
    half_width = width // 2
    units = w_dn.shape[0] * w_dn.shape[1] * w_dn.shape[2] * w_dn.shape[3]
    part = units // 3
    half = toks // 2
    step = 32

    dp, fs = lax.axis_index("dp"), lax.axis_index("fsdp")
    number = dp * fsdp_count + fs
    v = lax.div(number, copies_of_place)
    rep = lax.rem(number, copies_of_place)
    c = lax.rem(v, 2)
    x = lax.rem(lax.div(v, 2), 2)
    y = lax.rem(lax.div(v, 4), 2)
    z0 = lax.rem(lax.div(v, 8), 2)
    z1 = lax.div(v, 16)
    p = 2 * y + x
    px = 2 * y + (1 - x)
    py = 2 * (1 - y) + x
    pd = 2 * (1 - y) + (1 - x)

    def dev(place):
        whole = place * copies_of_place + rep
        return (lax.div(whole, fsdp_count), lax.rem(whole, fsdp_count))

    cn = dev(v + (1 - 2 * c))
    xn = dev(v + 2 * (1 - 2 * x))
    yn = dev(v + 4 * (1 - 2 * y))
    dn = dev(v + 2 * (1 - 2 * x) + 4 * (1 - 2 * y))
    z0n = dev(v + 8 * (1 - 2 * z0))
    z1n = dev(v + 16 * (1 - 2 * z1))
    following = (dp, lax.rem(fs + 1, fsdp_count))
    preceding = (dp, lax.rem(fs + fsdp_count - 1, fsdp_count))

    counter = [0]
    started = []

    def remote(src, dst, target):
        at = counter[0]
        counter[0] += 1
        return pltpu.make_async_remote_copy(
            src_ref=src, dst_ref=dst, send_sem=send.at[at], recv_sem=recv.at[at],
            device_id=target, device_id_type=MESH,
        )

    def go(copy):
        copy.start()
        started.append(copy)
        return copy

    def same(ref, target):
        return remote(ref, ref, target)

    def sent(copy):
        copy.wait_send()
        started[:] = [other for other in started if other is not copy]

    barrier = pltpu.get_barrier_semaphore()

    def greet(m, _):
        pl.semaphore_signal(
            barrier, inc=1, device_id=dev(lax.rem(v + m, PLACES)), device_id_type=MESH
        )
        return 0

    lax.fori_loop(1, PLACES, greet, 0)
    pl.semaphore_signal(barrier, inc=1, device_id=following, device_id_type=MESH)
    pl.semaphore_signal(barrier, inc=1, device_id=preceding, device_id_type=MESH)

    load_out = pltpu.make_async_copy(mixer_out, w_mo.at[z1, z0, y, c], load_sem.at[0])
    load_down = pltpu.make_async_copy(down, w_dn.at[z1, z0, c], load_sem.at[1])
    load_cot = pltpu.make_async_copy(cotangent, gs.at[p], load_sem.at[2])
    load_out.start()
    load_down.start()
    load_cot.start()

    lane = lax.broadcasted_iota(jnp.int32, (1, 128), 1)
    mine = lax.div(lane, 32) == lax.rem(v, 4)
    small_tile[...] = jnp.zeros_like(small_tile)

    def spread(values):
        wide = jnp.concatenate([values.astype(F32)] * 4, axis=1)
        return jnp.where(mine, wide, 0.0)

    small_tile[0:1, :] = spread(gain_one[...])
    small_tile[1:2, :] = spread(gain_two[...])
    small_tile[2:5, :] = spread(taps[...])

    lanes128 = lax.broadcasted_iota(jnp.int32, (rows, 128), 1)
    low = lanes128 < 64
    for b in range(3):
        for q in range(width // 256):
            at = b * width + 256 * q
            even = mixer_in[:, at : at + 128].astype(F32)
            odd = mixer_in[:, at + 128 : at + 256].astype(F32)
            to = b * half_width + 128 * q
            mi_stage[0, :, to : to + 128] = jnp.where(low, even, pltpu.roll(odd, 64, 1)).astype(BF16)
            mi_stage[1, :, to : to + 128] = jnp.where(low, pltpu.roll(even, 64, 1), odd).astype(BF16)
    w_mi[z1, z0, y, x, c] = mi_stage[x]
    small_all[v] = small_tile[...]

    pl.semaphore_wait(barrier, PLACES + 1)

    def small_copy(src, dst, m, sems=(small_send, small_recv)):
        return pltpu.make_async_remote_copy(
            src_ref=src, dst_ref=dst, send_sem=sems[0].at[m], recv_sem=sems[1].at[m],
            device_id=dev(lax.rem(v + m, PLACES)), device_id_type=MESH,
        )

    def small_start(m, _):
        small_copy(small_tile, small_all.at[v], m).start()
        return 0

    mi_swap = go(remote(mi_stage.at[1 - x], w_mi.at[z1, z0, y, x, c], xn))
    lax.fori_loop(1, PLACES, small_start, 0)
    tok_swap = go(remote(tokens, xs.at[x], xn))

    def mo_at(a, b, yy, cc):
        return w_mo.at[a, b, yy, cc]

    def mi_at(a, b, yy, cc):
        return w_mi.at[a, b, yy, :, cc]

    every = slice(None)

    def mix_gather(at):
        return dict(
            s1=same(at(z1, z0, y, c), z1n),
            s2=same(at(z1, z0, y, c), z0n),
            s3=same(at(1 - z1, z0, y, c), z0n),
            y0=same(at(z1, z0, y, c), yn),
            y1=same(at(1 - z1, z0, y, c), yn),
            y2=same(at(z1, 1 - z0, y, c), yn),
            y3=same(at(1 - z1, 1 - z0, y, c), yn),
            ca=same(at(every, every, y, c), cn),
            cb=same(at(every, every, 1 - y, c), cn),
        )

    mo_g, mi_g = mix_gather(mo_at), mix_gather(mi_at)
    mi_swap.wait_recv()
    for name in ("s1", "s2", "y0"):
        go(mi_g[name])
    load_out.wait()
    for name in ("s1", "s2", "y0"):
        go(mo_g[name])

    offset = fs * toks
    ids = document[...].astype(F32) + 1.0
    mask_row = loss_mask[...].astype(F32)
    id_lane = lax.broadcasted_iota(jnp.int32, (step, ids.shape[1]), 1)
    id_row = lax.broadcasted_iota(jnp.int32, (step, ids.shape[1]), 0)
    ma_lane = lax.broadcasted_iota(jnp.int32, (step, toks), 1)
    ma_row = lax.broadcasted_iota(jnp.int32, (step, toks), 0)
    fl_lane = lax.broadcasted_iota(jnp.int32, (step, 128), 1)

    def flag_rows(i, _):
        base = i * step
        at = pl.ds(pl.multiple_of(base, step), step)

        def column(shift):
            hit = id_lane == id_row + (offset + base + shift)
            return jnp.sum(jnp.where(hit, ids, 0.0), axis=1, keepdims=True)

        centre = column(0)
        tile = jnp.zeros((step, 128), F32)
        for k, shift in enumerate((-1, -2, 1, 2)):
            tile = jnp.where(
                jnp.logical_and(fl_lane == k, column(shift) == centre), 1.0, tile
            )
        flags[x, at, :] = tile.astype(BF16)
        keep = jnp.sum(
            jnp.where(ma_lane == ma_row + base, mask_row, 0.0), axis=1, keepdims=True
        )
        gs[p, at, :] = (gs[p, at, :].astype(F32) * keep).astype(BF16)
        return 0

    run = units // 4

    def pick(ref, at_p):
        whole = ref[...].astype(F32)
        return jnp.concatenate(
            [whole[:, run * (4 * z + at_p) : run * (4 * z + at_p) + run] for z in range(4)], axis=1
        ).astype(BF16)

    def forward(g, arrived, names):
        g[arrived].wait_recv()
        for name in names:
            go(g[name])

    def z_gather(at):
        return dict(
            s1=same(at(z1, z0, c), z1n),
            s2=same(at(z1, z0, c), z0n),
            s3=same(at(1 - z1, z0, c), z0n),
            core=same(at(every, every, c), cn),
        )

    dn_g = z_gather(lambda a, b, cc: w_dn.at[a, b, cc])
    gu_g = [z_gather(lambda a, b, cc, j=j: w_gu.at[j, a, b, :, cc]) for j in range(3)]

    def z_start(g):
        go(g["s1"])
        go(g["s2"])

    def z_forward(g):
        forward(g, "s1", ("s3",))

    def z_core(g):
        g["s2"].wait_recv()
        g["s3"].wait_recv()
        go(g["core"])

    def plane_gather(buf, halves):
        lo, hi = pl.ds(0, half), pl.ds(half, half)
        return dict(
            x0=same(buf.at[p, lo], xn),
            y1=same(buf.at[p, hi], yn),
            x1=same(buf.at[p, hi], xn),
            y0=same(buf.at[p, lo], yn),
            fx=same(buf.at[px, lo] if halves else buf.at[px], yn),
            **(dict(fy=same(buf.at[py, hi], xn)) if halves else {}),
        )

    def plane_forward(g):
        forward(g, "x0", ("fx",))
        forward(g, "y1", ("fy",))

    gs_g, hs_g = plane_gather(gs, False), plane_gather(hs, True)

    load_cot.wait()
    lax.fori_loop(0, toks // step, flag_rows, 0)
    flag_swap = go(same(flags.at[x], xn))
    for at_p in range(4):
        picked_gate, picked_up = pick(gate, at_p), pick(up, at_p)
        for j in range(3):
            gu_stage[at_p, j, :, 0:part] = picked_gate[:, j * part : j * part + part]
            gu_stage[at_p, j, :, part:] = picked_up[:, j * part : j * part + part]
    xs[x] = tokens[...]
    for j in range(3):
        w_gu[j, z1, z0, p, c] = gu_stage[p, j]

    forward(mi_g, "s1", ("s3", "y1"))
    forward(mi_g, "s2", ("y2",))
    gu_swap = [
        go(remote(gu_stage.at[px], w_gu.at[:, z1, z0, p, c], xn)),
        go(remote(gu_stage.at[py], w_gu.at[:, z1, z0, p, c], yn)),
        go(remote(gu_stage.at[pd], w_gu.at[:, z1, z0, p, c], dn)),
    ]
    go(gs_g["x0"])
    go(gs_g["x1"])
    forward(mo_g, "s1", ("s3",))
    load_down.wait()
    z_start(dn_g)

    def small_wait(m, _):
        copy = small_copy(small_tile, small_all.at[v], m)
        copy.wait()
        return 0

    lax.fori_loop(1, PLACES, small_wait, 0)
    natural = []
    for q in range(8):
        natural.append(
            small_all[4 * q] + small_all[4 * q + 1] + small_all[4 * q + 2] + small_all[4 * q + 3]
        )
    for q in range(8):
        rows_buf[:, 128 * q : 128 * q + 128] = natural[q]
    low8 = lax.broadcasted_iota(jnp.int32, (8, 128), 1) < 64
    is_one = x == 1
    for q in range(4):
        even, odd = natural[2 * q], natural[2 * q + 1]
        first = jnp.where(low8, even, pltpu.roll(odd, 64, 1))
        second = jnp.where(low8, pltpu.roll(even, 64, 1), odd)
        rows_buf[:, width + 128 * q : width + 128 * q + 128] = jnp.where(is_one, second, first)
    g1 = rows_buf[0:1, 0:width]
    g2 = rows_buf[1:2, 0:width]
    tap0 = rows_buf[2:3, width : width + half_width]
    tap1 = rows_buf[3:4, width : width + half_width]
    tap2 = rows_buf[4:5, width : width + half_width]

    def inverse_rms(values):
        return lax.rsqrt(jnp.mean(values * values, axis=1, keepdims=True) + EPSILON)

    def loop(count, body):
        def wrapped(i, _):
            body(pl.ds(pl.multiple_of(i * step, step), step))
            return 0

        lax.fori_loop(0, count // step, wrapped, 0)

    def hidden_one(s):
        def body(at):
            values = xs[s, at, :].astype(F32)
            xs[s, at, :] = (values * inverse_rms(values) * g1).astype(BF16)

        loop(toks, body)

    forward(mi_g, "s3", ("y3",))
    go(mi_g["ca"])
    go(mo_g["y1"])
    forward(mo_g, "s2", ("y2",))
    forward(mo_g, "s3", ("y3",))
    go(mo_g["ca"])
    hidden_one(x)
    tok_swap.wait_recv()
    hidden_one(1 - x)
    z_forward(dn_g)
    for copy in gu_swap:
        copy.wait_recv()
    z_start(gu_g[0])
    for name in ("y0", "y1", "y2", "y3"):
        mi_g[name].wait_recv()
    go(mi_g["cb"])
    go(gs_g["y1"])
    go(gs_g["y0"])
    mi_g["ca"].wait_recv()
    mi_g["cb"].wait_recv()
    h1 = xs[...].reshape(2 * toks, width)
    wide = 3 * half_width
    proj[...] = nn(h1, w_mi[...].reshape(width, wide)).reshape(2, toks, wide)

    for s in range(2):
        def body(at, s=s):
            ubuf[s, pl.ds(pl.multiple_of(at.start + 8, 8), step), :] = (
                proj[s, at, 0:half_width] * proj[s, at, 2 * half_width :]
            )

        loop(toks, body)
    halo = go(remote(ubuf.at[:, pl.ds(toks, 8), :], ubuf.at[:, pl.ds(0, 8), :], following))
    for name in ("y0", "y1", "y2", "y3"):
        mo_g[name].wait_recv()
    go(mo_g["cb"])
    flag_swap.wait_recv()
    halo.wait_recv()
    for s in range(2):
        for i in range(toks // step):
            a = i * step
            fl = flags[s, a : a + step, :].astype(F32)
            value = (
                tap2 * ubuf[s, a + 8 : a + 8 + step, :]
                + tap1 * (fl[:, 0:1] * ubuf[s, a + 7 : a + 7 + step, :])
                + tap0 * (fl[:, 1:2] * ubuf[s, a + 6 : a + 6 + step, :])
            )
            conv[s, a : a + step, :] = value
            ys[s, a : a + step, :] = (
                proj[s, a : a + step, half_width : 2 * half_width] * value
            ).astype(BF16)
    mo_g["ca"].wait_recv()
    mo_g["cb"].wait_recv()
    mo_flat = w_mo[...].reshape(half_width, width)
    o_send[...] = nn(ys[1 - x], mo_flat).astype(BF16)
    o_swap = go(remote(o_send, o_recv, xn))
    x2[...] = nn(ys[x], mo_flat)

    z_forward(gu_g[0])
    z_start(gu_g[1])
    forward(gs_g, "x0", ())
    forward(gs_g, "x1", ("fx",))
    z_core(dn_g)
    for copy in gu_swap:
        sent(copy)
    sent(mi_swap)

    def second_body(at):
        values = tokens[at, :].astype(F32) + x2[at, :] + o_recv[at, :].astype(F32)
        x2[at, :] = values
        hs[p, at, :] = (values * inverse_rms(values) * g2).astype(BF16)

    o_swap.wait_recv()
    loop(toks, second_body)
    for name in ("x0", "y1", "x1", "y0"):
        go(hs_g[name])
    z_start(gu_g[2])
    z_core(gu_g[0])
    plane_forward(hs_g)
    z_forward(gu_g[1])

    ya, yb = 2 * y, 2 * (1 - y)

    def plane_pair(g, names):
        for name in names:
            g[name].wait_recv()

    def pair_rows(ref, base):
        return ref[pl.ds(base, 2)].reshape(2 * toks, width)

    def feed(j, base):
        w = w_gu[j].reshape(width, 2 * part)
        pre[:, 0:toks, :] = nn(pair_rows(hs, base), w).reshape(2, toks, 2 * part)
        down_rows = w_dn[...].reshape(units, width)[j * part : j * part + part]
        dm_buf[...] = nt(pair_rows(gs, base), down_rows)

        def body(i, _):
            at = pl.ds(pl.multiple_of(i * step, step), step)
            slot = base + lax.div(i, toks // step)
            inner = pl.ds(pl.multiple_of(lax.rem(i, toks // step) * step, step), step)
            which = lax.div(i, toks // step)
            a = pre[which, inner, 0:part]
            b = pre[which, inner, part:]
            d = dm_buf[at, :]
            sg = jax.nn.sigmoid(a)
            silu = a * sg
            ms[slot, inner, j * part : j * part + part] = (silu * b).astype(BF16)
            dabs[j, slot, inner, 0:part] = (d * b * sg * (1.0 + a * (1.0 - sg))).astype(BF16)
            dabs[j, slot, inner, part:] = (d * silu).astype(BF16)
            return 0

        lax.fori_loop(0, 2 * toks // step, body, 0)
        back = nt(dabs[j, pl.ds(base, 2)].reshape(2 * toks, 2 * part), w)
        back = back.reshape(2, toks, width)
        if j == 0:
            acc[pl.ds(base, 2)] = back
        elif j == 1:
            acc[pl.ds(base, 2)] += back
        else:
            total = acc[pl.ds(base, 2)] + back
            acc[pl.ds(base, 2)] = total
            dhp[pl.ds(base, 2)] = total.astype(BF16)

    def gu_weight_grad(j):
        w_gu[j] = (
            tn(hs[...].reshape(4 * toks, width), dabs[j].reshape(4 * toks, 2 * part))
            .astype(BF16)
            .reshape(w_gu.shape[1:])
        )

    def plane_scatter(buf, r_a, r_b, r_x, r_y):
        lo, hi = pl.ds(0, half), pl.ds(half, half)
        return dict(
            a=remote(buf.at[pd, lo], r_a, xn),
            b=remote(buf.at[pd, hi], r_b, yn),
            x0=remote(buf.at[px, lo], r_x.at[lo], xn),
            y1=remote(buf.at[py, hi], r_y.at[hi], yn),
            x1=remote(buf.at[px, hi], r_x.at[hi], xn),
            y0=remote(buf.at[py, lo], r_y.at[lo], yn),
        )

    def add_rows(buf, slot, start, other):
        def body(at):
            into = pl.ds(pl.multiple_of(at.start + start, step), step)
            buf[slot, into, :] = (
                buf[slot, into, :].astype(F32) + other[at, :].astype(F32)
            ).astype(BF16)

        loop(half, body)

    def scatter_rest(g, buf, r_a, r_b):
        g["b"].wait_recv()
        add_rows(buf, px, half, r_b)
        go(g["x1"])
        g["a"].wait_recv()
        add_rows(buf, py, 0, r_a)
        go(g["y0"])

    def z_reduce(at, r_c, r_0, r_1):
        return dict(
            core=remote(at(every, every, 1 - c), r_c, cn),
            z0=remote(at(every, 1 - z0, c), r_0, z0n),
            z1=remote(at(1 - z1, z0, c), r_1, z1n),
        )

    gu_r = [
        z_reduce(lambda a, b, cc, j=j: w_gu.at[j, a, b, :, cc], r_gu_c.at[j % 2], r_gu_0.at[j], r_gu_1.at[j])
        for j in range(3)
    ]
    dn_r = z_reduce(lambda a, b, cc: w_dn.at[a, b, cc], r_dn_c, r_dn_0, r_dn_1)

    def plus(one, two):
        return (one.astype(F32) + two.astype(F32)).astype(BF16)

    def gu_after_core(j):
        gu_r[j]["core"].wait_recv()
        for a in range(2):
            for b in range(2):
                w_gu[j, a, b, :, c] = plus(w_gu[j, a, b, :, c], r_gu_c[j % 2, a, b])
        go(gu_r[j]["z0"])

    def gu_after_z0(j):
        gu_r[j]["z0"].wait_recv()
        for a in range(2):
            w_gu[j, a, z0, :, c] = plus(w_gu[j, a, z0, :, c], r_gu_0[j, a])
        go(gu_r[j]["z1"])

    gu_back = []

    def gu_sum_z1(j):
        gu_r[j]["z1"].wait_recv()
        w_gu[j, z1, z0, :, c] = plus(w_gu[j, z1, z0, :, c], r_gu_1[j])
        gu_stage[p, j] = w_gu[j, z1, z0, p, c]

    def gu_return(j):
        for place, target in ((px, xn), (py, yn), (pd, dn)):
            gu_back.append(go(remote(w_gu.at[j, z1, z0, place, c], gu_stage.at[p, j], target)))

    def gathered(g):
        for name in ("s1", "s2", "s3", "core"):
            sent(g[name])

    dn_g["core"].wait_recv()
    plane_pair(hs_g, ("x1",))
    gu_g[0]["core"].wait_recv()
    feed(0, ya)
    plane_pair(gs_g, ("y0", "y1", "fx"))
    z_core(gu_g[1])
    plane_pair(hs_g, ("y0", "fx", "fy"))
    feed(0, yb)
    z_forward(gu_g[2])
    gu_g[1]["core"].wait_recv()
    feed(1, yb)
    gathered(gu_g[0])
    gu_weight_grad(0)
    go(gu_r[0]["core"])
    feed(1, ya)
    z_core(gu_g[2])
    gu_after_core(0)
    gu_g[2]["core"].wait_recv()
    feed(2, yb)
    dh_g = plane_scatter(dhp, dh_a, dh_b, dh_x, dh_y)
    go(dh_g["a"])
    go(dh_g["b"])
    go(dh_g["y1"])
    feed(2, ya)
    go(dh_g["x0"])
    gathered(gu_g[1])
    gu_weight_grad(1)
    go(gu_r[1]["core"])
    scatter_rest(dh_g, dhp, dh_a, dh_b)
    gu_after_core(1)
    gu_after_z0(0)
    gathered(gu_g[2])
    gu_weight_grad(2)
    go(gu_r[2]["core"])

    for name in ("x0", "x1", "y0", "y1", "fx", "fy"):
        sent(hs_g[name])
    dn_flat = w_dn[...].reshape(units, width)
    for base in (ya, yb):
        m = ms[pl.ds(base, 2)].reshape(2 * toks, units)
        hs[pl.ds(base, 2)] = nn(m, dn_flat).astype(BF16).reshape(2, toks, width)
    gathered(dn_g)
    w_dn[...] = (
        tn(ms[...].reshape(4 * toks, units), gs[...].reshape(4 * toks, width))
        .astype(BF16)
        .reshape(w_dn.shape)
    )
    go(dn_r["core"])
    gu_after_core(2)

    for name in ("x0", "x1", "y0", "y1"):
        dh_g[name].wait_recv()
    small_grad[...] = jnp.zeros_like(small_grad)

    def norm_two(at):
        dh = acc[p, at, :] + dh_x[at, :].astype(F32) + dh_y[at, :].astype(F32)
        values = x2[at, :]
        inverse = inverse_rms(values)
        normed = values * inverse
        small_grad[1:2, :] += jnp.sum(dh * normed, axis=0, keepdims=True)
        q = dh * g2
        grad = gs[p, at, :].astype(F32) + inverse * (
            q - normed * jnp.mean(q * normed, axis=1, keepdims=True)
        )
        input_grad[at, :] = grad
        dos[x, at, :] = grad.astype(BF16)

    loop(toks, norm_two)
    do_swap = go(same(dos.at[x], xn))
    ou_b = remote(hs.at[pd], dhp.at[px], yn)
    ou_y = remote(hs.at[py], dhp.at[p], yn)
    ou_x = remote(hs.at[px], dhp.at[p], xn)
    for copy in dh_g.values():
        sent(copy)
    pl.semaphore_signal(free_x, inc=1, device_id=xn, device_id_type=MESH)
    pl.semaphore_signal(free_y, inc=1, device_id=yn, device_id_type=MESH)
    pl.semaphore_wait(free_x, 1)
    pl.semaphore_wait(free_y, 1)
    go(ou_b)
    go(ou_y)

    mo_flat = w_mo[...].reshape(half_width, width)

    def split_dy(s):
        def body(at):
            dy = dkbuf[s, at, 0:half_width]
            dps[s, at, half_width : 2 * half_width] = (dy * conv[s, at, :]).astype(BF16)
            dkbuf[s, at, 0:half_width] = dy * proj[s, at, half_width : 2 * half_width]

        loop(toks, body)

    dkbuf[x, 0:toks, 0:half_width] = nt(dos[x], mo_flat)
    split_dy(x)
    gu_after_z0(1)
    dn_r["core"].wait_recv()
    for a in range(2):
        for b in range(2):
            w_dn[a, b, c] = plus(w_dn[a, b, c], r_dn_c[a, b])
    go(dn_r["z0"])
    gu_sum_z1(0)
    do_swap.wait_recv()
    dkbuf[1 - x, 0:toks, 0:half_width] = nt(dos[1 - x], mo_flat)
    split_dy(1 - x)
    dk_halo = go(
        remote(
            dkbuf.at[:, pl.ds(0, 8), pl.ds(0, half_width)],
            dkbuf.at[:, pl.ds(toks, 8), pl.ds(0, half_width)],
            preceding,
        )
    )
    for g in (mo_g, mi_g):
        for copy in g.values():
            sent(copy)
    w_mo[...] = (
        tn(ys[...].reshape(2 * toks, half_width), dos[...].reshape(2 * toks, width))
        .astype(BF16)
        .reshape(w_mo.shape)
    )

    def mix_reduce(at, r_c, r_y, r_0, r_1):
        return dict(
            core=remote(at(every, every, every, 1 - c), r_c, cn),
            y3=remote(at(1 - z1, 1 - z0, 1 - y, c), r_y.at[1 - z1, 1 - z0], yn),
            y2=remote(at(z1, 1 - z0, 1 - y, c), r_y.at[z1, 1 - z0], yn),
            y1=remote(at(1 - z1, z0, 1 - y, c), r_y.at[1 - z1, z0], yn),
            y0=remote(at(z1, z0, 1 - y, c), r_y.at[z1, z0], yn),
            s3=remote(at(1 - z1, 1 - z0, y, c), r_0.at[1 - z1], z0n),
            s2=remote(at(z1, 1 - z0, y, c), r_0.at[z1], z0n),
            s1=remote(at(1 - z1, z0, y, c), r_1, z1n),
        )

    mo_r = mix_reduce(mo_at, r_mo_c, r_mo_y, r_mo_0, r_mo_1)
    mi_r = mix_reduce(mi_at, r_mi_c, r_mi_y, r_mi_0, r_mi_1)
    go(mo_r["core"])
    gu_after_z0(2)

    def mix_core(w, r_c, g, with_x):
        g["core"].wait_recv()
        for a in range(2):
            for b in range(2):
                for yy in range(2):
                    if with_x:
                        w[a, b, yy, :, c] = plus(w[a, b, yy, :, c], r_c[a, b, yy])
                    else:
                        w[a, b, yy, c] = plus(w[a, b, yy, c], r_c[a, b, yy])
        for name in ("y3", "y1", "y2", "y0"):
            go(g[name])

    dk_halo.wait_recv()
    ek = [jnp.zeros((1, half_width), F32) for _ in range(3)]
    for s in range(2):
        for i in range(toks // step):
            a = i * step
            fl = flags[s, a : a + step, :].astype(F32)
            dk = dkbuf[s, a : a + step, 0:half_width]
            ek[2] += jnp.sum(dk * ubuf[s, a + 8 : a + 8 + step, :], axis=0, keepdims=True)
            ek[1] += jnp.sum(
                dk * (fl[:, 0:1] * ubuf[s, a + 7 : a + 7 + step, :]), axis=0, keepdims=True
            )
            ek[0] += jnp.sum(
                dk * (fl[:, 1:2] * ubuf[s, a + 6 : a + 6 + step, :]), axis=0, keepdims=True
            )
            du = (
                tap2 * dk
                + tap1 * (fl[:, 2:3] * dkbuf[s, a + 1 : a + 1 + step, 0:half_width])
                + tap0 * (fl[:, 3:4] * dkbuf[s, a + 2 : a + 2 + step, 0:half_width])
            )
            dps[s, a : a + step, 0:half_width] = (
                du * proj[s, a : a + step, 2 * half_width :]
            ).astype(BF16)
            dps[s, a : a + step, 2 * half_width :] = (
                du * proj[s, a : a + step, 0:half_width]
            ).astype(BF16)
    for k in range(3):
        for q in range(4):
            chunk = jnp.broadcast_to(ek[k][:, 128 * q : 128 * q + 128], (8, 128))
            turned = pltpu.roll(chunk, 64, 1)
            even = jnp.where(is_one, jnp.where(low8, 0.0, turned), jnp.where(low8, chunk, 0.0))
            odd = jnp.where(is_one, jnp.where(low8, 0.0, chunk), jnp.where(low8, turned, 0.0))
            small_grad[2 + k : 3 + k, 256 * q : 256 * q + 128] = even[0:1]
            small_grad[2 + k : 3 + k, 256 * q + 128 : 256 * q + 256] = odd[0:1]

    mix_core(w_mo, r_mo_c, mo_r, False)
    mi_flat = w_mi[...].reshape(width, wide)
    sent(o_swap)
    o_send[...] = nt(dps[1 - x], mi_flat).astype(BF16)
    dh1_swap = go(remote(o_send, o_recv, xn))
    acc[p] = nt(dps[x], mi_flat)
    w_mi[...] = (
        tn(xs[...].reshape(2 * toks, width), dps[...].reshape(2 * toks, wide))
        .astype(BF16)
        .reshape(w_mi.shape)
    )
    go(mi_r["core"])

    mix_core(w_mi, r_mi_c, mi_r, True)
    ou_b.wait_recv()

    def far_part(at):
        hs[px, at, :] = (hs[px, at, :].astype(F32) + dhp[pd, at, :].astype(F32)).astype(BF16)

    loop(toks, far_part)
    gu_sum_z1(1)
    gu_return(0)
    gu_return(1)
    go(ou_x)

    dn_r["z0"].wait_recv()
    for a in range(2):
        w_dn[a, z0, c] = plus(w_dn[a, z0, c], r_dn_0[a])
    go(dn_r["z1"])

    dh1_swap.wait_recv()

    def norm_one(at):
        dh = acc[p, at, :] + o_recv[at, :].astype(F32)
        values = tokens[at, :].astype(F32)
        inverse = inverse_rms(values)
        normed = values * inverse
        small_grad[0:1, :] += jnp.sum(dh * normed, axis=0, keepdims=True)
        q = dh * g1
        input_grad[at, :] = input_grad[at, :] + inverse * (
            q - normed * jnp.mean(q * normed, axis=1, keepdims=True)
        )

    loop(toks, norm_one)

    for q in range(8):
        small_in[PLACES + q] = small_grad[:, 128 * q : 128 * q + 128]

    def small_back(m):
        target = lax.rem(v + m, PLACES)
        source = small_in.at[PLACES + lax.div(target, 4)]
        return small_copy(source, small_in.at[v], m, (back_send, back_recv))

    def small_back_start(m, _):
        small_back(m).start()
        return 0

    lax.fori_loop(1, PLACES, small_back_start, 0)
    small_in[v] = small_in[PLACES + lax.div(v, 4)]

    def mo_idx(a, b):
        return (a, b, y, c)

    def mi_idx(a, b):
        return (a, b, y, every, c)

    def mix_rest(w, idx, g, r_y, r_0, r_1):
        def add(a, b, other):
            w[idx(a, b)] = plus(w[idx(a, b)], other)

        g["y3"].wait_recv()
        add(1 - z1, 1 - z0, r_y[1 - z1, 1 - z0])
        go(g["s3"])
        g["y1"].wait_recv()
        add(1 - z1, z0, r_y[1 - z1, z0])
        g["s3"].wait_recv()
        add(1 - z1, z0, r_0[1 - z1])
        go(g["s1"])
        g["y2"].wait_recv()
        add(z1, 1 - z0, r_y[z1, 1 - z0])
        go(g["s2"])
        g["y0"].wait_recv()
        add(z1, z0, r_y[z1, z0])
        g["s2"].wait_recv()
        add(z1, z0, r_0[z1])

    mix_rest(w_mo, mo_idx, mo_r, r_mo_y, r_mo_0, r_mo_1)
    gu_sum_z1(2)
    gu_return(2)
    mix_rest(w_mi, mi_idx, mi_r, r_mi_y, r_mi_0, r_mi_1)
    ou_x.wait_recv()
    ou_y.wait_recv()

    def out_body(at):
        o_send[at, :] = (
            x2[at, :]
            + hs[p, at, :].astype(F32)
            + dhp[px, at, :].astype(F32)
            + dhp[py, at, :].astype(F32)
        ).astype(BF16)

    sent(dh1_swap)
    loop(toks, out_body)

    stores = []

    def store(src, dst):
        copy = pltpu.make_async_copy(src, dst, store_sem.at[len(stores)])
        copy.start()
        stores.append(copy)

    store(o_send, block_out)
    down_rows = w_dn.shape[3]
    dn_r["z1"].wait_recv()
    acc[3, 0:down_rows] = (w_dn[z1, z0, c].astype(F32) + r_dn_1[...].astype(F32)) * factor
    store(acc.at[3, pl.ds(0, down_rows)], dn_sum)
    mo_r["s1"].wait_recv()
    acc[2, 96 : 96 + rows] = (w_mo[z1, z0, y, c].astype(F32) + r_mo_1[...].astype(F32)) * factor
    store(acc.at[2, pl.ds(96, rows)], mo_sum)
    mi_r["s1"].wait_recv()
    w_mi[z1, z0, y, :, c] = plus(w_mi[z1, z0, y, :, c], r_mi_1[...])
    mi_stage[x] = w_mi[z1, z0, y, x, c]
    mi_back = go(remote(w_mi.at[z1, z0, y, 1 - x, c], mi_stage.at[x], xn))

    for copy in gu_back:
        copy.wait_recv()
    store(gu_stage, gu_sum)
    mi_back.wait_recv()
    store(mi_stage, mi_sum)

    def small_back_wait(m, _):
        small_back(m).wait()
        return 0

    lax.fori_loop(1, PLACES, small_back_wait, 0)
    total = small_in[0]
    for q in range(1, PLACES):
        total = total + small_in[q]
    total = total * factor
    small_out[...] = total

    for copy in stores:
        copy.wait()
    for copy in list(started):
        sent(copy)


COPIES = 160


def finish(
    fsdp_count,
    copies_of_place,
    factor,
    block_sum,
    input_sum,
    small,
    mi_sum,
    mo_sum,
    gu_sum,
    dn_sum,
    block_out,
    input_grad,
    gain_one_grad,
    mixer_in_grad,
    taps_grad,
    mixer_out_grad,
    gain_two_grad,
    gate_grad,
    up_grad,
    down_grad,
):
    input_grad[...] = input_sum[...]
    block_out[...] = block_sum[...]
    down_grad[...] = dn_sum[...]
    mixer_out_grad[...] = mo_sum[...]
    rows, ff = gate_grad.shape
    width = mixer_out_grad.shape[1]
    part, run, half_width = ff // 12, ff // 16, width // 2
    for ref, start in ((gate_grad, 0), (up_grad, part)):
        pieces = [
            jnp.concatenate(
                [gu_sum[at_p, j, :, start : start + part] for j in range(3)], axis=1
            ).astype(F32)
            * factor
            for at_p in range(4)
        ]
        ref[...] = jnp.concatenate(
            [pieces[q % 4][:, run * (q // 4) : run * (q // 4) + run] for q in range(16)], axis=1
        )
    low = lax.broadcasted_iota(jnp.int32, (rows, 128), 1) < 64
    for b in range(3):
        for q in range(width // 256):
            at = b * half_width + 128 * q
            first = mi_sum[0, :, at : at + 128].astype(F32) * factor
            second = mi_sum[1, :, at : at + 128].astype(F32) * factor
            to = b * width + 256 * q
            mixer_in_grad[:, to : to + 128] = jnp.where(low, first, pltpu.roll(second, 64, 1))
            mixer_in_grad[:, to + 128 : to + 256] = jnp.where(low, pltpu.roll(first, 64, 1), second)
    number = lax.axis_index("dp") * fsdp_count + lax.axis_index("fsdp")
    quarter = lax.rem(lax.div(number, copies_of_place), 4)
    values = small[...]
    own = values[:, 0:rows]
    for k in range(1, 4):
        own = jnp.where(quarter == k, values[:, k * rows : k * rows + rows], own)
    gain_one_grad[...] = own[0:1]
    gain_two_grad[...] = own[1:2]
    taps_grad[...] = own[2:5]


def per_device(
    fsdp_count,
    device_count,
    tokens,
    document_index,
    loss_token_mask,
    cotangent,
    first_gain,
    mixer_in,
    conv_kernel,
    mixer_out,
    second_gain,
    gate_weight,
    up_weight,
    down_weight,
):
    row_count, seq_here, width = tokens.shape
    toks = row_count * seq_here
    spare = device_count // PLACES
    groups = [[place * spare + k for k in range(spare)] for place in range(PLACES)]
    axes = ("dp", "fsdp")

    def joined(shard, axis=0):
        if spare == 1:
            return shard
        return lax.all_gather(shard, axes, axis=axis, tiled=True, axis_index_groups=groups)

    first_gain, second_gain = joined(first_gain), joined(second_gain)
    conv_kernel = joined(conv_kernel, 1)
    mixer_in, mixer_out = joined(mixer_in), joined(mixer_out)
    gate_weight, up_weight, down_weight = joined(gate_weight), joined(up_weight), joined(down_weight)
    rows = mixer_in.shape[0]
    down_rows = down_weight.shape[0]
    ff = gate_weight.shape[1]
    part = ff // 12
    half_width = width // 2
    wide = 3 * half_width
    factor = 1.0 / math.sqrt(toks * device_count)

    def vm(shape, dtype=BF16):
        return pltpu.VMEM(shape, dtype)

    half = toks // 2
    scratch = [
        vm((8, 128), F32),
        vm((PLACES, 8, 128), F32),
        vm((8, width), F32),
        vm((PLACES + 8, 8, 128), F32),
        vm((2, 2, 2, 2, 2, rows, wide)),
        vm((2, 2, 2, 2, rows, width)),
        vm((3, 2, 2, 4, 2, rows, 2 * part)),
        vm((2, 2, 2, down_rows, width)),
        vm((2, rows, wide)),
        vm((4, 3, rows, 2 * part)),
        vm((2, toks, width)),
        vm((2, toks, 128)),
        vm((4, toks, width)),
        vm((4, toks, width)),
        vm((2, toks, wide), F32),
        vm((2, toks + 8, half_width), F32),
        vm((2, toks, half_width), F32),
        vm((2, toks, half_width)),
        vm((2, toks, wide)),
        vm((toks, width), F32),
        vm((toks, width)),
        vm((toks, width)),
        vm((2, toks + 8, 2 * part), F32),
        vm((2 * toks, part), F32),
        vm((4, toks, 3 * part)),
        vm((3, 4, toks, 2 * part)),
        vm((4, toks, width), F32),
        vm((4, toks, width)),
        vm((half, width)),
        vm((half, width)),
        vm((toks, width)),
        vm((toks, width)),
        vm((2, toks, width)),
        vm((2, 2, 2, 4, rows, 2 * part)),
        vm((3, 2, 4, rows, 2 * part)),
        vm((3, 4, rows, 2 * part)),
        vm((2, 2, down_rows, width)),
        vm((2, down_rows, width)),
        vm((down_rows, width)),
        vm((2, 2, 2, 2, rows, wide)),
        vm((2, 2, 2, rows, wide)),
        vm((2, 2, rows, wide)),
        vm((2, rows, wide)),
        vm((2, 2, 2, rows, width)),
        vm((2, 2, rows, width)),
        vm((2, rows, width)),
        vm((rows, width)),
        vm((8, width + half_width), F32),
        pltpu.SemaphoreType.DMA((COPIES,)),
        pltpu.SemaphoreType.DMA((COPIES,)),
        pltpu.SemaphoreType.DMA((3,)),
        pltpu.SemaphoreType.DMA((20,)),
        pltpu.SemaphoreType.DMA((PLACES,)),
        pltpu.SemaphoreType.DMA((PLACES,)),
        pltpu.SemaphoreType.DMA((PLACES,)),
        pltpu.SemaphoreType.DMA((PLACES,)),
        pltpu.SemaphoreType.REGULAR,
        pltpu.SemaphoreType.REGULAR,
    ]
    outs = [
        jax.ShapeDtypeStruct((toks, width), BF16),
        jax.ShapeDtypeStruct((toks, width), F32),
        jax.ShapeDtypeStruct((8, 128), F32),
        jax.ShapeDtypeStruct((2, rows, wide), BF16),
        jax.ShapeDtypeStruct((rows, width), F32),
        jax.ShapeDtypeStruct((4, 3, rows, 2 * part), BF16),
        jax.ShapeDtypeStruct((down_rows, width), F32),
    ]
    vmem = pl.BlockSpec(memory_space=pltpu.VMEM)
    hbm = pl.BlockSpec(memory_space=pl.ANY)
    result = pl.pallas_call(
        functools.partial(kernel, fsdp_count, spare, factor),
        out_shape=outs,
        in_specs=[vmem, hbm] + [vmem] * 6 + [hbm] + [vmem] * 2 + [hbm],
        out_specs=[hbm] + [vmem] * 2 + [hbm] * 4,
        scratch_shapes=scratch,
        compiler_params=pltpu.CompilerParams(
            collective_id=0, has_side_effects=True, vmem_limit_bytes=60 << 20
        ),
    )(
        tokens.reshape(toks, width),
        cotangent.reshape(toks, width),
        document_index,
        loss_token_mask,
        first_gain.reshape(1, rows),
        second_gain.reshape(1, rows),
        conv_kernel,
        mixer_in,
        mixer_out,
        gate_weight,
        up_weight,
        down_weight,
    )
    finished = pl.pallas_call(
        functools.partial(finish, fsdp_count, spare, factor),
        out_shape=[
            jax.ShapeDtypeStruct((toks, width), BF16),
            jax.ShapeDtypeStruct((toks, width), F32),
            jax.ShapeDtypeStruct((1, rows), F32),
            jax.ShapeDtypeStruct((rows, 3 * width), F32),
            jax.ShapeDtypeStruct((3, rows), F32),
            jax.ShapeDtypeStruct((rows, width), F32),
            jax.ShapeDtypeStruct((1, rows), F32),
            jax.ShapeDtypeStruct((rows, ff), F32),
            jax.ShapeDtypeStruct((rows, ff), F32),
            jax.ShapeDtypeStruct((down_rows, width), F32),
        ],
        in_specs=[vmem] * 7,
        out_specs=[vmem] * 10,
        compiler_params=pltpu.CompilerParams(vmem_limit_bytes=60 << 20),
    )(*result)
    block_out, input_grad, g_one, g_mi, g_taps, g_mo, g_two, g_gate, g_up, g_down = finished

    def shared(item, axis=0):
        if spare == 1:
            return item
        return lax.psum_scatter(
            item, axes, scatter_dimension=axis, axis_index_groups=groups, tiled=True
        )

    return (
        block_out.reshape(row_count, seq_here, width),
        input_grad.reshape(row_count, seq_here, width),
        shared(g_one.reshape(rows)),
        shared(g_mi),
        shared(g_taps, 1),
        shared(g_mo),
        shared(g_two.reshape(rows)),
        shared(g_gate),
        shared(g_up),
        shared(g_down),
    )


def solution(mesh):
    fsdp_count = mesh.shape["fsdp"]
    device_count = mesh.shape["dp"] * fsdp_count
    return jax.shard_map(
        functools.partial(per_device, fsdp_count, device_count),
        mesh=mesh,
        in_specs=(
            P("dp", "fsdp", None),
            P("dp", None),
            P("dp", "fsdp"),
            P("dp", "fsdp", None),
            P(("dp", "fsdp")),
            P(("dp", "fsdp"), None),
            P(None, ("dp", "fsdp")),
            P(("dp", "fsdp"), None),
            P(("dp", "fsdp")),
            P(("dp", "fsdp"), None),
            P(("dp", "fsdp"), None),
            P(("dp", "fsdp"), None),
        ),
        out_specs=(
            P("dp", "fsdp", None),
            P("dp", "fsdp", None),
            P(("dp", "fsdp")),
            P(("dp", "fsdp"), None),
            P(None, ("dp", "fsdp")),
            P(("dp", "fsdp"), None),
            P(("dp", "fsdp")),
            P(("dp", "fsdp"), None),
            P(("dp", "fsdp"), None),
            P(("dp", "fsdp"), None),
        ),
        check_vma=False,
    )
```

```python
import functools
import math

import jax
import jax.numpy as jnp
from jax import lax
from jax.experimental import pallas as pl
from jax.experimental.pallas import tpu as pltpu
from jax.sharding import PartitionSpec as P

EPSILON = 1e-05
MESH = pl.DeviceIdType.MESH
F32 = jnp.float32
BF16 = jnp.bfloat16
PLACES = 32


def nn(a, b):
    return jnp.dot(a, b, preferred_element_type=F32)


def nt(a, b):
    return lax.dot_general(a, b, (((1,), (1,)), ((), ())), preferred_element_type=F32)


def tn(a, b):
    return lax.dot_general(a, b, (((0,), (0,)), ((), ())), preferred_element_type=F32)


def kernel(
    fsdp_count,
    copies_of_place,
    factor,
    tokens_hbm,
    cotangent,
    document,
    loss_mask,
    gain_one,
    gain_two,
    taps,
    mixer_in_hbm,
    mixer_out,
    gate_hbm,
    up_hbm,
    down,
    block_out,
    input_sum,
    small_out,
    mi_sum,
    mo_sum,
    gu_sum,
    dn_sum,
    input_grad,
    tokens,
    mixer_in,
    gate,
    up,
    small_tile,
    small_all,
    small_grad,
    small_in,
    w_mi,
    w_mo,
    w_gu,
    w_dn,
    mi_stage,
    gu_stage,
    xs,
    flags,
    gs,
    hs,
    proj,
    ubuf,
    conv,
    ys,
    dps,
    x2,
    o_send,
    o_recv,
    pre,
    dm_buf,
    ms,
    dabs,
    acc,
    dhp,
    dh_a,
    dh_b,
    dh_x,
    dh_y,
    dos,
    r_gu_c,
    r_gu_0,
    r_gu_1,
    r_dn_c,
    r_dn_0,
    r_dn_1,
    r_mi_c,
    r_mi_y,
    r_mi_0,
    r_mi_1,
    r_mo_c,
    r_mo_y,
    r_mo_0,
    r_mo_1,
    rows_buf,
    send,
    recv,
    load_sem,
    store_sem,
    small_send,
    small_recv,
    back_send,
    back_recv,
    free_x,
    free_y,
):
    toks, width = tokens.shape
    dkbuf = pre
    rows = mixer_in.shape[0]
    half_width = width // 2
    units = w_dn.shape[0] * w_dn.shape[1] * w_dn.shape[2] * w_dn.shape[3]
    part = units // 3
    half = toks // 2
    step = 32

    dp, fs = lax.axis_index("dp"), lax.axis_index("fsdp")
    number = dp * fsdp_count + fs
    v = lax.div(number, copies_of_place)
    rep = lax.rem(number, copies_of_place)
    c = lax.rem(v, 2)
    x = lax.rem(lax.div(v, 2), 2)
    y = lax.rem(lax.div(v, 4), 2)
    z0 = lax.rem(lax.div(v, 8), 2)
    z1 = lax.div(v, 16)
    p = 2 * y + x
    px = 2 * y + (1 - x)
    py = 2 * (1 - y) + x
    pd = 2 * (1 - y) + (1 - x)

    def dev(place):
        whole = place * copies_of_place + rep
        return (lax.div(whole, fsdp_count), lax.rem(whole, fsdp_count))

    cn = dev(v + (1 - 2 * c))
    xn = dev(v + 2 * (1 - 2 * x))
    yn = dev(v + 4 * (1 - 2 * y))
    dn = dev(v + 2 * (1 - 2 * x) + 4 * (1 - 2 * y))
    z0n = dev(v + 8 * (1 - 2 * z0))
    z1n = dev(v + 16 * (1 - 2 * z1))
    following = (dp, lax.rem(fs + 1, fsdp_count))
    preceding = (dp, lax.rem(fs + fsdp_count - 1, fsdp_count))

    counter = [0]
    started = []

    def remote(src, dst, target):
        at = counter[0]
        counter[0] += 1
        return pltpu.make_async_remote_copy(
            src_ref=src, dst_ref=dst, send_sem=send.at[at], recv_sem=recv.at[at],
            device_id=target, device_id_type=MESH,
        )

    def go(copy):
        copy.start()
        started.append(copy)
        return copy

    def same(ref, target):
        return remote(ref, ref, target)

    def sent(copy):
        copy.wait_send()
        started[:] = [other for other in started if other is not copy]

    barrier = pltpu.get_barrier_semaphore()

    def greet(m, _):
        pl.semaphore_signal(
            barrier, inc=1, device_id=dev(lax.rem(v + m, PLACES)), device_id_type=MESH
        )
        return 0

    lax.fori_loop(1, PLACES, greet, 0)
    pl.semaphore_signal(barrier, inc=1, device_id=following, device_id_type=MESH)
    pl.semaphore_signal(barrier, inc=1, device_id=preceding, device_id_type=MESH)

    load_mixer = pltpu.make_async_copy(mixer_in_hbm, mixer_in, load_sem.at[3])
    load_tokens = pltpu.make_async_copy(tokens_hbm, tokens, load_sem.at[4])
    load_gate = pltpu.make_async_copy(gate_hbm, gate, load_sem.at[5])
    load_up = pltpu.make_async_copy(up_hbm, up, load_sem.at[6])
    load_mixer.start()
    load_out = pltpu.make_async_copy(mixer_out, w_mo.at[z1, z0, y, c], load_sem.at[0])
    load_down = pltpu.make_async_copy(down, w_dn.at[z1, z0, c], load_sem.at[1])
    load_cot = pltpu.make_async_copy(cotangent, gs.at[p], load_sem.at[2])
    load_out.start()
    load_down.start()
    load_cot.start()
    load_gate.start()
    load_up.start()
    load_tokens.start()

    lane = lax.broadcasted_iota(jnp.int32, (1, 128), 1)
    mine = lax.div(lane, 32) == lax.rem(v, 4)
    small_tile[...] = jnp.zeros_like(small_tile)

    def spread(values):
        wide = jnp.concatenate([values.astype(F32)] * 4, axis=1)
        return jnp.where(mine, wide, 0.0)

    small_tile[0:1, :] = spread(gain_one[...])
    small_tile[1:2, :] = spread(gain_two[...])
    small_tile[2:5, :] = spread(taps[...])

    lanes128 = lax.broadcasted_iota(jnp.int32, (rows, 128), 1)
    low = lanes128 < 64
    load_mixer.wait()
    for b in range(3):
        for q in range(width // 256):
            at = b * width + 256 * q
            even = mixer_in[:, at : at + 128].astype(F32)
            odd = mixer_in[:, at + 128 : at + 256].astype(F32)
            to = b * half_width + 128 * q
            mi_stage[0, :, to : to + 128] = jnp.where(low, even, pltpu.roll(odd, 64, 1)).astype(BF16)
            mi_stage[1, :, to : to + 128] = jnp.where(low, pltpu.roll(even, 64, 1), odd).astype(BF16)
    w_mi[z1, z0, y, x, c] = mi_stage[x]
    small_all[v] = small_tile[...]

    pl.semaphore_wait(barrier, PLACES + 1)

    def small_copy(src, dst, m, sems=(small_send, small_recv)):
        return pltpu.make_async_remote_copy(
            src_ref=src, dst_ref=dst, send_sem=sems[0].at[m], recv_sem=sems[1].at[m],
            device_id=dev(lax.rem(v + m, PLACES)), device_id_type=MESH,
        )

    def small_start(m, _):
        small_copy(small_tile, small_all.at[v], m).start()
        return 0

    mi_swap = go(remote(mi_stage.at[1 - x], w_mi.at[z1, z0, y, x, c], xn))
    lax.fori_loop(1, PLACES, small_start, 0)
    tok_swap = go(remote(tokens_hbm, xs.at[x], xn))

    def mo_at(a, b, yy, cc):
        return w_mo.at[a, b, yy, cc]

    def mi_at(a, b, yy, cc):
        return w_mi.at[a, b, yy, :, cc]

    every = slice(None)

    def mix_gather(at):
        return dict(
            s1=same(at(z1, z0, y, c), z1n),
            s2=same(at(z1, z0, y, c), z0n),
            s3=same(at(1 - z1, z0, y, c), z0n),
            y0=same(at(z1, z0, y, c), yn),
            y1=same(at(1 - z1, z0, y, c), yn),
            y2=same(at(z1, 1 - z0, y, c), yn),
            y3=same(at(1 - z1, 1 - z0, y, c), yn),
            ca=same(at(every, every, y, c), cn),
            cb=same(at(every, every, 1 - y, c), cn),
        )

    wide = 3 * half_width

    def mi_half(h):
        columns = pl.ds(h * (wide // 2), wide // 2)
        return lambda a, b, yy, cc: w_mi.at[a, b, yy, :, cc, :, columns]

    mo_g = mix_gather(mo_at)
    mi_gs = [mix_gather(mi_half(0)), mix_gather(mi_half(1))]
    mi_swap.wait_recv()
    for g in mi_gs:
        for name in ("s1", "s2", "y0"):
            go(g[name])

    offset = fs * toks
    ids = document[...].astype(F32) + 1.0
    mask_row = loss_mask[...].astype(F32)
    id_lane = lax.broadcasted_iota(jnp.int32, (step, ids.shape[1]), 1)
    id_row = lax.broadcasted_iota(jnp.int32, (step, ids.shape[1]), 0)
    ma_lane = lax.broadcasted_iota(jnp.int32, (step, toks), 1)
    ma_row = lax.broadcasted_iota(jnp.int32, (step, toks), 0)
    fl_lane = lax.broadcasted_iota(jnp.int32, (step, 128), 1)

    def flag_rows(i, _):
        base = i * step
        at = pl.ds(pl.multiple_of(base, step), step)

        def column(shift):
            hit = id_lane == id_row + (offset + base + shift)
            return jnp.sum(jnp.where(hit, ids, 0.0), axis=1, keepdims=True)

        centre = column(0)
        tile = jnp.zeros((step, 128), F32)
        for k, shift in enumerate((-1, -2, 1, 2)):
            tile = jnp.where(
                jnp.logical_and(fl_lane == k, column(shift) == centre), 1.0, tile
            )
        flags[x, at, :] = tile.astype(BF16)
        keep = jnp.sum(
            jnp.where(ma_lane == ma_row + base, mask_row, 0.0), axis=1, keepdims=True
        )
        gs[p, at, :] = (gs[p, at, :].astype(F32) * keep).astype(BF16)
        return 0

    run = units // 4

    def pick(ref, at_p):
        whole = ref[...].astype(F32)
        return jnp.concatenate(
            [whole[:, run * (4 * z + at_p) : run * (4 * z + at_p) + run] for z in range(4)], axis=1
        ).astype(BF16)

    def forward(g, arrived, names):
        g[arrived].wait_recv()
        for name in names:
            go(g[name])

    def z_gather(at):
        return dict(
            s1=same(at(z1, z0, c), z1n),
            s2=same(at(z1, z0, c), z0n),
            s3=same(at(1 - z1, z0, c), z0n),
            core=same(at(every, every, c), cn),
        )

    dn_g = z_gather(lambda a, b, cc: w_dn.at[a, b, cc])
    gu_g = [z_gather(lambda a, b, cc, j=j: w_gu.at[j, a, b, :, cc]) for j in range(3)]

    def z_start(g):
        go(g["s1"])
        go(g["s2"])

    def z_forward(g):
        forward(g, "s1", ("s3",))

    def z_core(g):
        g["s2"].wait_recv()
        g["s3"].wait_recv()
        go(g["core"])

    def plane_gather(buf, halves):
        lo, hi = pl.ds(0, half), pl.ds(half, half)
        return dict(
            x0=same(buf.at[p, lo], xn),
            y1=same(buf.at[p, hi], yn),
            x1=same(buf.at[p, hi], xn),
            y0=same(buf.at[p, lo], yn),
            fx=same(buf.at[px, lo] if halves else buf.at[px], yn),
            **(dict(fy=same(buf.at[py, hi], xn)) if halves else {}),
        )

    def plane_forward(g):
        forward(g, "x0", ("fx",))
        forward(g, "y1", ("fy",))

    gs_g, hs_g = plane_gather(gs, False), plane_gather(hs, True)

    load_cot.wait()
    lax.fori_loop(0, toks // step, flag_rows, 0)
    flag_swap = go(same(flags.at[x], xn))
    load_gate.wait()
    load_up.wait()
    for at_p in range(4):
        picked_gate, picked_up = pick(gate, at_p), pick(up, at_p)
        for j in range(3):
            gu_stage[at_p, j, :, 0:part] = picked_gate[:, j * part : j * part + part]
            gu_stage[at_p, j, :, part:] = picked_up[:, j * part : j * part + part]
    load_tokens.wait()
    xs[x] = tokens[...]
    for j in range(3):
        w_gu[j, z1, z0, p, c] = gu_stage[p, j]

    for g in mi_gs:
        forward(g, "s1", ("s3", "y1"))
        forward(g, "s2", ("y2",))
    load_out.wait()
    go(mo_g["s1"])
    go(mo_g["s2"])
    gu_swap = [
        remote(gu_stage.at[px], w_gu.at[:, z1, z0, p, c], xn),
        remote(gu_stage.at[py], w_gu.at[:, z1, z0, p, c], yn),
        remote(gu_stage.at[pd], w_gu.at[:, z1, z0, p, c], dn),
    ]
    go(gu_swap[2])
    go(gu_swap[0])
    go(gs_g["x0"])
    go(gs_g["x1"])

    def small_wait(m, _):
        copy = small_copy(small_tile, small_all.at[v], m)
        copy.wait()
        return 0

    lax.fori_loop(1, PLACES, small_wait, 0)
    natural = []
    for q in range(8):
        natural.append(
            small_all[4 * q] + small_all[4 * q + 1] + small_all[4 * q + 2] + small_all[4 * q + 3]
        )
    for q in range(8):
        rows_buf[:, 128 * q : 128 * q + 128] = natural[q]
    low8 = lax.broadcasted_iota(jnp.int32, (8, 128), 1) < 64
    is_one = x == 1
    for q in range(4):
        even, odd = natural[2 * q], natural[2 * q + 1]
        first = jnp.where(low8, even, pltpu.roll(odd, 64, 1))
        second = jnp.where(low8, pltpu.roll(even, 64, 1), odd)
        rows_buf[:, width + 128 * q : width + 128 * q + 128] = jnp.where(is_one, second, first)
    g1 = rows_buf[0:1, 0:width]
    g2 = rows_buf[1:2, 0:width]
    tap0 = rows_buf[2:3, width : width + half_width]
    tap1 = rows_buf[3:4, width : width + half_width]
    tap2 = rows_buf[4:5, width : width + half_width]

    def inverse_rms(values):
        return lax.rsqrt(jnp.mean(values * values, axis=1, keepdims=True) + EPSILON)

    def loop(count, body):
        def wrapped(i, _):
            body(pl.ds(pl.multiple_of(i * step, step), step))
            return 0

        lax.fori_loop(0, count // step, wrapped, 0)

    def hidden_one(s):
        def body(at):
            values = xs[s, at, :].astype(F32)
            xs[s, at, :] = (values * inverse_rms(values) * g1).astype(BF16)

        loop(toks, body)

    for g in mi_gs:
        forward(g, "s3", ("y3",))
        go(g["ca"])
    go(gu_swap[1])
    go(mo_g["y0"])
    forward(mo_g, "s1", ("s3", "y1"))
    load_down.wait()
    z_start(dn_g)
    hidden_one(x)
    tok_swap.wait_recv()
    hidden_one(1 - x)
    forward(mo_g, "s2", ("y2",))
    forward(mo_g, "s3", ("y3",))
    go(mo_g["ca"])
    for g in mi_gs:
        for name in ("y0", "y1", "y2", "y3"):
            g[name].wait_recv()
        go(g["cb"])
    go(gs_g["y1"])
    go(gs_g["y0"])
    for g in mi_gs:
        g["ca"].wait_recv()
        g["cb"].wait_recv()
    h1 = xs[...].reshape(2 * toks, width)
    proj[...] = nn(h1, w_mi[...].reshape(width, wide)).reshape(2, toks, wide)

    for s in range(2):
        def body(at, s=s):
            ubuf[s, pl.ds(pl.multiple_of(at.start + 8, 8), step), :] = (
                proj[s, at, 0:half_width] * proj[s, at, 2 * half_width :]
            )

        loop(toks, body)
    halo = go(remote(ubuf.at[:, pl.ds(toks, 8), :], ubuf.at[:, pl.ds(0, 8), :], following))
    z_forward(dn_g)
    for copy in gu_swap:
        copy.wait_recv()
    z_start(gu_g[0])
    z_start(gu_g[1])
    for name in ("y0", "y1", "y2", "y3"):
        mo_g[name].wait_recv()
    go(mo_g["cb"])
    flag_swap.wait_recv()
    halo.wait_recv()
    for s in range(2):
        for i in range(toks // step):
            a = i * step
            fl = flags[s, a : a + step, :].astype(F32)
            value = (
                tap2 * ubuf[s, a + 8 : a + 8 + step, :]
                + tap1 * (fl[:, 0:1] * ubuf[s, a + 7 : a + 7 + step, :])
                + tap0 * (fl[:, 1:2] * ubuf[s, a + 6 : a + 6 + step, :])
            )
            conv[s, a : a + step, :] = value
            ys[s, a : a + step, :] = (
                proj[s, a : a + step, half_width : 2 * half_width] * value
            ).astype(BF16)
    mo_g["ca"].wait_recv()
    mo_g["cb"].wait_recv()
    mo_flat = w_mo[...].reshape(half_width, width)
    o_send[...] = nn(ys[1 - x], mo_flat).astype(BF16)
    o_swap = go(remote(o_send, o_recv, xn))
    x2[...] = nn(ys[x], mo_flat)

    forward(gs_g, "x0", ())
    forward(gs_g, "x1", ("fx",))
    z_core(dn_g)
    for copy in gu_swap:
        sent(copy)
    sent(mi_swap)

    def second_body(at):
        values = tokens[at, :].astype(F32) + x2[at, :] + o_recv[at, :].astype(F32)
        x2[at, :] = values
        hs[p, at, :] = (values * inverse_rms(values) * g2).astype(BF16)

    o_swap.wait_recv()
    loop(toks, second_body)
    for name in ("x0", "y1", "x1", "y0"):
        go(hs_g[name])
    z_forward(gu_g[0])
    z_forward(gu_g[1])
    z_start(gu_g[2])
    plane_forward(hs_g)
    z_core(gu_g[0])

    ya, yb = 2 * y, 2 * (1 - y)

    def plane_pair(g, names):
        for name in names:
            g[name].wait_recv()

    def pair_rows(ref, base):
        return ref[pl.ds(base, 2)].reshape(2 * toks, width)

    def feed(j, base):
        w = w_gu[j].reshape(width, 2 * part)
        pre[:, 0:toks, :] = nn(pair_rows(hs, base), w).reshape(2, toks, 2 * part)
        down_rows = w_dn[...].reshape(units, width)[j * part : j * part + part]
        dm_buf[...] = nt(pair_rows(gs, base), down_rows)

        def body(i, _):
            at = pl.ds(pl.multiple_of(i * step, step), step)
            slot = base + lax.div(i, toks // step)
            inner = pl.ds(pl.multiple_of(lax.rem(i, toks // step) * step, step), step)
            which = lax.div(i, toks // step)
            a = pre[which, inner, 0:part]
            b = pre[which, inner, part:]
            d = dm_buf[at, :]
            sg = jax.nn.sigmoid(a)
            silu = a * sg
            ms[slot, inner, j * part : j * part + part] = (silu * b).astype(BF16)
            dabs[j, slot, inner, 0:part] = (d * b * sg * (1.0 + a * (1.0 - sg))).astype(BF16)
            dabs[j, slot, inner, part:] = (d * silu).astype(BF16)
            return 0

        lax.fori_loop(0, 2 * toks // step, body, 0)
        back = nt(dabs[j, pl.ds(base, 2)].reshape(2 * toks, 2 * part), w)
        back = back.reshape(2, toks, width)
        if j == 0:
            acc[pl.ds(base, 2)] = back
        elif j == 1:
            acc[pl.ds(base, 2)] += back
        else:
            total = acc[pl.ds(base, 2)] + back
            acc[pl.ds(base, 2)] = total
            dhp[pl.ds(base, 2)] = total.astype(BF16)

    def gu_weight_grad(j):
        w_gu[j] = (
            tn(hs[...].reshape(4 * toks, width), dabs[j].reshape(4 * toks, 2 * part))
            .astype(BF16)
            .reshape(w_gu.shape[1:])
        )

    def plane_scatter(buf, r_a, r_b, r_x, r_y):
        lo, hi = pl.ds(0, half), pl.ds(half, half)
        return dict(
            a=remote(buf.at[pd, lo], r_a, xn),
            b=remote(buf.at[pd, hi], r_b, yn),
            x0=remote(buf.at[px, lo], r_x.at[lo], xn),
            y1=remote(buf.at[py, hi], r_y.at[hi], yn),
            x1=remote(buf.at[px, hi], r_x.at[hi], xn),
            y0=remote(buf.at[py, lo], r_y.at[lo], yn),
        )

    def add_rows(buf, slot, start, other):
        def body(at):
            into = pl.ds(pl.multiple_of(at.start + start, step), step)
            buf[slot, into, :] = (
                buf[slot, into, :].astype(F32) + other[at, :].astype(F32)
            ).astype(BF16)

        loop(half, body)

    def scatter_rest(g, buf, r_a, r_b):
        g["b"].wait_recv()
        add_rows(buf, px, half, r_b)
        go(g["x1"])
        g["a"].wait_recv()
        add_rows(buf, py, 0, r_a)
        go(g["y0"])

    def z_reduce(at, r_c, r_0, r_1):
        return dict(
            core=remote(at(every, every, 1 - c), r_c, cn),
            z0=remote(at(every, 1 - z0, c), r_0, z0n),
            z1=remote(at(1 - z1, z0, c), r_1, z1n),
        )

    gu_r = [
        z_reduce(lambda a, b, cc, j=j: w_gu.at[j, a, b, :, cc], r_gu_c.at[j % 2], r_gu_0.at[j], r_gu_1.at[j])
        for j in range(3)
    ]
    dn_r = z_reduce(lambda a, b, cc: w_dn.at[a, b, cc], r_dn_c, r_dn_0, r_dn_1)

    def plus(one, two):
        return (one.astype(F32) + two.astype(F32)).astype(BF16)

    def gu_after_core(j):
        gu_r[j]["core"].wait_recv()
        for a in range(2):
            for b in range(2):
                w_gu[j, a, b, :, c] = plus(w_gu[j, a, b, :, c], r_gu_c[j % 2, a, b])
        go(gu_r[j]["z0"])

    def gu_after_z0(j):
        gu_r[j]["z0"].wait_recv()
        for a in range(2):
            w_gu[j, a, z0, :, c] = plus(w_gu[j, a, z0, :, c], r_gu_0[j, a])
        go(gu_r[j]["z1"])

    gu_back = []

    def gu_sum_z1(j):
        gu_r[j]["z1"].wait_recv()
        w_gu[j, z1, z0, :, c] = plus(w_gu[j, z1, z0, :, c], r_gu_1[j])
        gu_stage[p, j] = w_gu[j, z1, z0, p, c]

    def gu_return(j):
        for place, target in ((px, xn), (py, yn), (pd, dn)):
            gu_back.append(go(remote(w_gu.at[j, z1, z0, place, c], gu_stage.at[p, j], target)))

    def gathered(g):
        for name in ("s1", "s2", "s3", "core"):
            sent(g[name])

    dn_g["core"].wait_recv()
    plane_pair(hs_g, ("x1",))
    gu_g[0]["core"].wait_recv()
    feed(0, ya)
    z_core(gu_g[1])
    z_forward(gu_g[2])
    plane_pair(gs_g, ("y0", "y1", "fx"))
    plane_pair(hs_g, ("y0", "fx", "fy"))
    feed(0, yb)
    gathered(gu_g[0])
    gu_weight_grad(0)
    go(gu_r[0]["core"])
    z_core(gu_g[2])
    gu_g[1]["core"].wait_recv()
    feed(1, yb)
    gu_after_core(0)
    feed(1, ya)
    gu_g[2]["core"].wait_recv()
    feed(2, yb)
    dh_g = plane_scatter(dhp, dh_a, dh_b, dh_x, dh_y)
    go(dh_g["a"])
    go(dh_g["b"])
    go(dh_g["y1"])
    feed(2, ya)
    go(dh_g["x0"])
    gu_after_z0(0)
    gathered(gu_g[1])
    gu_weight_grad(1)
    go(gu_r[1]["core"])
    gathered(gu_g[2])
    gu_weight_grad(2)
    gu_after_core(1)
    go(gu_r[2]["core"])
    scatter_rest(dh_g, dhp, dh_a, dh_b)

    for name in ("x0", "x1", "y0", "y1", "fx", "fy"):
        sent(hs_g[name])
    dn_flat = w_dn[...].reshape(units, width)
    for base in (ya, yb):
        m = ms[pl.ds(base, 2)].reshape(2 * toks, units)
        hs[pl.ds(base, 2)] = nn(m, dn_flat).astype(BF16).reshape(2, toks, width)
    gu_after_core(2)
    gathered(dn_g)
    w_dn[...] = (
        tn(ms[...].reshape(4 * toks, units), gs[...].reshape(4 * toks, width))
        .astype(BF16)
        .reshape(w_dn.shape)
    )
    go(dn_r["core"])
    dn_r["core"].wait_recv()
    for a in range(2):
        for b in range(2):
            w_dn[a, b, c] = plus(w_dn[a, b, c], r_dn_c[a, b])
    go(dn_r["z0"])

    for name in ("x0", "x1", "y0", "y1"):
        dh_g[name].wait_recv()
    small_grad[...] = jnp.zeros_like(small_grad)

    def norm_two(at):
        dh = acc[p, at, :] + dh_x[at, :].astype(F32) + dh_y[at, :].astype(F32)
        values = x2[at, :]
        inverse = inverse_rms(values)
        normed = values * inverse
        small_grad[1:2, :] += jnp.sum(dh * normed, axis=0, keepdims=True)
        q = dh * g2
        grad = gs[p, at, :].astype(F32) + inverse * (
            q - normed * jnp.mean(q * normed, axis=1, keepdims=True)
        )
        input_grad[at, :] = grad
        dos[x, at, :] = grad.astype(BF16)

    loop(toks, norm_two)
    do_swap = go(same(dos.at[x], xn))
    lo, hi = pl.ds(0, half), pl.ds(half, half)
    ou_g = plane_scatter(hs, dhp.at[py, lo], dhp.at[px, hi], dhp.at[p], dhp.at[p])
    for copy in dh_g.values():
        sent(copy)
    pl.semaphore_signal(free_x, inc=1, device_id=xn, device_id_type=MESH)
    pl.semaphore_signal(free_y, inc=1, device_id=yn, device_id_type=MESH)
    pl.semaphore_wait(free_x, 1)
    pl.semaphore_wait(free_y, 1)
    for name in ("b", "y1", "a"):
        go(ou_g[name])

    mo_flat = w_mo[...].reshape(half_width, width)

    def split_dy(s):
        def body(at):
            dy = dkbuf[s, at, 0:half_width]
            dps[s, at, half_width : 2 * half_width] = (dy * conv[s, at, :]).astype(BF16)
            dkbuf[s, at, 0:half_width] = dy * proj[s, at, half_width : 2 * half_width]

        loop(toks, body)

    dkbuf[x, 0:toks, 0:half_width] = nt(dos[x], mo_flat)
    split_dy(x)
    gu_after_z0(1)
    gu_sum_z1(0)
    gu_return(0)
    do_swap.wait_recv()
    dkbuf[1 - x, 0:toks, 0:half_width] = nt(dos[1 - x], mo_flat)
    split_dy(1 - x)
    dk_halo = go(
        remote(
            dkbuf.at[:, pl.ds(0, 8), pl.ds(0, half_width)],
            dkbuf.at[:, pl.ds(toks, 8), pl.ds(0, half_width)],
            preceding,
        )
    )
    for g in (mo_g, *mi_gs):
        for copy in g.values():
            sent(copy)
    w_mo[...] = (
        tn(ys[...].reshape(2 * toks, half_width), dos[...].reshape(2 * toks, width))
        .astype(BF16)
        .reshape(w_mo.shape)
    )

    def mix_reduce(at, r_c, r_y, r_0, r_1):
        return dict(
            ca=remote(at(every, every, 1 - y, 1 - c), r_c.at[:, :, 1 - y], cn),
            cb=remote(at(every, every, y, 1 - c), r_c.at[:, :, y], cn),
            y3=remote(at(1 - z1, 1 - z0, 1 - y, c), r_y.at[1 - z1, 1 - z0], yn),
            y2=remote(at(z1, 1 - z0, 1 - y, c), r_y.at[z1, 1 - z0], yn),
            y1=remote(at(1 - z1, z0, 1 - y, c), r_y.at[1 - z1, z0], yn),
            y0=remote(at(z1, z0, 1 - y, c), r_y.at[z1, z0], yn),
            s3=remote(at(1 - z1, 1 - z0, y, c), r_0.at[1 - z1], z0n),
            s2=remote(at(z1, 1 - z0, y, c), r_0.at[z1], z0n),
            s1=remote(at(1 - z1, z0, y, c), r_1, z1n),
        )

    mo_r = mix_reduce(mo_at, r_mo_c, r_mo_y, r_mo_0, r_mo_1)
    mi_r = mix_reduce(mi_at, r_mi_c, r_mi_y, r_mi_0, r_mi_1)
    go(mo_r["ca"])
    go(mo_r["cb"])
    gu_after_z0(2)

    def mix_core(w, r_c, g, with_x):
        def add(yy):
            for a in range(2):
                for b in range(2):
                    if with_x:
                        w[a, b, yy, :, c] = plus(w[a, b, yy, :, c], r_c[a, b, yy])
                    else:
                        w[a, b, yy, c] = plus(w[a, b, yy, c], r_c[a, b, yy])

        g["ca"].wait_recv()
        add(1 - y)
        for name in ("y3", "y1", "y2", "y0"):
            go(g[name])
        g["cb"].wait_recv()
        add(y)

    dk_halo.wait_recv()
    ek = [jnp.zeros((1, half_width), F32) for _ in range(3)]
    for s in range(2):
        for i in range(toks // step):
            a = i * step
            fl = flags[s, a : a + step, :].astype(F32)
            dk = dkbuf[s, a : a + step, 0:half_width]
            ek[2] += jnp.sum(dk * ubuf[s, a + 8 : a + 8 + step, :], axis=0, keepdims=True)
            ek[1] += jnp.sum(
                dk * (fl[:, 0:1] * ubuf[s, a + 7 : a + 7 + step, :]), axis=0, keepdims=True
            )
            ek[0] += jnp.sum(
                dk * (fl[:, 1:2] * ubuf[s, a + 6 : a + 6 + step, :]), axis=0, keepdims=True
            )
            du = (
                tap2 * dk
                + tap1 * (fl[:, 2:3] * dkbuf[s, a + 1 : a + 1 + step, 0:half_width])
                + tap0 * (fl[:, 3:4] * dkbuf[s, a + 2 : a + 2 + step, 0:half_width])
            )
            dps[s, a : a + step, 0:half_width] = (
                du * proj[s, a : a + step, 2 * half_width :]
            ).astype(BF16)
            dps[s, a : a + step, 2 * half_width :] = (
                du * proj[s, a : a + step, 0:half_width]
            ).astype(BF16)
    for k in range(3):
        for q in range(4):
            chunk = jnp.broadcast_to(ek[k][:, 128 * q : 128 * q + 128], (8, 128))
            turned = pltpu.roll(chunk, 64, 1)
            even = jnp.where(is_one, jnp.where(low8, 0.0, turned), jnp.where(low8, chunk, 0.0))
            odd = jnp.where(is_one, jnp.where(low8, 0.0, chunk), jnp.where(low8, turned, 0.0))
            small_grad[2 + k : 3 + k, 256 * q : 256 * q + 128] = even[0:1]
            small_grad[2 + k : 3 + k, 256 * q + 128 : 256 * q + 256] = odd[0:1]

    for q in range(8):
        small_in[PLACES + q] = small_grad[:, 128 * q : 128 * q + 128]

    def small_back(m):
        target = lax.rem(v + m, PLACES)
        source = small_in.at[PLACES + lax.div(target, 4)]
        return small_copy(source, small_in.at[v], m, (back_send, back_recv))

    def small_back_start(m, _):
        small_back(m).start()
        return 0

    lax.fori_loop(1, PLACES, small_back_start, 0)
    small_in[v] = small_in[PLACES + lax.div(v, 4)]

    mix_core(w_mo, r_mo_c, mo_r, False)
    mi_flat = w_mi[...].reshape(width, wide)
    sent(o_swap)
    o_send[...] = nt(dps[1 - x], mi_flat).astype(BF16)
    dh1_swap = go(remote(o_send, o_recv, xn))
    ou_g["a"].wait_recv()
    add_rows(hs, py, 0, dhp.at[pd, lo])
    go(ou_g["y0"])
    ou_g["b"].wait_recv()
    add_rows(hs, px, half, dhp.at[pd, hi])
    go(ou_g["x0"])
    go(ou_g["x1"])
    acc[p] = nt(dps[x], mi_flat)
    w_mi[...] = (
        tn(xs[...].reshape(2 * toks, width), dps[...].reshape(2 * toks, wide))
        .astype(BF16)
        .reshape(w_mi.shape)
    )
    go(mi_r["ca"])
    go(mi_r["cb"])

    mix_core(w_mi, r_mi_c, mi_r, True)

    dn_r["z0"].wait_recv()
    for a in range(2):
        w_dn[a, z0, c] = plus(w_dn[a, z0, c], r_dn_0[a])
    go(dn_r["z1"])

    def mo_idx(a, b):
        return (a, b, y, c)

    def mi_idx(a, b):
        return (a, b, y, every, c)

    mo_parts = (w_mo, mo_idx, mo_r, r_mo_y, r_mo_0)
    mi_parts = (w_mi, mi_idx, mi_r, r_mi_y, r_mi_0)

    def mix_three(w, idx, g, r_y, r_0):
        g["y3"].wait_recv()
        at = idx(1 - z1, 1 - z0)
        w[at] = plus(w[at], r_y[1 - z1, 1 - z0])
        go(g["s3"])

    def mix_one(w, idx, g, r_y, r_0):
        g["y1"].wait_recv()
        g["s3"].wait_recv()
        at = idx(1 - z1, z0)
        w[at] = plus(plus(w[at], r_y[1 - z1, z0]), r_0[1 - z1])
        go(g["s1"])

    def mix_two(w, idx, g, r_y, r_0):
        g["y2"].wait_recv()
        at = idx(z1, 1 - z0)
        w[at] = plus(w[at], r_y[z1, 1 - z0])
        go(g["s2"])

    def mix_last(w, idx, g, r_y, r_0):
        g["y0"].wait_recv()
        g["s2"].wait_recv()
        at = idx(z1, z0)
        w[at] = plus(plus(w[at], r_y[z1, z0]), r_0[z1])

    mix_three(*mo_parts)
    mix_three(*mi_parts)
    gu_sum_z1(1)
    gu_return(1)
    dh1_swap.wait_recv()

    def norm_one(at):
        dh = acc[p, at, :] + o_recv[at, :].astype(F32)
        values = tokens[at, :].astype(F32)
        inverse = inverse_rms(values)
        normed = values * inverse
        q = dh * g1
        input_grad[at, :] = input_grad[at, :] + inverse * (
            q - normed * jnp.mean(q * normed, axis=1, keepdims=True)
        )

    loop(toks, norm_one)

    stores = []

    def store(src, dst):
        copy = pltpu.make_async_copy(src, dst, store_sem.at[len(stores)])
        copy.start()
        stores.append(copy)

    store(input_grad, input_sum)

    mix_one(*mo_parts)
    mix_one(*mi_parts)
    mix_two(*mo_parts)
    mix_two(*mi_parts)
    gu_sum_z1(2)
    gu_return(2)
    for name in ("x0", "x1", "y0", "y1"):
        ou_g[name].wait_recv()

    def out_body(at):
        o_send[at, :] = (
            x2[at, :]
            + hs[p, at, :].astype(F32)
            + dhp[px, at, :].astype(F32)
            + dhp[py, at, :].astype(F32)
        ).astype(BF16)

    sent(dh1_swap)
    loop(toks, out_body)

    store(o_send, block_out)
    down_rows = w_dn.shape[3]
    def small_back_wait(m, _):
        small_back(m).wait()
        return 0

    lax.fori_loop(1, PLACES, small_back_wait, 0)
    total = small_in[0]
    for q in range(1, PLACES):
        total = total + small_in[q]
    total = total * factor
    small_out[...] = total

    mix_last(*mo_parts)
    dn_r["z1"].wait_recv()
    acc[3, 0:down_rows] = (w_dn[z1, z0, c].astype(F32) + r_dn_1[...].astype(F32)) * factor
    store(acc.at[3, pl.ds(0, down_rows)], dn_sum)
    mo_r["s1"].wait_recv()
    acc[2, 96 : 96 + rows] = (w_mo[z1, z0, y, c].astype(F32) + r_mo_1[...].astype(F32)) * factor
    store(acc.at[2, pl.ds(96, rows)], mo_sum)
    for copy in gu_back:
        copy.wait_recv()
    store(gu_stage, gu_sum)
    mix_last(*mi_parts)
    mi_r["s1"].wait_recv()
    w_mi[z1, z0, y, :, c] = plus(w_mi[z1, z0, y, :, c], r_mi_1[...])
    mi_stage[x] = w_mi[z1, z0, y, x, c]
    mi_back = go(remote(w_mi.at[z1, z0, y, 1 - x, c], mi_stage.at[x], xn))

    mi_back.wait_recv()
    store(mi_stage, mi_sum)

    for copy in stores:
        copy.wait()
    for copy in list(started):
        sent(copy)


COPIES = 160


def finish(
    fsdp_count,
    copies_of_place,
    factor,
    block_sum,
    input_sum,
    small,
    mi_sum,
    mo_sum,
    gu_sum,
    dn_sum,
    mixer_in,
    gain_one,
    block_out,
    input_grad,
    gain_one_grad,
    mixer_in_grad,
    taps_grad,
    mixer_out_grad,
    gain_two_grad,
    gate_grad,
    up_grad,
    down_grad,
):
    input_grad[...] = input_sum[...]
    block_out[...] = block_sum[...]
    down_grad[...] = dn_sum[...]
    mixer_out_grad[...] = mo_sum[...]
    rows, ff = gate_grad.shape
    width = mixer_out_grad.shape[1]
    part, run, half_width = ff // 12, ff // 16, width // 2
    for ref, start in ((gate_grad, 0), (up_grad, part)):
        pieces = [
            jnp.concatenate(
                [gu_sum[at_p, j, :, start : start + part] for j in range(3)], axis=1
            ).astype(F32)
            * factor
            for at_p in range(4)
        ]
        ref[...] = jnp.concatenate(
            [pieces[q % 4][:, run * (q // 4) : run * (q // 4) + run] for q in range(16)], axis=1
        )
    low = lax.broadcasted_iota(jnp.int32, (rows, 128), 1) < 64
    by_row = jnp.zeros((rows, 128), F32)
    for b in range(3):
        for q in range(width // 256):
            at = b * half_width + 128 * q
            first = mi_sum[0, :, at : at + 128].astype(F32) * factor
            second = mi_sum[1, :, at : at + 128].astype(F32) * factor
            to = b * width + 256 * q
            even = jnp.where(low, first, pltpu.roll(second, 64, 1))
            odd = jnp.where(low, pltpu.roll(first, 64, 1), second)
            mixer_in_grad[:, to : to + 128] = even
            mixer_in_grad[:, to + 128 : to + 256] = odd
            by_row += even * mixer_in[:, to : to + 128].astype(F32)
            by_row += odd * mixer_in[:, to + 128 : to + 256].astype(F32)
    column = jnp.sum(by_row, axis=1, keepdims=True)
    row_at = lax.broadcasted_iota(jnp.int32, (rows, rows), 0)
    col_at = lax.broadcasted_iota(jnp.int32, (rows, rows), 1)
    turned = jnp.sum(jnp.where(row_at == col_at, column, 0.0), axis=0, keepdims=True)
    number = lax.axis_index("dp") * fsdp_count + lax.axis_index("fsdp")
    quarter = lax.rem(lax.div(number, copies_of_place), 4)
    values = small[...]
    own = values[:, 0:rows]
    for k in range(1, 4):
        own = jnp.where(quarter == k, values[:, k * rows : k * rows + rows], own)
    gain_one_grad[...] = turned / gain_one[...].astype(F32)
    gain_two_grad[...] = own[1:2]
    taps_grad[...] = own[2:5]


def per_device(
    fsdp_count,
    device_count,
    tokens,
    document_index,
    loss_token_mask,
    cotangent,
    first_gain,
    mixer_in,
    conv_kernel,
    mixer_out,
    second_gain,
    gate_weight,
    up_weight,
    down_weight,
):
    row_count, seq_here, width = tokens.shape
    toks = row_count * seq_here
    spare = device_count // PLACES
    groups = [[place * spare + k for k in range(spare)] for place in range(PLACES)]
    axes = ("dp", "fsdp")

    def joined(shard, axis=0):
        if spare == 1:
            return shard
        return lax.all_gather(shard, axes, axis=axis, tiled=True, axis_index_groups=groups)

    first_gain, second_gain = joined(first_gain), joined(second_gain)
    conv_kernel = joined(conv_kernel, 1)
    mixer_in, mixer_out = joined(mixer_in), joined(mixer_out)
    gate_weight, up_weight, down_weight = joined(gate_weight), joined(up_weight), joined(down_weight)
    rows = mixer_in.shape[0]
    down_rows = down_weight.shape[0]
    ff = gate_weight.shape[1]
    part = ff // 12
    half_width = width // 2
    wide = 3 * half_width
    factor = 1.0 / math.sqrt(toks * device_count)

    def vm(shape, dtype=BF16):
        return pltpu.VMEM(shape, dtype)

    half = toks // 2
    scratch = [
        vm((toks, width), F32),
        vm((toks, width)),
        vm((rows, 3 * width)),
        vm((rows, ff)),
        vm((rows, ff)),
        vm((8, 128), F32),
        vm((PLACES, 8, 128), F32),
        vm((8, width), F32),
        vm((PLACES + 8, 8, 128), F32),
        vm((2, 2, 2, 2, 2, rows, wide)),
        vm((2, 2, 2, 2, rows, width)),
        vm((3, 2, 2, 4, 2, rows, 2 * part)),
        vm((2, 2, 2, down_rows, width)),
        vm((2, rows, wide)),
        vm((4, 3, rows, 2 * part)),
        vm((2, toks, width)),
        vm((2, toks, 128)),
        vm((4, toks, width)),
        vm((4, toks, width)),
        vm((2, toks, wide), F32),
        vm((2, toks + 8, half_width), F32),
        vm((2, toks, half_width), F32),
        vm((2, toks, half_width)),
        vm((2, toks, wide)),
        vm((toks, width), F32),
        vm((toks, width)),
        vm((toks, width)),
        vm((2, toks + 8, 2 * part), F32),
        vm((2 * toks, part), F32),
        vm((4, toks, 3 * part)),
        vm((3, 4, toks, 2 * part)),
        vm((4, toks, width), F32),
        vm((4, toks, width)),
        vm((half, width)),
        vm((half, width)),
        vm((toks, width)),
        vm((toks, width)),
        vm((2, toks, width)),
        vm((2, 2, 2, 4, rows, 2 * part)),
        vm((3, 2, 4, rows, 2 * part)),
        vm((3, 4, rows, 2 * part)),
        vm((2, 2, down_rows, width)),
        vm((2, down_rows, width)),
        vm((down_rows, width)),
        vm((2, 2, 2, 2, rows, wide)),
        vm((2, 2, 2, rows, wide)),
        vm((2, 2, rows, wide)),
        vm((2, rows, wide)),
        vm((2, 2, 2, rows, width)),
        vm((2, 2, rows, width)),
        vm((2, rows, width)),
        vm((rows, width)),
        vm((8, width + half_width), F32),
        pltpu.SemaphoreType.DMA((COPIES,)),
        pltpu.SemaphoreType.DMA((COPIES,)),
        pltpu.SemaphoreType.DMA((7,)),
        pltpu.SemaphoreType.DMA((20,)),
        pltpu.SemaphoreType.DMA((PLACES,)),
        pltpu.SemaphoreType.DMA((PLACES,)),
        pltpu.SemaphoreType.DMA((PLACES,)),
        pltpu.SemaphoreType.DMA((PLACES,)),
        pltpu.SemaphoreType.REGULAR,
        pltpu.SemaphoreType.REGULAR,
    ]
    outs = [
        jax.ShapeDtypeStruct((toks, width), BF16),
        jax.ShapeDtypeStruct((toks, width), F32),
        jax.ShapeDtypeStruct((8, 128), F32),
        jax.ShapeDtypeStruct((2, rows, wide), BF16),
        jax.ShapeDtypeStruct((rows, width), F32),
        jax.ShapeDtypeStruct((4, 3, rows, 2 * part), BF16),
        jax.ShapeDtypeStruct((down_rows, width), F32),
    ]
    vmem = pl.BlockSpec(memory_space=pltpu.VMEM)
    hbm = pl.BlockSpec(memory_space=pl.ANY)
    result = pl.pallas_call(
        functools.partial(kernel, fsdp_count, spare, factor),
        out_shape=outs,
        in_specs=[hbm] * 2 + [vmem] * 5 + [hbm] * 5,
        out_specs=[hbm] * 2 + [vmem] + [hbm] * 4,
        scratch_shapes=scratch,
        compiler_params=pltpu.CompilerParams(
            collective_id=0, has_side_effects=True, vmem_limit_bytes=60 << 20
        ),
    )(
        tokens.reshape(toks, width),
        cotangent.reshape(toks, width),
        document_index,
        loss_token_mask,
        first_gain.reshape(1, rows),
        second_gain.reshape(1, rows),
        conv_kernel,
        mixer_in,
        mixer_out,
        gate_weight,
        up_weight,
        down_weight,
    )
    finished = pl.pallas_call(
        functools.partial(finish, fsdp_count, spare, factor),
        out_shape=[
            jax.ShapeDtypeStruct((toks, width), BF16),
            jax.ShapeDtypeStruct((toks, width), F32),
            jax.ShapeDtypeStruct((1, rows), F32),
            jax.ShapeDtypeStruct((rows, 3 * width), F32),
            jax.ShapeDtypeStruct((3, rows), F32),
            jax.ShapeDtypeStruct((rows, width), F32),
            jax.ShapeDtypeStruct((1, rows), F32),
            jax.ShapeDtypeStruct((rows, ff), F32),
            jax.ShapeDtypeStruct((rows, ff), F32),
            jax.ShapeDtypeStruct((down_rows, width), F32),
        ],
        in_specs=[vmem] * 9,
        out_specs=[vmem] * 10,
        compiler_params=pltpu.CompilerParams(vmem_limit_bytes=60 << 20),
    )(*result, mixer_in, first_gain.reshape(1, rows))
    block_out, input_grad, g_one, g_mi, g_taps, g_mo, g_two, g_gate, g_up, g_down = finished

    def shared(item, axis=0):
        if spare == 1:
            return item
        return lax.psum_scatter(
            item, axes, scatter_dimension=axis, axis_index_groups=groups, tiled=True
        )

    return (
        block_out.reshape(row_count, seq_here, width),
        input_grad.reshape(row_count, seq_here, width),
        shared(g_one.reshape(rows)),
        shared(g_mi),
        shared(g_taps, 1),
        shared(g_mo),
        shared(g_two.reshape(rows)),
        shared(g_gate),
        shared(g_up),
        shared(g_down),
    )


def solution(mesh):
    fsdp_count = mesh.shape["fsdp"]
    device_count = mesh.shape["dp"] * fsdp_count
    return jax.shard_map(
        functools.partial(per_device, fsdp_count, device_count),
        mesh=mesh,
        in_specs=(
            P("dp", "fsdp", None),
            P("dp", None),
            P("dp", "fsdp"),
            P("dp", "fsdp", None),
            P(("dp", "fsdp")),
            P(("dp", "fsdp"), None),
            P(None, ("dp", "fsdp")),
            P(("dp", "fsdp"), None),
            P(("dp", "fsdp")),
            P(("dp", "fsdp"), None),
            P(("dp", "fsdp"), None),
            P(("dp", "fsdp"), None),
        ),
        out_specs=(
            P("dp", "fsdp", None),
            P("dp", "fsdp", None),
            P(("dp", "fsdp")),
            P(("dp", "fsdp"), None),
            P(None, ("dp", "fsdp")),
            P(("dp", "fsdp"), None),
            P(("dp", "fsdp")),
            P(("dp", "fsdp"), None),
            P(("dp", "fsdp"), None),
            P(("dp", "fsdp"), None),
        ),
        check_vma=False,
    )
```

```python
import functools
import math

import jax
import jax.numpy as jnp
from jax import lax
from jax.experimental import pallas as pl
from jax.experimental.pallas import tpu as pltpu
from jax.sharding import PartitionSpec as P

EPSILON = 1e-05
MESH = pl.DeviceIdType.MESH
F32 = jnp.float32
BF16 = jnp.bfloat16
PLACES = 32


def nn(a, b):
    return jnp.dot(a, b, preferred_element_type=F32)


def nt(a, b):
    return lax.dot_general(a, b, (((1,), (1,)), ((), ())), preferred_element_type=F32)


def tn(a, b):
    return lax.dot_general(a, b, (((0,), (0,)), ((), ())), preferred_element_type=F32)


def kernel(
    fsdp_count,
    copies_of_place,
    factor,
    tokens_hbm,
    cotangent,
    document,
    loss_mask,
    gain_one,
    gain_two,
    taps,
    mixer_in_hbm,
    mixer_out,
    gate_hbm,
    up_hbm,
    down,
    block_out,
    input_sum,
    small_out,
    mi_sum,
    mo_sum,
    gu_sum,
    dn_sum,
    input_grad,
    tokens,
    mixer_in,
    gate,
    up,
    small_tile,
    small_all,
    small_grad,
    small_in,
    w_mi,
    w_mo,
    w_gu,
    w_dn,
    mi_stage,
    gu_stage,
    xs,
    flags,
    gs,
    hs,
    proj,
    ubuf,
    conv,
    ys,
    dps,
    x2,
    o_send,
    o_recv,
    pre,
    dm_buf,
    ms,
    dabs,
    acc,
    dhp,
    dh_a,
    dh_b,
    dh_x,
    dh_y,
    dos,
    r_gu_c,
    r_gu_0,
    r_gu_1,
    r_dn_c,
    r_dn_0,
    r_dn_1,
    r_mi_c,
    r_mi_y,
    r_mi_0,
    r_mi_1,
    r_mo_c,
    r_mo_y,
    r_mo_0,
    r_mo_1,
    rows_buf,
    send,
    recv,
    load_sem,
    store_sem,
    small_send,
    small_recv,
    back_send,
    back_recv,
    free_x,
    free_y,
):
    toks, width = tokens.shape
    dkbuf = pre
    rows = mixer_in.shape[0]
    half_width = width // 2
    units = w_dn.shape[0] * w_dn.shape[1] * w_dn.shape[2] * w_dn.shape[3]
    part = units // 3
    half = toks // 2
    step = 32

    dp, fs = lax.axis_index("dp"), lax.axis_index("fsdp")
    number = dp * fsdp_count + fs
    v = lax.div(number, copies_of_place)
    rep = lax.rem(number, copies_of_place)
    c = lax.rem(v, 2)
    x = lax.rem(lax.div(v, 2), 2)
    y = lax.rem(lax.div(v, 4), 2)
    z0 = lax.rem(lax.div(v, 8), 2)
    z1 = lax.div(v, 16)
    p = 2 * y + x
    px = 2 * y + (1 - x)
    py = 2 * (1 - y) + x
    pd = 2 * (1 - y) + (1 - x)

    def dev(place):
        whole = place * copies_of_place + rep
        return (lax.div(whole, fsdp_count), lax.rem(whole, fsdp_count))

    cn = dev(v + (1 - 2 * c))
    xn = dev(v + 2 * (1 - 2 * x))
    yn = dev(v + 4 * (1 - 2 * y))
    dn = dev(v + 2 * (1 - 2 * x) + 4 * (1 - 2 * y))
    z0n = dev(v + 8 * (1 - 2 * z0))
    z1n = dev(v + 16 * (1 - 2 * z1))
    following = (dp, lax.rem(fs + 1, fsdp_count))
    preceding = (dp, lax.rem(fs + fsdp_count - 1, fsdp_count))

    counter = [0]
    started = []

    def remote(src, dst, target):
        at = counter[0]
        counter[0] += 1
        return pltpu.make_async_remote_copy(
            src_ref=src, dst_ref=dst, send_sem=send.at[at], recv_sem=recv.at[at],
            device_id=target, device_id_type=MESH,
        )

    def go(copy):
        copy.start()
        started.append(copy)
        return copy

    def same(ref, target):
        return remote(ref, ref, target)

    def sent(copy):
        copy.wait_send()
        started[:] = [other for other in started if other is not copy]

    barrier = pltpu.get_barrier_semaphore()

    def greet(m, _):
        pl.semaphore_signal(
            barrier, inc=1, device_id=dev(lax.rem(v + m, PLACES)), device_id_type=MESH
        )
        return 0

    lax.fori_loop(1, PLACES, greet, 0)
    pl.semaphore_signal(barrier, inc=1, device_id=following, device_id_type=MESH)
    pl.semaphore_signal(barrier, inc=1, device_id=preceding, device_id_type=MESH)

    load_mixer = pltpu.make_async_copy(mixer_in_hbm, mixer_in, load_sem.at[3])
    load_tokens = pltpu.make_async_copy(tokens_hbm, tokens, load_sem.at[4])
    load_gate = pltpu.make_async_copy(gate_hbm, gate, load_sem.at[5])
    load_up = pltpu.make_async_copy(up_hbm, up, load_sem.at[6])
    load_mixer.start()
    load_out = pltpu.make_async_copy(mixer_out, w_mo.at[z1, z0, y, c], load_sem.at[0])
    load_down = pltpu.make_async_copy(down, w_dn.at[z1, z0, c], load_sem.at[1])
    load_cot = pltpu.make_async_copy(cotangent, gs.at[p], load_sem.at[2])
    load_out.start()
    load_down.start()
    load_cot.start()
    load_gate.start()
    load_up.start()
    load_tokens.start()

    lane = lax.broadcasted_iota(jnp.int32, (1, 128), 1)
    mine = lax.div(lane, 32) == lax.rem(v, 4)
    small_tile[...] = jnp.zeros_like(small_tile)

    def spread(values):
        wide = jnp.concatenate([values.astype(F32)] * 4, axis=1)
        return jnp.where(mine, wide, 0.0)

    small_tile[0:1, :] = spread(gain_one[...])
    small_tile[1:2, :] = spread(gain_two[...])
    small_tile[2:5, :] = spread(taps[...])

    lanes128 = lax.broadcasted_iota(jnp.int32, (rows, 128), 1)
    low = lanes128 < 64
    load_mixer.wait()
    for b in range(3):
        for q in range(width // 256):
            at = b * width + 256 * q
            even = mixer_in[:, at : at + 128].astype(F32)
            odd = mixer_in[:, at + 128 : at + 256].astype(F32)
            to = b * half_width + 128 * q
            mi_stage[0, :, to : to + 128] = jnp.where(low, even, pltpu.roll(odd, 64, 1)).astype(BF16)
            mi_stage[1, :, to : to + 128] = jnp.where(low, pltpu.roll(even, 64, 1), odd).astype(BF16)
    w_mi[z1, z0, y, x, c] = mi_stage[x]
    small_all[v] = small_tile[...]

    pl.semaphore_wait(barrier, PLACES + 1)

    def small_copy(src, dst, m, sems=(small_send, small_recv)):
        return pltpu.make_async_remote_copy(
            src_ref=src, dst_ref=dst, send_sem=sems[0].at[m], recv_sem=sems[1].at[m],
            device_id=dev(lax.rem(v + m, PLACES)), device_id_type=MESH,
        )

    def small_start(m, _):
        small_copy(small_tile, small_all.at[v], m).start()
        return 0

    mi_swap = go(remote(mi_stage.at[1 - x], w_mi.at[z1, z0, y, x, c], xn))
    lax.fori_loop(1, PLACES, small_start, 0)
    tok_swap = go(remote(tokens_hbm, xs.at[x], xn))

    def mo_at(a, b, yy, cc):
        return w_mo.at[a, b, yy, cc]

    def mi_at(a, b, yy, cc):
        return w_mi.at[a, b, yy, :, cc]

    every = slice(None)

    def mix_gather(at):
        return dict(
            s1=same(at(z1, z0, y, c), z1n),
            s2=same(at(z1, z0, y, c), z0n),
            s3=same(at(1 - z1, z0, y, c), z0n),
            y0=same(at(z1, z0, y, c), yn),
            y1=same(at(1 - z1, z0, y, c), yn),
            y2=same(at(z1, 1 - z0, y, c), yn),
            y3=same(at(1 - z1, 1 - z0, y, c), yn),
            ca=same(at(every, every, y, c), cn),
            cb=same(at(every, every, 1 - y, c), cn),
        )

    wide = 3 * half_width

    def mi_half(h):
        columns = pl.ds(h * (wide // 2), wide // 2)
        return lambda a, b, yy, cc: w_mi.at[a, b, yy, :, cc, :, columns]

    mo_g = mix_gather(mo_at)
    mi_gs = [mix_gather(mi_half(0)), mix_gather(mi_half(1))]
    load_out.wait()
    go(mo_g["s1"])
    go(mo_g["s2"])
    mi_swap.wait_recv()
    for g in mi_gs:
        for name in ("s1", "s2", "y0"):
            go(g[name])

    offset = fs * toks
    ids = document[...].astype(F32) + 1.0
    mask_row = loss_mask[...].astype(F32)
    id_lane = lax.broadcasted_iota(jnp.int32, (step, ids.shape[1]), 1)
    id_row = lax.broadcasted_iota(jnp.int32, (step, ids.shape[1]), 0)
    ma_lane = lax.broadcasted_iota(jnp.int32, (step, toks), 1)
    ma_row = lax.broadcasted_iota(jnp.int32, (step, toks), 0)
    fl_lane = lax.broadcasted_iota(jnp.int32, (step, 128), 1)

    def flag_rows(i, _):
        base = i * step
        at = pl.ds(pl.multiple_of(base, step), step)

        def column(shift):
            hit = id_lane == id_row + (offset + base + shift)
            return jnp.sum(jnp.where(hit, ids, 0.0), axis=1, keepdims=True)

        centre = column(0)
        tile = jnp.zeros((step, 128), F32)
        for k, shift in enumerate((-1, -2, 1, 2)):
            tile = jnp.where(
                jnp.logical_and(fl_lane == k, column(shift) == centre), 1.0, tile
            )
        flags[x, at, :] = tile.astype(BF16)
        keep = jnp.sum(
            jnp.where(ma_lane == ma_row + base, mask_row, 0.0), axis=1, keepdims=True
        )
        gs[p, at, :] = (gs[p, at, :].astype(F32) * keep).astype(BF16)
        return 0

    run = units // 4

    def pick(ref, at_p):
        whole = ref[...].astype(F32)
        return jnp.concatenate(
            [whole[:, run * (4 * z + at_p) : run * (4 * z + at_p) + run] for z in range(4)], axis=1
        ).astype(BF16)

    def forward(g, arrived, names):
        g[arrived].wait_recv()
        for name in names:
            go(g[name])

    def z_gather(at):
        return dict(
            s1=same(at(z1, z0, c), z1n),
            s2=same(at(z1, z0, c), z0n),
            s3=same(at(1 - z1, z0, c), z0n),
            core=same(at(every, every, c), cn),
        )

    dn_g = z_gather(lambda a, b, cc: w_dn.at[a, b, cc])
    gu_g = [z_gather(lambda a, b, cc, j=j: w_gu.at[j, a, b, :, cc]) for j in range(3)]

    def z_start(g):
        go(g["s1"])
        go(g["s2"])

    def z_forward(g):
        forward(g, "s1", ("s3",))

    def z_core(g):
        g["s2"].wait_recv()
        g["s3"].wait_recv()
        go(g["core"])

    def plane_gather(buf, halves):
        lo, hi = pl.ds(0, half), pl.ds(half, half)
        return dict(
            x0=same(buf.at[p, lo], xn),
            y1=same(buf.at[p, hi], yn),
            x1=same(buf.at[p, hi], xn),
            y0=same(buf.at[p, lo], yn),
            fx=same(buf.at[px, lo] if halves else buf.at[px], yn),
            **(dict(fy=same(buf.at[py, hi], xn)) if halves else {}),
        )

    def plane_forward(g):
        forward(g, "x0", ("fx",))
        forward(g, "y1", ("fy",))

    gs_g, hs_g = plane_gather(gs, False), plane_gather(hs, True)

    load_cot.wait()
    lax.fori_loop(0, toks // step, flag_rows, 0)
    flag_swap = go(same(flags.at[x], xn))
    load_gate.wait()
    load_up.wait()
    for at_p in range(4):
        picked_gate, picked_up = pick(gate, at_p), pick(up, at_p)
        for j in range(3):
            gu_stage[at_p, j, :, 0:part] = picked_gate[:, j * part : j * part + part]
            gu_stage[at_p, j, :, part:] = picked_up[:, j * part : j * part + part]
    load_tokens.wait()
    xs[x] = tokens[...]
    for j in range(3):
        w_gu[j, z1, z0, p, c] = gu_stage[p, j]

    go(mo_g["y0"])
    forward(mo_g, "s1", ("s3", "y1"))
    forward(mo_g, "s2", ("y2",))
    for g in mi_gs:
        forward(g, "s1", ("s3", "y1"))
        forward(g, "s2", ("y2",))
    gu_swap = [
        remote(gu_stage.at[px], w_gu.at[:, z1, z0, p, c], xn),
        remote(gu_stage.at[py], w_gu.at[:, z1, z0, p, c], yn),
        remote(gu_stage.at[pd], w_gu.at[:, z1, z0, p, c], dn),
    ]
    go(gu_swap[2])
    go(gu_swap[0])
    go(gs_g["x0"])
    go(gs_g["x1"])

    def small_wait(m, _):
        copy = small_copy(small_tile, small_all.at[v], m)
        copy.wait()
        return 0

    lax.fori_loop(1, PLACES, small_wait, 0)
    natural = []
    for q in range(8):
        natural.append(
            small_all[4 * q] + small_all[4 * q + 1] + small_all[4 * q + 2] + small_all[4 * q + 3]
        )
    for q in range(8):
        rows_buf[:, 128 * q : 128 * q + 128] = natural[q]
    low8 = lax.broadcasted_iota(jnp.int32, (8, 128), 1) < 64
    is_one = x == 1
    for q in range(4):
        even, odd = natural[2 * q], natural[2 * q + 1]
        first = jnp.where(low8, even, pltpu.roll(odd, 64, 1))
        second = jnp.where(low8, pltpu.roll(even, 64, 1), odd)
        rows_buf[:, width + 128 * q : width + 128 * q + 128] = jnp.where(is_one, second, first)
    g1 = rows_buf[0:1, 0:width]
    g2 = rows_buf[1:2, 0:width]
    tap0 = rows_buf[2:3, width : width + half_width]
    tap1 = rows_buf[3:4, width : width + half_width]
    tap2 = rows_buf[4:5, width : width + half_width]

    def inverse_rms(values):
        return lax.rsqrt(jnp.mean(values * values, axis=1, keepdims=True) + EPSILON)

    def loop(count, body):
        def wrapped(i, _):
            body(pl.ds(pl.multiple_of(i * step, step), step))
            return 0

        lax.fori_loop(0, count // step, wrapped, 0)

    def hidden_one(s):
        def body(at):
            values = xs[s, at, :].astype(F32)
            xs[s, at, :] = (values * inverse_rms(values) * g1).astype(BF16)

        loop(toks, body)

    for g in mi_gs:
        forward(g, "s3", ("y3",))
        go(g["ca"])
    forward(mo_g, "s3", ("y3",))
    go(mo_g["ca"])
    go(gu_swap[1])
    load_down.wait()
    z_start(dn_g)
    hidden_one(x)
    tok_swap.wait_recv()
    hidden_one(1 - x)
    for g in mi_gs:
        for name in ("y0", "y1", "y2", "y3"):
            g[name].wait_recv()
        go(g["cb"])
    go(gs_g["y1"])
    go(gs_g["y0"])
    for g in mi_gs:
        g["ca"].wait_recv()
        g["cb"].wait_recv()
    h1 = xs[...].reshape(2 * toks, width)
    proj[...] = nn(h1, w_mi[...].reshape(width, wide)).reshape(2, toks, wide)

    for s in range(2):
        def body(at, s=s):
            ubuf[s, pl.ds(pl.multiple_of(at.start + 8, 8), step), :] = (
                proj[s, at, 0:half_width] * proj[s, at, 2 * half_width :]
            )

        loop(toks, body)
    halo = go(remote(ubuf.at[:, pl.ds(toks, 8), :], ubuf.at[:, pl.ds(0, 8), :], following))
    z_forward(dn_g)
    for copy in gu_swap:
        copy.wait_recv()
    z_start(gu_g[0])
    z_start(gu_g[1])
    for name in ("y0", "y1", "y2", "y3"):
        mo_g[name].wait_recv()
    go(mo_g["cb"])
    flag_swap.wait_recv()
    halo.wait_recv()
    for s in range(2):
        for i in range(toks // step):
            a = i * step
            fl = flags[s, a : a + step, :].astype(F32)
            value = (
                tap2 * ubuf[s, a + 8 : a + 8 + step, :]
                + tap1 * (fl[:, 0:1] * ubuf[s, a + 7 : a + 7 + step, :])
                + tap0 * (fl[:, 1:2] * ubuf[s, a + 6 : a + 6 + step, :])
            )
            conv[s, a : a + step, :] = value
            ys[s, a : a + step, :] = (
                proj[s, a : a + step, half_width : 2 * half_width] * value
            ).astype(BF16)
    mo_g["ca"].wait_recv()
    mo_g["cb"].wait_recv()
    mo_flat = w_mo[...].reshape(half_width, width)
    o_send[...] = nn(ys[1 - x], mo_flat).astype(BF16)
    o_swap = go(remote(o_send, o_recv, xn))
    x2[...] = nn(ys[x], mo_flat)

    forward(gs_g, "x0", ())
    forward(gs_g, "x1", ("fx",))
    z_core(dn_g)
    for copy in gu_swap:
        sent(copy)
    sent(mi_swap)

    def second_body(at):
        values = tokens[at, :].astype(F32) + x2[at, :] + o_recv[at, :].astype(F32)
        x2[at, :] = values
        hs[p, at, :] = (values * inverse_rms(values) * g2).astype(BF16)

    o_swap.wait_recv()
    loop(toks, second_body)
    for name in ("x0", "y1", "x1", "y0"):
        go(hs_g[name])
    z_forward(gu_g[0])
    z_forward(gu_g[1])
    z_start(gu_g[2])
    plane_forward(hs_g)
    z_core(gu_g[0])

    ya, yb = 2 * y, 2 * (1 - y)

    def plane_pair(g, names):
        for name in names:
            g[name].wait_recv()

    def pair_rows(ref, base):
        return ref[pl.ds(base, 2)].reshape(2 * toks, width)

    def feed(j, base):
        w = w_gu[j].reshape(width, 2 * part)
        pre[:, 0:toks, :] = nn(pair_rows(hs, base), w).reshape(2, toks, 2 * part)
        down_rows = w_dn[...].reshape(units, width)[j * part : j * part + part]
        dm_buf[...] = nt(pair_rows(gs, base), down_rows)

        def body(i, _):
            at = pl.ds(pl.multiple_of(i * step, step), step)
            slot = base + lax.div(i, toks // step)
            inner = pl.ds(pl.multiple_of(lax.rem(i, toks // step) * step, step), step)
            which = lax.div(i, toks // step)
            a = pre[which, inner, 0:part]
            b = pre[which, inner, part:]
            d = dm_buf[at, :]
            sg = jax.nn.sigmoid(a)
            silu = a * sg
            ms[slot, inner, j * part : j * part + part] = (silu * b).astype(BF16)
            chunk = lax.rem(i, toks // step)
            at = (lax.div(chunk, 4), lax.rem(lax.div(chunk, 2), 2), lax.rem(chunk, 2))
            dabs[(j, lax.div(base, 2), which, *at, every, slice(0, part))] = (
                d * b * sg * (1.0 + a * (1.0 - sg))
            ).astype(BF16)
            dabs[(j, lax.div(base, 2), which, *at, every, slice(part, 2 * part))] = (
                d * silu
            ).astype(BF16)
            return 0

        lax.fori_loop(0, 2 * toks // step, body, 0)
        back = nt(dabs[j, lax.div(base, 2)].reshape(2 * toks, 2 * part), w)
        back = back.reshape(2, toks, width)
        if j == 0:
            acc[pl.ds(base, 2)] = back
        elif j == 1:
            acc[pl.ds(base, 2)] += back
        else:
            total = acc[pl.ds(base, 2)] + back
            acc[pl.ds(base, 2)] = total
            dhp[pl.ds(base, 2)] = total.astype(BF16)

    def gu_weight_grad(j):
        w_gu[j] = (
            tn(hs[...].reshape(4 * toks, width), dabs[j].reshape(4 * toks, 2 * part))
            .astype(BF16)
            .reshape(w_gu.shape[1:])
        )

    def plane_scatter(buf, r_a, r_b, r_x, r_y):
        lo, hi = pl.ds(0, half), pl.ds(half, half)
        return dict(
            a=remote(buf.at[pd, lo], r_a, xn),
            b=remote(buf.at[pd, hi], r_b, yn),
            x0=remote(buf.at[px, lo], r_x.at[lo], xn),
            y1=remote(buf.at[py, hi], r_y.at[hi], yn),
            x1=remote(buf.at[px, hi], r_x.at[hi], xn),
            y0=remote(buf.at[py, lo], r_y.at[lo], yn),
        )

    def add_rows(buf, slot, start, other):
        def body(at):
            into = pl.ds(pl.multiple_of(at.start + start, step), step)
            buf[slot, into, :] = (
                buf[slot, into, :].astype(F32) + other[at, :].astype(F32)
            ).astype(BF16)

        loop(half, body)

    def scatter_rest(g, buf, r_a, r_b):
        g["b"].wait_recv()
        add_rows(buf, px, half, r_b)
        go(g["x1"])
        g["a"].wait_recv()
        add_rows(buf, py, 0, r_a)
        go(g["y0"])

    def z_reduce(at, r_c, r_0, r_1):
        return dict(
            core=remote(at(every, every, 1 - c), r_c, cn),
            z0=remote(at(every, 1 - z0, c), r_0, z0n),
            z1=remote(at(1 - z1, z0, c), r_1, z1n),
        )

    gu_r = [
        z_reduce(lambda a, b, cc, j=j: w_gu.at[j, a, b, :, cc], r_gu_c.at[j % 2], r_gu_0.at[j], r_gu_1.at[j])
        for j in range(3)
    ]
    dn_r = z_reduce(lambda a, b, cc: w_dn.at[a, b, cc], r_dn_c, r_dn_0, r_dn_1)

    def plus(one, two):
        return (one.astype(F32) + two.astype(F32)).astype(BF16)

    def gu_after_core(j):
        gu_r[j]["core"].wait_recv()
        for a in range(2):
            for b in range(2):
                w_gu[j, a, b, :, c] = plus(w_gu[j, a, b, :, c], r_gu_c[j % 2, a, b])
        go(gu_r[j]["z0"])

    def gu_after_z0(j):
        gu_r[j]["z0"].wait_recv()
        for a in range(2):
            w_gu[j, a, z0, :, c] = plus(w_gu[j, a, z0, :, c], r_gu_0[j, a])
        go(gu_r[j]["z1"])

    gu_back = []

    def gu_sum_z1(j):
        gu_r[j]["z1"].wait_recv()
        w_gu[j, z1, z0, :, c] = plus(w_gu[j, z1, z0, :, c], r_gu_1[j])
        gu_stage[p, j] = w_gu[j, z1, z0, p, c]

    def gu_return(j):
        for place, target in ((px, xn), (py, yn), (pd, dn)):
            gu_back.append(go(remote(w_gu.at[j, z1, z0, place, c], gu_stage.at[p, j], target)))

    def gathered(g):
        for name in ("s1", "s2", "s3", "core"):
            sent(g[name])

    dn_g["core"].wait_recv()
    plane_pair(hs_g, ("x1",))
    gu_g[0]["core"].wait_recv()
    feed(0, ya)
    z_core(gu_g[1])
    plane_pair(gs_g, ("y0", "y1", "fx"))
    plane_pair(hs_g, ("y0", "fx", "fy"))
    feed(0, yb)
    gathered(gu_g[0])
    gu_weight_grad(0)
    go(gu_r[0]["core"])
    z_forward(gu_g[2])
    gu_g[1]["core"].wait_recv()
    feed(1, yb)
    gu_after_core(0)
    z_core(gu_g[2])
    feed(1, ya)
    gu_g[2]["core"].wait_recv()
    feed(2, yb)
    dh_g = plane_scatter(dhp, dh_a, dh_b, dh_x, dh_y)
    go(dh_g["a"])
    go(dh_g["b"])
    go(dh_g["y1"])
    gu_after_z0(0)
    feed(2, ya)
    go(dh_g["x0"])
    gathered(gu_g[1])
    gu_weight_grad(1)
    go(gu_r[1]["core"])
    gathered(gu_g[2])
    gu_weight_grad(2)
    gu_after_core(1)
    go(gu_r[2]["core"])
    scatter_rest(dh_g, dhp, dh_a, dh_b)

    for name in ("x0", "x1", "y0", "y1", "fx", "fy"):
        sent(hs_g[name])
    dn_flat = w_dn[...].reshape(units, width)
    for base in (ya, yb):
        m = ms[pl.ds(base, 2)].reshape(2 * toks, units)
        hs[pl.ds(base, 2)] = nn(m, dn_flat).astype(BF16).reshape(2, toks, width)
    gu_after_core(2)
    gathered(dn_g)
    w_dn[...] = (
        tn(ms[...].reshape(4 * toks, units), gs[...].reshape(4 * toks, width))
        .astype(BF16)
        .reshape(w_dn.shape)
    )
    go(dn_r["core"])
    dn_r["core"].wait_recv()
    for a in range(2):
        for b in range(2):
            w_dn[a, b, c] = plus(w_dn[a, b, c], r_dn_c[a, b])
    go(dn_r["z0"])

    for name in ("x0", "x1", "y0", "y1"):
        dh_g[name].wait_recv()
    small_grad[...] = jnp.zeros_like(small_grad)

    def norm_two(at):
        dh = acc[p, at, :] + dh_x[at, :].astype(F32) + dh_y[at, :].astype(F32)
        values = x2[at, :]
        inverse = inverse_rms(values)
        normed = values * inverse
        small_grad[1:2, :] += jnp.sum(dh * normed, axis=0, keepdims=True)
        q = dh * g2
        grad = gs[p, at, :].astype(F32) + inverse * (
            q - normed * jnp.mean(q * normed, axis=1, keepdims=True)
        )
        input_grad[at, :] = grad
        dos[x, at, :] = grad.astype(BF16)

    loop(toks, norm_two)
    do_swap = go(same(dos.at[x], xn))
    lo, hi = pl.ds(0, half), pl.ds(half, half)
    ou_g = plane_scatter(hs, dhp.at[py, lo], dhp.at[px, hi], dhp.at[p], dhp.at[p])
    for copy in dh_g.values():
        sent(copy)
    pl.semaphore_signal(free_x, inc=1, device_id=xn, device_id_type=MESH)
    pl.semaphore_signal(free_y, inc=1, device_id=yn, device_id_type=MESH)
    pl.semaphore_wait(free_x, 1)
    pl.semaphore_wait(free_y, 1)
    for name in ("b", "y1", "a"):
        go(ou_g[name])

    mo_flat = w_mo[...].reshape(half_width, width)

    def split_dy(s):
        def body(at):
            dy = dkbuf[s, at, 0:half_width]
            dps[s, at, half_width : 2 * half_width] = (dy * conv[s, at, :]).astype(BF16)
            dkbuf[s, at, 0:half_width] = dy * proj[s, at, half_width : 2 * half_width]

        loop(toks, body)

    dkbuf[x, 0:toks, 0:half_width] = nt(dos[x], mo_flat)
    split_dy(x)
    gu_after_z0(1)
    gu_sum_z1(0)
    gu_return(0)
    gu_after_z0(2)
    do_swap.wait_recv()
    dkbuf[1 - x, 0:toks, 0:half_width] = nt(dos[1 - x], mo_flat)
    split_dy(1 - x)
    dk_halo = go(
        remote(
            dkbuf.at[:, pl.ds(0, 8), pl.ds(0, half_width)],
            dkbuf.at[:, pl.ds(toks, 8), pl.ds(0, half_width)],
            preceding,
        )
    )
    for g in (mo_g, *mi_gs):
        for copy in g.values():
            sent(copy)
    w_mo[...] = (
        tn(ys[...].reshape(2 * toks, half_width), dos[...].reshape(2 * toks, width))
        .astype(BF16)
        .reshape(w_mo.shape)
    )

    def mix_reduce(at, r_c, r_y, r_0, r_1):
        return dict(
            ca=remote(at(every, every, 1 - y, 1 - c), r_c.at[:, :, 1 - y], cn),
            cb=remote(at(every, every, y, 1 - c), r_c.at[:, :, y], cn),
            y3=remote(at(1 - z1, 1 - z0, 1 - y, c), r_y.at[1 - z1, 1 - z0], yn),
            y2=remote(at(z1, 1 - z0, 1 - y, c), r_y.at[z1, 1 - z0], yn),
            y1=remote(at(1 - z1, z0, 1 - y, c), r_y.at[1 - z1, z0], yn),
            y0=remote(at(z1, z0, 1 - y, c), r_y.at[z1, z0], yn),
            s3=remote(at(1 - z1, 1 - z0, y, c), r_0.at[1 - z1], z0n),
            s2=remote(at(z1, 1 - z0, y, c), r_0.at[z1], z0n),
            s1=remote(at(1 - z1, z0, y, c), r_1, z1n),
        )

    mo_r = mix_reduce(mo_at, r_mo_c, r_mo_y, r_mo_0, r_mo_1)
    mi_rs = [
        mix_reduce(
            lambda a, b, yy, cc, h=h: dabs.at[h, a, b, yy, :, cc],
            r_mi_c.at[h], r_mi_y.at[h], r_mi_0.at[h], r_mi_1.at[h],
        )
        for h in range(2)
    ]
    go(mo_r["ca"])
    go(mo_r["cb"])
    def mix_core(w, r_c, g, with_x):
        def add(yy):
            for a in range(2):
                for b in range(2):
                    if with_x:
                        w[a, b, yy, :, c] = plus(w[a, b, yy, :, c], r_c[a, b, yy])
                    else:
                        w[a, b, yy, c] = plus(w[a, b, yy, c], r_c[a, b, yy])

        g["ca"].wait_recv()
        add(1 - y)
        for name in ("y3", "y1", "y2", "y0"):
            go(g[name])
        g["cb"].wait_recv()
        add(y)

    dk_halo.wait_recv()
    ek = [jnp.zeros((1, half_width), F32) for _ in range(3)]
    for s in range(2):
        for i in range(toks // step):
            a = i * step
            fl = flags[s, a : a + step, :].astype(F32)
            dk = dkbuf[s, a : a + step, 0:half_width]
            ek[2] += jnp.sum(dk * ubuf[s, a + 8 : a + 8 + step, :], axis=0, keepdims=True)
            ek[1] += jnp.sum(
                dk * (fl[:, 0:1] * ubuf[s, a + 7 : a + 7 + step, :]), axis=0, keepdims=True
            )
            ek[0] += jnp.sum(
                dk * (fl[:, 1:2] * ubuf[s, a + 6 : a + 6 + step, :]), axis=0, keepdims=True
            )
            du = (
                tap2 * dk
                + tap1 * (fl[:, 2:3] * dkbuf[s, a + 1 : a + 1 + step, 0:half_width])
                + tap0 * (fl[:, 3:4] * dkbuf[s, a + 2 : a + 2 + step, 0:half_width])
            )
            dps[s, a : a + step, 0:half_width] = (
                du * proj[s, a : a + step, 2 * half_width :]
            ).astype(BF16)
            dps[s, a : a + step, 2 * half_width :] = (
                du * proj[s, a : a + step, 0:half_width]
            ).astype(BF16)
    for k in range(3):
        for q in range(4):
            chunk = jnp.broadcast_to(ek[k][:, 128 * q : 128 * q + 128], (8, 128))
            turned = pltpu.roll(chunk, 64, 1)
            even = jnp.where(is_one, jnp.where(low8, 0.0, turned), jnp.where(low8, chunk, 0.0))
            odd = jnp.where(is_one, jnp.where(low8, 0.0, chunk), jnp.where(low8, turned, 0.0))
            small_grad[2 + k : 3 + k, 256 * q : 256 * q + 128] = even[0:1]
            small_grad[2 + k : 3 + k, 256 * q + 128 : 256 * q + 256] = odd[0:1]

    for q in range(8):
        small_in[PLACES + q] = small_grad[:, 128 * q : 128 * q + 128]

    def small_back(m):
        target = lax.rem(v + m, PLACES)
        source = small_in.at[PLACES + lax.div(target, 4)]
        return small_copy(source, small_in.at[v], m, (back_send, back_recv))

    def small_back_start(m, _):
        small_back(m).start()
        return 0

    lax.fori_loop(1, PLACES, small_back_start, 0)
    small_in[v] = small_in[PLACES + lax.div(v, 4)]

    mix_core(w_mo, r_mo_c, mo_r, False)
    columns = 2 * part
    for h in range(2):
        dabs[h] = (
            tn(
                xs[...].reshape(2 * toks, width),
                dps[:, :, h * columns : (h + 1) * columns].reshape(2 * toks, columns),
            )
            .astype(BF16)
            .reshape(dabs.shape[1:])
        )
        go(mi_rs[h]["ca"])
        go(mi_rs[h]["cb"])
    mi_flat = w_mi[...].reshape(width, wide)
    sent(o_swap)
    o_send[...] = nt(dps[1 - x], mi_flat).astype(BF16)
    dh1_swap = go(remote(o_send, o_recv, xn))
    mix_core(dabs.at[0], r_mi_c.at[0], mi_rs[0], True)
    mix_core(dabs.at[1], r_mi_c.at[1], mi_rs[1], True)
    ou_g["a"].wait_recv()
    add_rows(hs, py, 0, dhp.at[pd, lo])
    go(ou_g["y0"])
    ou_g["b"].wait_recv()
    add_rows(hs, px, half, dhp.at[pd, hi])
    go(ou_g["x0"])
    go(ou_g["x1"])
    dn_r["z0"].wait_recv()
    for a in range(2):
        w_dn[a, z0, c] = plus(w_dn[a, z0, c], r_dn_0[a])
    go(dn_r["z1"])
    acc[p] = nt(dps[x], mi_flat)

    def mo_idx(a, b):
        return (a, b, y, c)

    def mi_idx(a, b):
        return (a, b, y, every, c)

    mo_parts = (w_mo, mo_idx, mo_r, r_mo_y, r_mo_0)
    mi_parts = [
        (dabs.at[h], mi_idx, mi_rs[h], r_mi_y.at[h], r_mi_0.at[h]) for h in range(2)
    ]

    def mix_three(w, idx, g, r_y, r_0):
        g["y3"].wait_recv()
        at = idx(1 - z1, 1 - z0)
        w[at] = plus(w[at], r_y[1 - z1, 1 - z0])
        go(g["s3"])

    def mix_one(w, idx, g, r_y, r_0):
        g["y1"].wait_recv()
        g["s3"].wait_recv()
        at = idx(1 - z1, z0)
        w[at] = plus(plus(w[at], r_y[1 - z1, z0]), r_0[1 - z1])
        go(g["s1"])

    def mix_two(w, idx, g, r_y, r_0):
        g["y2"].wait_recv()
        at = idx(z1, 1 - z0)
        w[at] = plus(w[at], r_y[z1, 1 - z0])
        go(g["s2"])

    def mix_last(w, idx, g, r_y, r_0):
        g["y0"].wait_recv()
        g["s2"].wait_recv()
        at = idx(z1, z0)
        w[at] = plus(plus(w[at], r_y[z1, z0]), r_0[z1])

    mix_three(*mo_parts)
    mix_three(*mi_parts[0])
    mix_three(*mi_parts[1])
    gu_sum_z1(1)
    gu_return(1)
    dh1_swap.wait_recv()

    def norm_one(at):
        dh = acc[p, at, :] + o_recv[at, :].astype(F32)
        values = tokens[at, :].astype(F32)
        inverse = inverse_rms(values)
        normed = values * inverse
        q = dh * g1
        input_grad[at, :] = input_grad[at, :] + inverse * (
            q - normed * jnp.mean(q * normed, axis=1, keepdims=True)
        )

    loop(toks, norm_one)

    stores = []

    def store(src, dst):
        copy = pltpu.make_async_copy(src, dst, store_sem.at[len(stores)])
        copy.start()
        stores.append(copy)

    store(input_grad, input_sum)

    mix_one(*mo_parts)
    mix_one(*mi_parts[0])
    mix_one(*mi_parts[1])
    mix_two(*mo_parts)
    mix_two(*mi_parts[0])
    mix_two(*mi_parts[1])
    gu_sum_z1(2)
    gu_return(2)
    for name in ("x0", "x1", "y0", "y1"):
        ou_g[name].wait_recv()

    def out_body(at):
        o_send[at, :] = (
            x2[at, :]
            + hs[p, at, :].astype(F32)
            + dhp[px, at, :].astype(F32)
            + dhp[py, at, :].astype(F32)
        ).astype(BF16)

    sent(dh1_swap)
    loop(toks, out_body)

    store(o_send, block_out)
    down_rows = w_dn.shape[3]
    def small_back_wait(m, _):
        small_back(m).wait()
        return 0

    lax.fori_loop(1, PLACES, small_back_wait, 0)
    total = small_in[0]
    for q in range(1, PLACES):
        total = total + small_in[q]
    total = total * factor
    small_out[...] = total

    mix_last(*mo_parts)
    dn_r["z1"].wait_recv()
    acc[3, 0:down_rows] = (w_dn[z1, z0, c].astype(F32) + r_dn_1[...].astype(F32)) * factor
    store(acc.at[3, pl.ds(0, down_rows)], dn_sum)
    mo_r["s1"].wait_recv()
    acc[2, 96 : 96 + rows] = (w_mo[z1, z0, y, c].astype(F32) + r_mo_1[...].astype(F32)) * factor
    store(acc.at[2, pl.ds(96, rows)], mo_sum)
    for copy in gu_back:
        copy.wait_recv()
    store(gu_stage, gu_sum)
    mi_back = []
    for h in range(2):
        mix_last(*mi_parts[h])
        mi_rs[h]["s1"].wait_recv()
        dabs[h, z1, z0, y, :, c] = plus(dabs[h, z1, z0, y, :, c], r_mi_1[h])
        into = pl.ds(h * columns, columns)
        mi_stage[x, :, into] = dabs[h, z1, z0, y, x, c]
        mi_back.append(go(remote(dabs.at[h, z1, z0, y, 1 - x, c], mi_stage.at[x, :, into], xn)))
    for copy in mi_back:
        copy.wait_recv()
    store(mi_stage, mi_sum)

    for copy in stores:
        copy.wait()
    for copy in list(started):
        sent(copy)


COPIES = 160


def finish(
    fsdp_count,
    copies_of_place,
    factor,
    block_sum,
    input_sum,
    small,
    mi_sum,
    mo_sum,
    gu_sum,
    dn_sum,
    mixer_in,
    gain_one,
    block_out,
    input_grad,
    gain_one_grad,
    mixer_in_grad,
    taps_grad,
    mixer_out_grad,
    gain_two_grad,
    gate_grad,
    up_grad,
    down_grad,
):
    input_grad[...] = input_sum[...]
    block_out[...] = block_sum[...]
    down_grad[...] = dn_sum[...]
    mixer_out_grad[...] = mo_sum[...]
    rows, ff = gate_grad.shape
    width = mixer_out_grad.shape[1]
    part, run, half_width = ff // 12, ff // 16, width // 2
    for ref, start in ((gate_grad, 0), (up_grad, part)):
        pieces = [
            jnp.concatenate(
                [gu_sum[at_p, j, :, start : start + part] for j in range(3)], axis=1
            ).astype(F32)
            * factor
            for at_p in range(4)
        ]
        ref[...] = jnp.concatenate(
            [pieces[q % 4][:, run * (q // 4) : run * (q // 4) + run] for q in range(16)], axis=1
        )
    low = lax.broadcasted_iota(jnp.int32, (rows, 128), 1) < 64
    by_row = jnp.zeros((rows, 128), F32)
    for b in range(3):
        for q in range(width // 256):
            at = b * half_width + 128 * q
            first = mi_sum[0, :, at : at + 128].astype(F32) * factor
            second = mi_sum[1, :, at : at + 128].astype(F32) * factor
            to = b * width + 256 * q
            even = jnp.where(low, first, pltpu.roll(second, 64, 1))
            odd = jnp.where(low, pltpu.roll(first, 64, 1), second)
            mixer_in_grad[:, to : to + 128] = even
            mixer_in_grad[:, to + 128 : to + 256] = odd
            by_row += even * mixer_in[:, to : to + 128].astype(F32)
            by_row += odd * mixer_in[:, to + 128 : to + 256].astype(F32)
    column = jnp.sum(by_row, axis=1, keepdims=True)
    row_at = lax.broadcasted_iota(jnp.int32, (rows, rows), 0)
    col_at = lax.broadcasted_iota(jnp.int32, (rows, rows), 1)
    turned = jnp.sum(jnp.where(row_at == col_at, column, 0.0), axis=0, keepdims=True)
    number = lax.axis_index("dp") * fsdp_count + lax.axis_index("fsdp")
    quarter = lax.rem(lax.div(number, copies_of_place), 4)
    values = small[...]
    own = values[:, 0:rows]
    for k in range(1, 4):
        own = jnp.where(quarter == k, values[:, k * rows : k * rows + rows], own)
    gain_one_grad[...] = turned / gain_one[...].astype(F32)
    gain_two_grad[...] = own[1:2]
    taps_grad[...] = own[2:5]


def per_device(
    fsdp_count,
    device_count,
    tokens,
    document_index,
    loss_token_mask,
    cotangent,
    first_gain,
    mixer_in,
    conv_kernel,
    mixer_out,
    second_gain,
    gate_weight,
    up_weight,
    down_weight,
):
    row_count, seq_here, width = tokens.shape
    toks = row_count * seq_here
    spare = device_count // PLACES
    groups = [[place * spare + k for k in range(spare)] for place in range(PLACES)]
    axes = ("dp", "fsdp")

    def joined(shard, axis=0):
        if spare == 1:
            return shard
        return lax.all_gather(shard, axes, axis=axis, tiled=True, axis_index_groups=groups)

    first_gain, second_gain = joined(first_gain), joined(second_gain)
    conv_kernel = joined(conv_kernel, 1)
    mixer_in, mixer_out = joined(mixer_in), joined(mixer_out)
    gate_weight, up_weight, down_weight = joined(gate_weight), joined(up_weight), joined(down_weight)
    rows = mixer_in.shape[0]
    down_rows = down_weight.shape[0]
    ff = gate_weight.shape[1]
    part = ff // 12
    half_width = width // 2
    wide = 3 * half_width
    factor = 1.0 / math.sqrt(toks * device_count)

    def vm(shape, dtype=BF16):
        return pltpu.VMEM(shape, dtype)

    half = toks // 2
    scratch = [
        vm((toks, width), F32),
        vm((toks, width)),
        vm((rows, 3 * width)),
        vm((rows, ff)),
        vm((rows, ff)),
        vm((8, 128), F32),
        vm((PLACES, 8, 128), F32),
        vm((8, width), F32),
        vm((PLACES + 8, 8, 128), F32),
        vm((2, 2, 2, 2, 2, rows, wide)),
        vm((2, 2, 2, 2, rows, width)),
        vm((3, 2, 2, 4, 2, rows, 2 * part)),
        vm((2, 2, 2, down_rows, width)),
        vm((2, rows, wide)),
        vm((4, 3, rows, 2 * part)),
        vm((2, toks, width)),
        vm((2, toks, 128)),
        vm((4, toks, width)),
        vm((4, toks, width)),
        vm((2, toks, wide), F32),
        vm((2, toks + 8, half_width), F32),
        vm((2, toks, half_width), F32),
        vm((2, toks, half_width)),
        vm((2, toks, wide)),
        vm((toks, width), F32),
        vm((toks, width)),
        vm((toks, width)),
        vm((2, toks + 8, 2 * part), F32),
        vm((2 * toks, part), F32),
        vm((4, toks, 3 * part)),
        vm((3, 2, 2, 2, 2, 2, rows, 2 * part)),
        vm((4, toks, width), F32),
        vm((4, toks, width)),
        vm((half, width)),
        vm((half, width)),
        vm((toks, width)),
        vm((toks, width)),
        vm((2, toks, width)),
        vm((2, 2, 2, 4, rows, 2 * part)),
        vm((3, 2, 4, rows, 2 * part)),
        vm((3, 4, rows, 2 * part)),
        vm((2, 2, down_rows, width)),
        vm((2, down_rows, width)),
        vm((down_rows, width)),
        vm((2, 2, 2, 2, 2, rows, 2 * part)),
        vm((2, 2, 2, 2, rows, 2 * part)),
        vm((2, 2, 2, rows, 2 * part)),
        vm((2, 2, rows, 2 * part)),
        vm((2, 2, 2, rows, width)),
        vm((2, 2, rows, width)),
        vm((2, rows, width)),
        vm((rows, width)),
        vm((8, width + half_width), F32),
        pltpu.SemaphoreType.DMA((COPIES,)),
        pltpu.SemaphoreType.DMA((COPIES,)),
        pltpu.SemaphoreType.DMA((7,)),
        pltpu.SemaphoreType.DMA((20,)),
        pltpu.SemaphoreType.DMA((PLACES,)),
        pltpu.SemaphoreType.DMA((PLACES,)),
        pltpu.SemaphoreType.DMA((PLACES,)),
        pltpu.SemaphoreType.DMA((PLACES,)),
        pltpu.SemaphoreType.REGULAR,
        pltpu.SemaphoreType.REGULAR,
    ]
    outs = [
        jax.ShapeDtypeStruct((toks, width), BF16),
        jax.ShapeDtypeStruct((toks, width), F32),
        jax.ShapeDtypeStruct((8, 128), F32),
        jax.ShapeDtypeStruct((2, rows, wide), BF16),
        jax.ShapeDtypeStruct((rows, width), F32),
        jax.ShapeDtypeStruct((4, 3, rows, 2 * part), BF16),
        jax.ShapeDtypeStruct((down_rows, width), F32),
    ]
    vmem = pl.BlockSpec(memory_space=pltpu.VMEM)
    hbm = pl.BlockSpec(memory_space=pl.ANY)
    result = pl.pallas_call(
        functools.partial(kernel, fsdp_count, spare, factor),
        out_shape=outs,
        in_specs=[hbm] * 2 + [vmem] * 5 + [hbm] * 5,
        out_specs=[hbm] * 2 + [vmem] + [hbm] * 4,
        scratch_shapes=scratch,
        compiler_params=pltpu.CompilerParams(
            collective_id=0, has_side_effects=True, vmem_limit_bytes=60 << 20
        ),
    )(
        tokens.reshape(toks, width),
        cotangent.reshape(toks, width),
        document_index,
        loss_token_mask,
        first_gain.reshape(1, rows),
        second_gain.reshape(1, rows),
        conv_kernel,
        mixer_in,
        mixer_out,
        gate_weight,
        up_weight,
        down_weight,
    )
    finished = pl.pallas_call(
        functools.partial(finish, fsdp_count, spare, factor),
        out_shape=[
            jax.ShapeDtypeStruct((toks, width), BF16),
            jax.ShapeDtypeStruct((toks, width), F32),
            jax.ShapeDtypeStruct((1, rows), F32),
            jax.ShapeDtypeStruct((rows, 3 * width), F32),
            jax.ShapeDtypeStruct((3, rows), F32),
            jax.ShapeDtypeStruct((rows, width), F32),
            jax.ShapeDtypeStruct((1, rows), F32),
            jax.ShapeDtypeStruct((rows, ff), F32),
            jax.ShapeDtypeStruct((rows, ff), F32),
            jax.ShapeDtypeStruct((down_rows, width), F32),
        ],
        in_specs=[vmem] * 9,
        out_specs=[vmem] * 10,
        compiler_params=pltpu.CompilerParams(vmem_limit_bytes=60 << 20),
    )(*result, mixer_in, first_gain.reshape(1, rows))
    block_out, input_grad, g_one, g_mi, g_taps, g_mo, g_two, g_gate, g_up, g_down = finished

    def shared(item, axis=0):
        if spare == 1:
            return item
        return lax.psum_scatter(
            item, axes, scatter_dimension=axis, axis_index_groups=groups, tiled=True
        )

    return (
        block_out.reshape(row_count, seq_here, width),
        input_grad.reshape(row_count, seq_here, width),
        shared(g_one.reshape(rows)),
        shared(g_mi),
        shared(g_taps, 1),
        shared(g_mo),
        shared(g_two.reshape(rows)),
        shared(g_gate),
        shared(g_up),
        shared(g_down),
    )


def solution(mesh):
    fsdp_count = mesh.shape["fsdp"]
    device_count = mesh.shape["dp"] * fsdp_count
    return jax.shard_map(
        functools.partial(per_device, fsdp_count, device_count),
        mesh=mesh,
        in_specs=(
            P("dp", "fsdp", None),
            P("dp", None),
            P("dp", "fsdp"),
            P("dp", "fsdp", None),
            P(("dp", "fsdp")),
            P(("dp", "fsdp"), None),
            P(None, ("dp", "fsdp")),
            P(("dp", "fsdp"), None),
            P(("dp", "fsdp")),
            P(("dp", "fsdp"), None),
            P(("dp", "fsdp"), None),
            P(("dp", "fsdp"), None),
        ),
        out_specs=(
            P("dp", "fsdp", None),
            P("dp", "fsdp", None),
            P(("dp", "fsdp")),
            P(("dp", "fsdp"), None),
            P(None, ("dp", "fsdp")),
            P(("dp", "fsdp"), None),
            P(("dp", "fsdp")),
            P(("dp", "fsdp"), None),
            P(("dp", "fsdp"), None),
            P(("dp", "fsdp"), None),
        ),
        check_vma=False,
    )
```

```python
import functools
import math

import jax
import jax.numpy as jnp
from jax import lax
from jax.experimental import pallas as pl
from jax.experimental.pallas import tpu as pltpu
from jax.sharding import PartitionSpec as P

EPSILON = 1e-05
MESH = pl.DeviceIdType.MESH
F32 = jnp.float32
BF16 = jnp.bfloat16
PLACES = 32


def nn(a, b):
    return jnp.dot(a, b, preferred_element_type=F32)


def nt(a, b):
    return lax.dot_general(a, b, (((1,), (1,)), ((), ())), preferred_element_type=F32)


def tn(a, b):
    return lax.dot_general(a, b, (((0,), (0,)), ((), ())), preferred_element_type=F32)


def kernel(
    fsdp_count,
    copies_of_place,
    factor,
    tokens_hbm,
    cotangent,
    document,
    loss_mask,
    gain_one,
    gain_two,
    taps,
    mixer_in_hbm,
    mixer_out,
    gate_hbm,
    up_hbm,
    down,
    block_out,
    input_sum,
    small_out,
    mi_sum,
    mo_sum,
    gu_sum,
    dn_sum,
    input_grad,
    tokens,
    mixer_in,
    gate,
    up,
    small_tile,
    small_all,
    small_grad,
    small_in,
    w_mi,
    w_mo,
    w_gu,
    w_dn,
    mi_stage,
    gu_stage,
    xs,
    flags,
    gs,
    hs,
    proj,
    ubuf,
    conv,
    ys,
    dps,
    x2,
    o_send,
    o_recv,
    pre,
    dm_buf,
    ms,
    dabs,
    acc,
    dhp,
    dh_a,
    dh_b,
    dh_x,
    dh_y,
    dos,
    r_gu_c,
    r_gu_0,
    r_gu_1,
    r_dn_c,
    r_dn_0,
    r_dn_1,
    r_mi_c,
    r_mi_y,
    r_mi_0,
    r_mi_1,
    r_mo_c,
    r_mo_y,
    r_mo_0,
    r_mo_1,
    rows_buf,
    send,
    recv,
    load_sem,
    store_sem,
    small_send,
    small_recv,
    back_send,
    back_recv,
    free_x,
    free_y,
):
    toks, width = tokens.shape
    dkbuf = pre
    rows = mixer_in.shape[0]
    half_width = width // 2
    units = w_dn.shape[0] * w_dn.shape[1] * w_dn.shape[2] * w_dn.shape[3]
    part = units // 3
    half = toks // 2
    step = 32

    dp, fs = lax.axis_index("dp"), lax.axis_index("fsdp")
    number = dp * fsdp_count + fs
    v = lax.div(number, copies_of_place)
    rep = lax.rem(number, copies_of_place)
    c = lax.rem(v, 2)
    x = lax.rem(lax.div(v, 2), 2)
    y = lax.rem(lax.div(v, 4), 2)
    z0 = lax.rem(lax.div(v, 8), 2)
    z1 = lax.div(v, 16)
    p = 2 * y + x
    px = 2 * y + (1 - x)
    py = 2 * (1 - y) + x
    pd = 2 * (1 - y) + (1 - x)

    def dev(place):
        whole = place * copies_of_place + rep
        return (lax.div(whole, fsdp_count), lax.rem(whole, fsdp_count))

    cn = dev(v + (1 - 2 * c))
    xn = dev(v + 2 * (1 - 2 * x))
    yn = dev(v + 4 * (1 - 2 * y))
    dn = dev(v + 2 * (1 - 2 * x) + 4 * (1 - 2 * y))
    z0n = dev(v + 8 * (1 - 2 * z0))
    z1n = dev(v + 16 * (1 - 2 * z1))
    following = (dp, lax.rem(fs + 1, fsdp_count))
    preceding = (dp, lax.rem(fs + fsdp_count - 1, fsdp_count))

    counter = [0]
    started = []

    def remote(src, dst, target):
        at = counter[0]
        counter[0] += 1
        return pltpu.make_async_remote_copy(
            src_ref=src, dst_ref=dst, send_sem=send.at[at], recv_sem=recv.at[at],
            device_id=target, device_id_type=MESH,
        )

    def go(copy):
        copy.start()
        started.append(copy)
        return copy

    def same(ref, target):
        return remote(ref, ref, target)

    def sent(copy):
        copy.wait_send()
        started[:] = [other for other in started if other is not copy]

    barrier = pltpu.get_barrier_semaphore()

    def greet(m, _):
        pl.semaphore_signal(
            barrier, inc=1, device_id=dev(lax.rem(v + m, PLACES)), device_id_type=MESH
        )
        return 0

    lax.fori_loop(1, PLACES, greet, 0)
    pl.semaphore_signal(barrier, inc=1, device_id=following, device_id_type=MESH)
    pl.semaphore_signal(barrier, inc=1, device_id=preceding, device_id_type=MESH)

    load_mixer = pltpu.make_async_copy(mixer_in_hbm, mixer_in, load_sem.at[3])
    load_tokens = pltpu.make_async_copy(tokens_hbm, tokens, load_sem.at[4])
    load_gate = pltpu.make_async_copy(gate_hbm, gate, load_sem.at[5])
    load_up = pltpu.make_async_copy(up_hbm, up, load_sem.at[6])
    load_mixer.start()
    load_out = pltpu.make_async_copy(mixer_out, w_mo.at[z1, z0, y, c], load_sem.at[0])
    load_down = pltpu.make_async_copy(down, w_dn.at[z1, z0, c], load_sem.at[1])
    load_cot = pltpu.make_async_copy(cotangent, gs.at[p], load_sem.at[2])
    load_out.start()
    load_down.start()
    load_cot.start()
    load_gate.start()
    load_up.start()
    load_tokens.start()

    lane = lax.broadcasted_iota(jnp.int32, (1, 128), 1)
    mine = lax.div(lane, 32) == lax.rem(v, 4)
    small_tile[...] = jnp.zeros_like(small_tile)

    def spread(values):
        wide = jnp.concatenate([values.astype(F32)] * 4, axis=1)
        return jnp.where(mine, wide, 0.0)

    small_tile[0:1, :] = spread(gain_one[...])
    small_tile[1:2, :] = spread(gain_two[...])
    small_tile[2:5, :] = spread(taps[...])

    lanes128 = lax.broadcasted_iota(jnp.int32, (rows, 128), 1)
    low = lanes128 < 64
    load_mixer.wait()
    for b in range(3):
        for q in range(width // 256):
            at = b * width + 256 * q
            even = mixer_in[:, at : at + 128].astype(F32)
            odd = mixer_in[:, at + 128 : at + 256].astype(F32)
            to = b * half_width + 128 * q
            mi_stage[0, :, to : to + 128] = jnp.where(low, even, pltpu.roll(odd, 64, 1)).astype(BF16)
            mi_stage[1, :, to : to + 128] = jnp.where(low, pltpu.roll(even, 64, 1), odd).astype(BF16)
    w_mi[z1, z0, y, x, c] = mi_stage[x]
    small_all[v] = small_tile[...]

    pl.semaphore_wait(barrier, PLACES + 1)

    def small_copy(src, dst, m, sems=(small_send, small_recv)):
        return pltpu.make_async_remote_copy(
            src_ref=src, dst_ref=dst, send_sem=sems[0].at[m], recv_sem=sems[1].at[m],
            device_id=dev(lax.rem(v + m, PLACES)), device_id_type=MESH,
        )

    def small_start(m, _):
        small_copy(small_tile, small_all.at[v], m).start()
        return 0

    mi_swap = go(remote(mi_stage.at[1 - x], w_mi.at[z1, z0, y, x, c], xn))
    lax.fori_loop(1, PLACES, small_start, 0)
    tok_swap = go(remote(tokens_hbm, xs.at[x], xn))

    def mo_at(a, b, yy, cc):
        return w_mo.at[a, b, yy, cc]

    def mi_at(a, b, yy, cc):
        return w_mi.at[a, b, yy, :, cc]

    every = slice(None)

    def mix_gather(at):
        return dict(
            s1=same(at(z1, z0, y, c), z1n),
            s2=same(at(z1, z0, y, c), z0n),
            s3=same(at(1 - z1, z0, y, c), z0n),
            y0=same(at(z1, z0, y, c), yn),
            y1=same(at(1 - z1, z0, y, c), yn),
            y2=same(at(z1, 1 - z0, y, c), yn),
            y3=same(at(1 - z1, 1 - z0, y, c), yn),
            ca=same(at(every, every, y, c), cn),
            cb=same(at(every, every, 1 - y, c), cn),
        )

    wide = 3 * half_width

    def mi_half(h):
        columns = pl.ds(h * (wide // 2), wide // 2)
        return lambda a, b, yy, cc: w_mi.at[a, b, yy, :, cc, :, columns]

    mo_g = mix_gather(mo_at)
    mi_gs = [mix_gather(mi_half(0)), mix_gather(mi_half(1))]
    load_out.wait()
    go(mo_g["s1"])
    go(mo_g["s2"])
    mi_swap.wait_recv()
    for g in mi_gs:
        for name in ("s1", "s2", "y0"):
            go(g[name])

    offset = fs * toks
    ids = document[...].astype(F32) + 1.0
    mask_row = loss_mask[...].astype(F32)
    id_lane = lax.broadcasted_iota(jnp.int32, (step, ids.shape[1]), 1)
    id_row = lax.broadcasted_iota(jnp.int32, (step, ids.shape[1]), 0)
    ma_lane = lax.broadcasted_iota(jnp.int32, (step, toks), 1)
    ma_row = lax.broadcasted_iota(jnp.int32, (step, toks), 0)
    fl_lane = lax.broadcasted_iota(jnp.int32, (step, 128), 1)

    def flag_rows(i, _):
        base = i * step
        at = pl.ds(pl.multiple_of(base, step), step)

        def column(shift):
            hit = id_lane == id_row + (offset + base + shift)
            return jnp.sum(jnp.where(hit, ids, 0.0), axis=1, keepdims=True)

        centre = column(0)
        tile = jnp.zeros((step, 128), F32)
        for k, shift in enumerate((-1, -2, 1, 2)):
            tile = jnp.where(
                jnp.logical_and(fl_lane == k, column(shift) == centre), 1.0, tile
            )
        flags[x, at, :] = tile.astype(BF16)
        keep = jnp.sum(
            jnp.where(ma_lane == ma_row + base, mask_row, 0.0), axis=1, keepdims=True
        )
        gs[p, at, :] = (gs[p, at, :].astype(F32) * keep).astype(BF16)
        return 0

    run = units // 4

    def pick(ref, at_p):
        whole = ref[...].astype(F32)
        return jnp.concatenate(
            [whole[:, run * (4 * z + at_p) : run * (4 * z + at_p) + run] for z in range(4)], axis=1
        ).astype(BF16)

    def forward(g, arrived, names):
        g[arrived].wait_recv()
        for name in names:
            go(g[name])

    def z_gather(at):
        return dict(
            s1=same(at(z1, z0, c), z1n),
            s2=same(at(z1, z0, c), z0n),
            s3=same(at(1 - z1, z0, c), z0n),
            core=same(at(every, every, c), cn),
        )

    dn_g = z_gather(lambda a, b, cc: w_dn.at[a, b, cc])
    gu_g = [z_gather(lambda a, b, cc, j=j: w_gu.at[j, a, b, :, cc]) for j in range(3)]

    def z_start(g):
        go(g["s1"])
        go(g["s2"])

    def z_forward(g):
        forward(g, "s1", ("s3",))

    def z_core(g):
        g["s2"].wait_recv()
        g["s3"].wait_recv()
        go(g["core"])

    def plane_gather(buf, halves):
        lo, hi = pl.ds(0, half), pl.ds(half, half)
        return dict(
            x0=same(buf.at[p, lo], xn),
            y1=same(buf.at[p, hi], yn),
            x1=same(buf.at[p, hi], xn),
            y0=same(buf.at[p, lo], yn),
            fx=same(buf.at[px, lo] if halves else buf.at[px], yn),
            **(dict(fy=same(buf.at[py, hi], xn)) if halves else {}),
        )

    def plane_forward(g):
        forward(g, "x0", ("fx",))
        forward(g, "y1", ("fy",))

    gs_g, hs_g = plane_gather(gs, False), plane_gather(hs, True)

    load_cot.wait()
    lax.fori_loop(0, toks // step, flag_rows, 0)
    flag_swap = go(same(flags.at[x], xn))
    load_gate.wait()
    load_up.wait()
    for at_p in range(4):
        picked_gate, picked_up = pick(gate, at_p), pick(up, at_p)
        for j in range(3):
            gu_stage[at_p, j, :, 0:part] = picked_gate[:, j * part : j * part + part]
            gu_stage[at_p, j, :, part:] = picked_up[:, j * part : j * part + part]
    load_tokens.wait()
    xs[x] = tokens[...]
    for j in range(3):
        w_gu[j, z1, z0, p, c] = gu_stage[p, j]

    go(mo_g["y0"])
    forward(mo_g, "s1", ("s3", "y1"))
    forward(mo_g, "s2", ("y2",))
    for g in mi_gs:
        forward(g, "s1", ("s3", "y1"))
        forward(g, "s2", ("y2",))
    gu_swap = [
        remote(gu_stage.at[px], w_gu.at[:, z1, z0, p, c], xn),
        remote(gu_stage.at[py], w_gu.at[:, z1, z0, p, c], yn),
        remote(gu_stage.at[pd], w_gu.at[:, z1, z0, p, c], dn),
    ]
    go(gu_swap[2])
    go(gu_swap[0])
    go(gs_g["x0"])
    go(gs_g["x1"])

    def small_wait(m, _):
        copy = small_copy(small_tile, small_all.at[v], m)
        copy.wait()
        return 0

    lax.fori_loop(1, PLACES, small_wait, 0)
    natural = []
    for q in range(8):
        natural.append(
            small_all[4 * q] + small_all[4 * q + 1] + small_all[4 * q + 2] + small_all[4 * q + 3]
        )
    for q in range(8):
        rows_buf[:, 128 * q : 128 * q + 128] = natural[q]
    low8 = lax.broadcasted_iota(jnp.int32, (8, 128), 1) < 64
    is_one = x == 1
    for q in range(4):
        even, odd = natural[2 * q], natural[2 * q + 1]
        first = jnp.where(low8, even, pltpu.roll(odd, 64, 1))
        second = jnp.where(low8, pltpu.roll(even, 64, 1), odd)
        rows_buf[:, width + 128 * q : width + 128 * q + 128] = jnp.where(is_one, second, first)
    g1 = rows_buf[0:1, 0:width]
    g2 = rows_buf[1:2, 0:width]
    tap0 = rows_buf[2:3, width : width + half_width]
    tap1 = rows_buf[3:4, width : width + half_width]
    tap2 = rows_buf[4:5, width : width + half_width]

    def inverse_rms(values):
        return lax.rsqrt(jnp.mean(values * values, axis=1, keepdims=True) + EPSILON)

    def loop(count, body):
        def wrapped(i, _):
            body(pl.ds(pl.multiple_of(i * step, step), step))
            return 0

        lax.fori_loop(0, count // step, wrapped, 0)

    def hidden_one(s):
        def body(at):
            values = xs[s, at, :].astype(F32)
            xs[s, at, :] = (values * inverse_rms(values) * g1).astype(BF16)

        loop(toks, body)

    for g in mi_gs:
        forward(g, "s3", ("y3",))
        go(g["ca"])
    forward(mo_g, "s3", ("y3",))
    go(mo_g["ca"])
    go(gu_swap[1])
    load_down.wait()
    z_start(dn_g)
    hidden_one(x)
    tok_swap.wait_recv()
    hidden_one(1 - x)
    for g in mi_gs:
        for name in ("y0", "y1", "y2", "y3"):
            g[name].wait_recv()
        go(g["cb"])
    go(gs_g["y1"])
    go(gs_g["y0"])
    for g in mi_gs:
        g["ca"].wait_recv()
        g["cb"].wait_recv()
    h1 = xs[...].reshape(2 * toks, width)
    proj[...] = nn(h1, w_mi[...].reshape(width, wide)).reshape(2, toks, wide)

    for s in range(2):
        def body(at, s=s):
            ubuf[s, pl.ds(pl.multiple_of(at.start + 8, 8), step), :] = (
                proj[s, at, 0:half_width] * proj[s, at, 2 * half_width :]
            )

        loop(toks, body)
    halo = go(remote(ubuf.at[:, pl.ds(toks, 8), :], ubuf.at[:, pl.ds(0, 8), :], following))
    z_forward(dn_g)
    for copy in gu_swap:
        copy.wait_recv()
    z_start(gu_g[0])
    z_start(gu_g[1])
    for name in ("y0", "y1", "y2", "y3"):
        mo_g[name].wait_recv()
    go(mo_g["cb"])
    flag_swap.wait_recv()
    halo.wait_recv()
    for s in range(2):
        for i in range(toks // step):
            a = i * step
            fl = flags[s, a : a + step, :].astype(F32)
            value = (
                tap2 * ubuf[s, a + 8 : a + 8 + step, :]
                + tap1 * (fl[:, 0:1] * ubuf[s, a + 7 : a + 7 + step, :])
                + tap0 * (fl[:, 1:2] * ubuf[s, a + 6 : a + 6 + step, :])
            )
            conv[s, a : a + step, :] = value
            ys[s, a : a + step, :] = (
                proj[s, a : a + step, half_width : 2 * half_width] * value
            ).astype(BF16)
    mo_g["ca"].wait_recv()
    mo_g["cb"].wait_recv()
    mo_flat = w_mo[...].reshape(half_width, width)
    o_send[...] = nn(ys[1 - x], mo_flat).astype(BF16)
    o_swap = go(remote(o_send, o_recv, xn))
    x2[...] = nn(ys[x], mo_flat)

    forward(gs_g, "x0", ())
    forward(gs_g, "x1", ("fx",))
    z_core(dn_g)
    for copy in gu_swap:
        sent(copy)
    sent(mi_swap)

    def second_body(at):
        values = tokens[at, :].astype(F32) + x2[at, :] + o_recv[at, :].astype(F32)
        x2[at, :] = values
        hs[p, at, :] = (values * inverse_rms(values) * g2).astype(BF16)

    o_swap.wait_recv()
    loop(toks, second_body)
    for name in ("x0", "y1", "x1", "y0"):
        go(hs_g[name])
    z_forward(gu_g[0])
    z_forward(gu_g[1])
    z_start(gu_g[2])
    plane_forward(hs_g)
    z_core(gu_g[0])

    ya, yb = 2 * y, 2 * (1 - y)

    def plane_pair(g, names):
        for name in names:
            g[name].wait_recv()

    def pair_rows(ref, base):
        return ref[pl.ds(base, 2)].reshape(2 * toks, width)

    def feed(j, base):
        w = w_gu[j].reshape(width, 2 * part)
        pre[:, 0:toks, :] = nn(pair_rows(hs, base), w).reshape(2, toks, 2 * part)
        down_rows = w_dn[...].reshape(units, width)[j * part : j * part + part]
        dm_buf[...] = nt(pair_rows(gs, base), down_rows)

        def body(i, _):
            at = pl.ds(pl.multiple_of(i * step, step), step)
            slot = base + lax.div(i, toks // step)
            inner = pl.ds(pl.multiple_of(lax.rem(i, toks // step) * step, step), step)
            which = lax.div(i, toks // step)
            a = pre[which, inner, 0:part]
            b = pre[which, inner, part:]
            d = dm_buf[at, :]
            sg = jax.nn.sigmoid(a)
            silu = a * sg
            ms[slot, inner, j * part : j * part + part] = (silu * b).astype(BF16)
            chunk = lax.rem(i, toks // step)
            at = (lax.div(chunk, 4), lax.rem(lax.div(chunk, 2), 2), lax.rem(chunk, 2))
            dabs[(j, lax.div(base, 2), which, *at, every, slice(0, part))] = (
                d * b * sg * (1.0 + a * (1.0 - sg))
            ).astype(BF16)
            dabs[(j, lax.div(base, 2), which, *at, every, slice(part, 2 * part))] = (
                d * silu
            ).astype(BF16)
            return 0

        lax.fori_loop(0, 2 * toks // step, body, 0)
        back = nt(dabs[j, lax.div(base, 2)].reshape(2 * toks, 2 * part), w)
        back = back.reshape(2, toks, width)
        if j == 0:
            acc[pl.ds(base, 2)] = back
        elif j == 1:
            acc[pl.ds(base, 2)] += back
        else:
            total = acc[pl.ds(base, 2)] + back
            acc[pl.ds(base, 2)] = total
            dhp[pl.ds(base, 2)] = total.astype(BF16)

    def gu_weight_grad(j):
        w_gu[j] = (
            tn(hs[...].reshape(4 * toks, width), dabs[j].reshape(4 * toks, 2 * part))
            .astype(BF16)
            .reshape(w_gu.shape[1:])
        )

    def plane_scatter(buf, r_a, r_b, r_x, r_y):
        lo, hi = pl.ds(0, half), pl.ds(half, half)
        return dict(
            a=remote(buf.at[pd, lo], r_a, xn),
            b=remote(buf.at[pd, hi], r_b, yn),
            x0=remote(buf.at[px, lo], r_x.at[lo], xn),
            y1=remote(buf.at[py, hi], r_y.at[hi], yn),
            x1=remote(buf.at[px, hi], r_x.at[hi], xn),
            y0=remote(buf.at[py, lo], r_y.at[lo], yn),
        )

    def add_rows(buf, slot, start, other):
        def body(at):
            into = pl.ds(pl.multiple_of(at.start + start, step), step)
            buf[slot, into, :] = (
                buf[slot, into, :].astype(F32) + other[at, :].astype(F32)
            ).astype(BF16)

        loop(half, body)

    def scatter_rest(g, buf, r_a, r_b):
        g["b"].wait_recv()
        add_rows(buf, px, half, r_b)
        go(g["x1"])
        g["a"].wait_recv()
        add_rows(buf, py, 0, r_a)
        go(g["y0"])

    def z_reduce(at, r_c, r_0, r_1):
        return dict(
            core=remote(at(every, every, 1 - c), r_c, cn),
            z0=remote(at(every, 1 - z0, c), r_0, z0n),
            z1=remote(at(1 - z1, z0, c), r_1, z1n),
        )

    gu_r = [
        z_reduce(lambda a, b, cc, j=j: w_gu.at[j, a, b, :, cc], r_gu_c.at[j % 2], r_gu_0.at[j], r_gu_1.at[j])
        for j in range(3)
    ]
    dn_r = z_reduce(lambda a, b, cc: w_dn.at[a, b, cc], r_dn_c, r_dn_0, r_dn_1)

    def plus(one, two):
        return (one.astype(F32) + two.astype(F32)).astype(BF16)

    def gu_after_core(j):
        gu_r[j]["core"].wait_recv()
        for a in range(2):
            for b in range(2):
                w_gu[j, a, b, :, c] = plus(w_gu[j, a, b, :, c], r_gu_c[j % 2, a, b])
        go(gu_r[j]["z0"])

    def gu_after_z0(j):
        gu_r[j]["z0"].wait_recv()
        for a in range(2):
            w_gu[j, a, z0, :, c] = plus(w_gu[j, a, z0, :, c], r_gu_0[j, a])
        go(gu_r[j]["z1"])

    gu_back = []

    def gu_sum_z1(j):
        gu_r[j]["z1"].wait_recv()
        w_gu[j, z1, z0, :, c] = plus(w_gu[j, z1, z0, :, c], r_gu_1[j])
        gu_stage[p, j] = w_gu[j, z1, z0, p, c]

    def gu_return(j):
        for place, target in ((px, xn), (py, yn), (pd, dn)):
            gu_back.append(go(remote(w_gu.at[j, z1, z0, place, c], gu_stage.at[p, j], target)))

    def gathered(g):
        for name in ("s1", "s2", "s3", "core"):
            sent(g[name])

    dn_g["core"].wait_recv()
    plane_pair(hs_g, ("x1",))
    gu_g[0]["core"].wait_recv()
    feed(0, ya)
    z_core(gu_g[1])
    plane_pair(gs_g, ("y0", "y1", "fx"))
    plane_pair(hs_g, ("y0", "fx", "fy"))
    feed(0, yb)
    z_forward(gu_g[2])
    gathered(gu_g[0])
    gu_weight_grad(0)
    go(gu_r[0]["core"])
    gu_after_core(0)
    gu_g[1]["core"].wait_recv()
    feed(1, yb)
    z_core(gu_g[2])
    feed(1, ya)
    gu_g[2]["core"].wait_recv()
    feed(2, yb)
    dh_g = plane_scatter(dhp, dh_a, dh_b, dh_x, dh_y)
    go(dh_g["a"])
    go(dh_g["b"])
    go(dh_g["y1"])
    gu_after_z0(0)
    feed(2, ya)
    go(dh_g["x0"])
    gathered(gu_g[1])
    gu_weight_grad(1)
    go(gu_r[1]["core"])
    gathered(gu_g[2])
    gu_weight_grad(2)
    gu_after_core(1)
    go(gu_r[2]["core"])
    scatter_rest(dh_g, dhp, dh_a, dh_b)

    for name in ("x0", "x1", "y0", "y1", "fx", "fy"):
        sent(hs_g[name])
    dn_flat = w_dn[...].reshape(units, width)
    for base in (ya, yb):
        m = ms[pl.ds(base, 2)].reshape(2 * toks, units)
        hs[pl.ds(base, 2)] = nn(m, dn_flat).astype(BF16).reshape(2, toks, width)
    gu_after_core(2)
    gathered(dn_g)
    w_dn[...] = (
        tn(ms[...].reshape(4 * toks, units), gs[...].reshape(4 * toks, width))
        .astype(BF16)
        .reshape(w_dn.shape)
    )
    go(dn_r["core"])
    dn_r["core"].wait_recv()
    for a in range(2):
        for b in range(2):
            w_dn[a, b, c] = plus(w_dn[a, b, c], r_dn_c[a, b])
    go(dn_r["z0"])

    for name in ("x0", "x1", "y0", "y1"):
        dh_g[name].wait_recv()
    small_grad[...] = jnp.zeros_like(small_grad)

    def norm_two(at):
        dh = acc[p, at, :] + dh_x[at, :].astype(F32) + dh_y[at, :].astype(F32)
        values = x2[at, :]
        inverse = inverse_rms(values)
        normed = values * inverse
        small_grad[1:2, :] += jnp.sum(dh * normed, axis=0, keepdims=True)
        q = dh * g2
        grad = gs[p, at, :].astype(F32) + inverse * (
            q - normed * jnp.mean(q * normed, axis=1, keepdims=True)
        )
        input_grad[at, :] = grad
        dos[x, at, :] = grad.astype(BF16)

    loop(toks, norm_two)
    do_swap = go(same(dos.at[x], xn))
    lo, hi = pl.ds(0, half), pl.ds(half, half)
    ou_g = plane_scatter(hs, dhp.at[py, lo], dhp.at[px, hi], dhp.at[p], dhp.at[p])
    for copy in dh_g.values():
        sent(copy)
    pl.semaphore_signal(free_x, inc=1, device_id=xn, device_id_type=MESH)
    pl.semaphore_signal(free_y, inc=1, device_id=yn, device_id_type=MESH)
    pl.semaphore_wait(free_x, 1)
    pl.semaphore_wait(free_y, 1)
    for name in ("b", "y1", "a"):
        go(ou_g[name])

    mo_flat = w_mo[...].reshape(half_width, width)

    def split_dy(s):
        def body(at):
            dy = dkbuf[s, at, 0:half_width]
            dps[s, at, half_width : 2 * half_width] = (dy * conv[s, at, :]).astype(BF16)
            dkbuf[s, at, 0:half_width] = dy * proj[s, at, half_width : 2 * half_width]

        loop(toks, body)

    dkbuf[x, 0:toks, 0:half_width] = nt(dos[x], mo_flat)
    split_dy(x)
    gu_after_z0(1)
    gu_sum_z1(0)
    gu_return(0)
    gu_after_z0(2)
    do_swap.wait_recv()
    dkbuf[1 - x, 0:toks, 0:half_width] = nt(dos[1 - x], mo_flat)
    split_dy(1 - x)
    dk_halo = go(
        remote(
            dkbuf.at[:, pl.ds(0, 8), pl.ds(0, half_width)],
            dkbuf.at[:, pl.ds(toks, 8), pl.ds(0, half_width)],
            preceding,
        )
    )
    for g in (mo_g, *mi_gs):
        for copy in g.values():
            sent(copy)
    w_mo[...] = (
        tn(ys[...].reshape(2 * toks, half_width), dos[...].reshape(2 * toks, width))
        .astype(BF16)
        .reshape(w_mo.shape)
    )

    def mix_reduce(at, r_c, r_y, r_0, r_1):
        return dict(
            ca=remote(at(every, every, 1 - y, 1 - c), r_c.at[:, :, 1 - y], cn),
            cb=remote(at(every, every, y, 1 - c), r_c.at[:, :, y], cn),
            y3=remote(at(1 - z1, 1 - z0, 1 - y, c), r_y.at[1 - z1, 1 - z0], yn),
            y2=remote(at(z1, 1 - z0, 1 - y, c), r_y.at[z1, 1 - z0], yn),
            y1=remote(at(1 - z1, z0, 1 - y, c), r_y.at[1 - z1, z0], yn),
            y0=remote(at(z1, z0, 1 - y, c), r_y.at[z1, z0], yn),
            s3=remote(at(1 - z1, 1 - z0, y, c), r_0.at[1 - z1], z0n),
            s2=remote(at(z1, 1 - z0, y, c), r_0.at[z1], z0n),
            s1=remote(at(1 - z1, z0, y, c), r_1, z1n),
        )

    mo_r = mix_reduce(mo_at, r_mo_c, r_mo_y, r_mo_0, r_mo_1)
    mi_rs = [
        mix_reduce(
            lambda a, b, yy, cc, h=h: dabs.at[h, a, b, yy, :, cc],
            r_mi_c.at[h], r_mi_y.at[h], r_mi_0.at[h], r_mi_1.at[h],
        )
        for h in range(2)
    ]
    go(mo_r["ca"])
    go(mo_r["cb"])
    def mix_core(w, r_c, g, with_x):
        def add(yy):
            for a in range(2):
                for b in range(2):
                    if with_x:
                        w[a, b, yy, :, c] = plus(w[a, b, yy, :, c], r_c[a, b, yy])
                    else:
                        w[a, b, yy, c] = plus(w[a, b, yy, c], r_c[a, b, yy])

        g["ca"].wait_recv()
        add(1 - y)
        for name in ("y3", "y1", "y2", "y0"):
            go(g[name])
        g["cb"].wait_recv()
        add(y)

    dk_halo.wait_recv()
    ek = [jnp.zeros((1, half_width), F32) for _ in range(3)]
    for s in range(2):
        for i in range(toks // step):
            a = i * step
            fl = flags[s, a : a + step, :].astype(F32)
            dk = dkbuf[s, a : a + step, 0:half_width]
            ek[2] += jnp.sum(dk * ubuf[s, a + 8 : a + 8 + step, :], axis=0, keepdims=True)
            ek[1] += jnp.sum(
                dk * (fl[:, 0:1] * ubuf[s, a + 7 : a + 7 + step, :]), axis=0, keepdims=True
            )
            ek[0] += jnp.sum(
                dk * (fl[:, 1:2] * ubuf[s, a + 6 : a + 6 + step, :]), axis=0, keepdims=True
            )
            du = (
                tap2 * dk
                + tap1 * (fl[:, 2:3] * dkbuf[s, a + 1 : a + 1 + step, 0:half_width])
                + tap0 * (fl[:, 3:4] * dkbuf[s, a + 2 : a + 2 + step, 0:half_width])
            )
            dps[s, a : a + step, 0:half_width] = (
                du * proj[s, a : a + step, 2 * half_width :]
            ).astype(BF16)
            dps[s, a : a + step, 2 * half_width :] = (
                du * proj[s, a : a + step, 0:half_width]
            ).astype(BF16)
    for k in range(3):
        for q in range(4):
            chunk = jnp.broadcast_to(ek[k][:, 128 * q : 128 * q + 128], (8, 128))
            turned = pltpu.roll(chunk, 64, 1)
            even = jnp.where(is_one, jnp.where(low8, 0.0, turned), jnp.where(low8, chunk, 0.0))
            odd = jnp.where(is_one, jnp.where(low8, 0.0, chunk), jnp.where(low8, turned, 0.0))
            small_grad[2 + k : 3 + k, 256 * q : 256 * q + 128] = even[0:1]
            small_grad[2 + k : 3 + k, 256 * q + 128 : 256 * q + 256] = odd[0:1]

    for q in range(8):
        small_in[PLACES + q] = small_grad[:, 128 * q : 128 * q + 128]

    def small_back(m):
        target = lax.rem(v + m, PLACES)
        source = small_in.at[PLACES + lax.div(target, 4)]
        return small_copy(source, small_in.at[v], m, (back_send, back_recv))

    def small_back_start(m, _):
        small_back(m).start()
        return 0

    lax.fori_loop(1, PLACES, small_back_start, 0)
    small_in[v] = small_in[PLACES + lax.div(v, 4)]

    mix_core(w_mo, r_mo_c, mo_r, False)
    columns = 2 * part
    for h in range(2):
        dabs[h] = (
            tn(
                xs[...].reshape(2 * toks, width),
                dps[:, :, h * columns : (h + 1) * columns].reshape(2 * toks, columns),
            )
            .astype(BF16)
            .reshape(dabs.shape[1:])
        )
        go(mi_rs[h]["ca"])
        go(mi_rs[h]["cb"])
    mi_flat = w_mi[...].reshape(width, wide)
    sent(o_swap)
    o_send[...] = nt(dps[1 - x], mi_flat).astype(BF16)
    dh1_swap = go(remote(o_send, o_recv, xn))
    mix_core(dabs.at[0], r_mi_c.at[0], mi_rs[0], True)
    mix_core(dabs.at[1], r_mi_c.at[1], mi_rs[1], True)
    ou_g["a"].wait_recv()
    add_rows(hs, py, 0, dhp.at[pd, lo])
    go(ou_g["y0"])
    ou_g["b"].wait_recv()
    add_rows(hs, px, half, dhp.at[pd, hi])
    go(ou_g["x0"])
    go(ou_g["x1"])
    dn_r["z0"].wait_recv()
    for a in range(2):
        w_dn[a, z0, c] = plus(w_dn[a, z0, c], r_dn_0[a])
    go(dn_r["z1"])
    acc[p] = nt(dps[x], mi_flat)

    def mo_idx(a, b):
        return (a, b, y, c)

    def mi_idx(a, b):
        return (a, b, y, every, c)

    mo_parts = (w_mo, mo_idx, mo_r, r_mo_y, r_mo_0)
    mi_parts = [
        (dabs.at[h], mi_idx, mi_rs[h], r_mi_y.at[h], r_mi_0.at[h]) for h in range(2)
    ]

    def mix_three(w, idx, g, r_y, r_0):
        g["y3"].wait_recv()
        at = idx(1 - z1, 1 - z0)
        w[at] = plus(w[at], r_y[1 - z1, 1 - z0])
        go(g["s3"])

    def mix_one(w, idx, g, r_y, r_0):
        g["y1"].wait_recv()
        g["s3"].wait_recv()
        at = idx(1 - z1, z0)
        w[at] = plus(plus(w[at], r_y[1 - z1, z0]), r_0[1 - z1])
        go(g["s1"])

    def mix_two(w, idx, g, r_y, r_0):
        g["y2"].wait_recv()
        at = idx(z1, 1 - z0)
        w[at] = plus(w[at], r_y[z1, 1 - z0])
        go(g["s2"])

    def mix_last(w, idx, g, r_y, r_0):
        g["y0"].wait_recv()
        g["s2"].wait_recv()
        at = idx(z1, z0)
        w[at] = plus(plus(w[at], r_y[z1, z0]), r_0[z1])

    mix_three(*mo_parts)
    mix_three(*mi_parts[0])
    mix_three(*mi_parts[1])
    gu_sum_z1(1)
    gu_return(1)
    dh1_swap.wait_recv()

    def norm_one(at):
        dh = acc[p, at, :] + o_recv[at, :].astype(F32)
        values = tokens[at, :].astype(F32)
        inverse = inverse_rms(values)
        normed = values * inverse
        q = dh * g1
        input_grad[at, :] = input_grad[at, :] + inverse * (
            q - normed * jnp.mean(q * normed, axis=1, keepdims=True)
        )

    loop(toks, norm_one)

    stores = []

    def store(src, dst):
        copy = pltpu.make_async_copy(src, dst, store_sem.at[len(stores)])
        copy.start()
        stores.append(copy)

    store(input_grad, input_sum)

    mix_one(*mo_parts)
    mix_one(*mi_parts[0])
    mix_one(*mi_parts[1])
    mix_two(*mo_parts)
    mix_two(*mi_parts[0])
    mix_two(*mi_parts[1])
    gu_sum_z1(2)
    gu_return(2)
    for name in ("x0", "x1", "y0", "y1"):
        ou_g[name].wait_recv()

    def out_body(at):
        o_send[at, :] = (
            x2[at, :]
            + hs[p, at, :].astype(F32)
            + dhp[px, at, :].astype(F32)
            + dhp[py, at, :].astype(F32)
        ).astype(BF16)

    sent(dh1_swap)
    loop(toks, out_body)

    store(o_send, block_out)
    down_rows = w_dn.shape[3]
    def small_back_wait(m, _):
        small_back(m).wait()
        return 0

    lax.fori_loop(1, PLACES, small_back_wait, 0)
    total = small_in[0]
    for q in range(1, PLACES):
        total = total + small_in[q]
    total = total * factor
    small_out[...] = total

    mix_last(*mo_parts)
    dn_r["z1"].wait_recv()
    acc[3, 0:down_rows] = (w_dn[z1, z0, c].astype(F32) + r_dn_1[...].astype(F32)) * factor
    store(acc.at[3, pl.ds(0, down_rows)], dn_sum)
    mo_r["s1"].wait_recv()
    acc[2, 96 : 96 + rows] = (w_mo[z1, z0, y, c].astype(F32) + r_mo_1[...].astype(F32)) * factor
    store(acc.at[2, pl.ds(96, rows)], mo_sum)
    for copy in gu_back:
        copy.wait_recv()
    store(gu_stage, gu_sum)
    mi_back = []
    for h in range(2):
        mix_last(*mi_parts[h])
        mi_rs[h]["s1"].wait_recv()
        dabs[h, z1, z0, y, :, c] = plus(dabs[h, z1, z0, y, :, c], r_mi_1[h])
        into = pl.ds(h * columns, columns)
        mi_stage[x, :, into] = dabs[h, z1, z0, y, x, c]
        mi_back.append(go(remote(dabs.at[h, z1, z0, y, 1 - x, c], mi_stage.at[x, :, into], xn)))
    for copy in mi_back:
        copy.wait_recv()
    store(mi_stage, mi_sum)

    for copy in stores:
        copy.wait()
    for copy in list(started):
        sent(copy)


COPIES = 160


def finish(
    fsdp_count,
    copies_of_place,
    factor,
    block_sum,
    input_sum,
    small,
    mi_sum,
    mo_sum,
    gu_sum,
    dn_sum,
    mixer_in,
    gain_one,
    block_out,
    input_grad,
    gain_one_grad,
    mixer_in_grad,
    taps_grad,
    mixer_out_grad,
    gain_two_grad,
    gate_grad,
    up_grad,
    down_grad,
):
    input_grad[...] = input_sum[...]
    block_out[...] = block_sum[...]
    down_grad[...] = dn_sum[...]
    mixer_out_grad[...] = mo_sum[...]
    rows, ff = gate_grad.shape
    width = mixer_out_grad.shape[1]
    part, run, half_width = ff // 12, ff // 16, width // 2
    for ref, start in ((gate_grad, 0), (up_grad, part)):
        pieces = [
            jnp.concatenate(
                [gu_sum[at_p, j, :, start : start + part] for j in range(3)], axis=1
            ).astype(F32)
            * factor
            for at_p in range(4)
        ]
        ref[...] = jnp.concatenate(
            [pieces[q % 4][:, run * (q // 4) : run * (q // 4) + run] for q in range(16)], axis=1
        )
    low = lax.broadcasted_iota(jnp.int32, (rows, 128), 1) < 64
    by_row = jnp.zeros((rows, 128), F32)
    for b in range(3):
        for q in range(width // 256):
            at = b * half_width + 128 * q
            first = mi_sum[0, :, at : at + 128].astype(F32) * factor
            second = mi_sum[1, :, at : at + 128].astype(F32) * factor
            to = b * width + 256 * q
            even = jnp.where(low, first, pltpu.roll(second, 64, 1))
            odd = jnp.where(low, pltpu.roll(first, 64, 1), second)
            mixer_in_grad[:, to : to + 128] = even
            mixer_in_grad[:, to + 128 : to + 256] = odd
            by_row += even * mixer_in[:, to : to + 128].astype(F32)
            by_row += odd * mixer_in[:, to + 128 : to + 256].astype(F32)
    column = jnp.sum(by_row, axis=1, keepdims=True)
    row_at = lax.broadcasted_iota(jnp.int32, (rows, rows), 0)
    col_at = lax.broadcasted_iota(jnp.int32, (rows, rows), 1)
    turned = jnp.sum(jnp.where(row_at == col_at, column, 0.0), axis=0, keepdims=True)
    number = lax.axis_index("dp") * fsdp_count + lax.axis_index("fsdp")
    quarter = lax.rem(lax.div(number, copies_of_place), 4)
    values = small[...]
    own = values[:, 0:rows]
    for k in range(1, 4):
        own = jnp.where(quarter == k, values[:, k * rows : k * rows + rows], own)
    gain_one_grad[...] = turned / gain_one[...].astype(F32)
    gain_two_grad[...] = own[1:2]
    taps_grad[...] = own[2:5]


def per_device(
    fsdp_count,
    device_count,
    tokens,
    document_index,
    loss_token_mask,
    cotangent,
    first_gain,
    mixer_in,
    conv_kernel,
    mixer_out,
    second_gain,
    gate_weight,
    up_weight,
    down_weight,
):
    row_count, seq_here, width = tokens.shape
    toks = row_count * seq_here
    spare = device_count // PLACES
    groups = [[place * spare + k for k in range(spare)] for place in range(PLACES)]
    axes = ("dp", "fsdp")

    def joined(shard, axis=0):
        if spare == 1:
            return shard
        return lax.all_gather(shard, axes, axis=axis, tiled=True, axis_index_groups=groups)

    first_gain, second_gain = joined(first_gain), joined(second_gain)
    conv_kernel = joined(conv_kernel, 1)
    mixer_in, mixer_out = joined(mixer_in), joined(mixer_out)
    gate_weight, up_weight, down_weight = joined(gate_weight), joined(up_weight), joined(down_weight)
    rows = mixer_in.shape[0]
    down_rows = down_weight.shape[0]
    ff = gate_weight.shape[1]
    part = ff // 12
    half_width = width // 2
    wide = 3 * half_width
    factor = 1.0 / math.sqrt(toks * device_count)

    def vm(shape, dtype=BF16):
        return pltpu.VMEM(shape, dtype)

    half = toks // 2
    scratch = [
        vm((toks, width), F32),
        vm((toks, width)),
        vm((rows, 3 * width)),
        vm((rows, ff)),
        vm((rows, ff)),
        vm((8, 128), F32),
        vm((PLACES, 8, 128), F32),
        vm((8, width), F32),
        vm((PLACES + 8, 8, 128), F32),
        vm((2, 2, 2, 2, 2, rows, wide)),
        vm((2, 2, 2, 2, rows, width)),
        vm((3, 2, 2, 4, 2, rows, 2 * part)),
        vm((2, 2, 2, down_rows, width)),
        vm((2, rows, wide)),
        vm((4, 3, rows, 2 * part)),
        vm((2, toks, width)),
        vm((2, toks, 128)),
        vm((4, toks, width)),
        vm((4, toks, width)),
        vm((2, toks, wide), F32),
        vm((2, toks + 8, half_width), F32),
        vm((2, toks, half_width), F32),
        vm((2, toks, half_width)),
        vm((2, toks, wide)),
        vm((toks, width), F32),
        vm((toks, width)),
        vm((toks, width)),
        vm((2, toks + 8, 2 * part), F32),
        vm((2 * toks, part), F32),
        vm((4, toks, 3 * part)),
        vm((3, 2, 2, 2, 2, 2, rows, 2 * part)),
        vm((4, toks, width), F32),
        vm((4, toks, width)),
        vm((half, width)),
        vm((half, width)),
        vm((toks, width)),
        vm((toks, width)),
        vm((2, toks, width)),
        vm((2, 2, 2, 4, rows, 2 * part)),
        vm((3, 2, 4, rows, 2 * part)),
        vm((3, 4, rows, 2 * part)),
        vm((2, 2, down_rows, width)),
        vm((2, down_rows, width)),
        vm((down_rows, width)),
        vm((2, 2, 2, 2, 2, rows, 2 * part)),
        vm((2, 2, 2, 2, rows, 2 * part)),
        vm((2, 2, 2, rows, 2 * part)),
        vm((2, 2, rows, 2 * part)),
        vm((2, 2, 2, rows, width)),
        vm((2, 2, rows, width)),
        vm((2, rows, width)),
        vm((rows, width)),
        vm((8, width + half_width), F32),
        pltpu.SemaphoreType.DMA((COPIES,)),
        pltpu.SemaphoreType.DMA((COPIES,)),
        pltpu.SemaphoreType.DMA((7,)),
        pltpu.SemaphoreType.DMA((20,)),
        pltpu.SemaphoreType.DMA((PLACES,)),
        pltpu.SemaphoreType.DMA((PLACES,)),
        pltpu.SemaphoreType.DMA((PLACES,)),
        pltpu.SemaphoreType.DMA((PLACES,)),
        pltpu.SemaphoreType.REGULAR,
        pltpu.SemaphoreType.REGULAR,
    ]
    outs = [
        jax.ShapeDtypeStruct((toks, width), BF16),
        jax.ShapeDtypeStruct((toks, width), F32),
        jax.ShapeDtypeStruct((8, 128), F32),
        jax.ShapeDtypeStruct((2, rows, wide), BF16),
        jax.ShapeDtypeStruct((rows, width), F32),
        jax.ShapeDtypeStruct((4, 3, rows, 2 * part), BF16),
        jax.ShapeDtypeStruct((down_rows, width), F32),
    ]
    vmem = pl.BlockSpec(memory_space=pltpu.VMEM)
    hbm = pl.BlockSpec(memory_space=pl.ANY)
    result = pl.pallas_call(
        functools.partial(kernel, fsdp_count, spare, factor),
        out_shape=outs,
        in_specs=[hbm] * 2 + [vmem] * 5 + [hbm] * 5,
        out_specs=[hbm] * 2 + [vmem] + [hbm] * 4,
        scratch_shapes=scratch,
        compiler_params=pltpu.CompilerParams(
            collective_id=0, has_side_effects=True, vmem_limit_bytes=60 << 20
        ),
    )(
        tokens.reshape(toks, width),
        cotangent.reshape(toks, width),
        document_index,
        loss_token_mask,
        first_gain.reshape(1, rows),
        second_gain.reshape(1, rows),
        conv_kernel,
        mixer_in,
        mixer_out,
        gate_weight,
        up_weight,
        down_weight,
    )
    finished = pl.pallas_call(
        functools.partial(finish, fsdp_count, spare, factor),
        out_shape=[
            jax.ShapeDtypeStruct((toks, width), BF16),
            jax.ShapeDtypeStruct((toks, width), F32),
            jax.ShapeDtypeStruct((1, rows), F32),
            jax.ShapeDtypeStruct((rows, 3 * width), F32),
            jax.ShapeDtypeStruct((3, rows), F32),
            jax.ShapeDtypeStruct((rows, width), F32),
            jax.ShapeDtypeStruct((1, rows), F32),
            jax.ShapeDtypeStruct((rows, ff), F32),
            jax.ShapeDtypeStruct((rows, ff), F32),
            jax.ShapeDtypeStruct((down_rows, width), F32),
        ],
        in_specs=[vmem] * 9,
        out_specs=[vmem] * 10,
        compiler_params=pltpu.CompilerParams(vmem_limit_bytes=60 << 20),
    )(*result, mixer_in, first_gain.reshape(1, rows))
    block_out, input_grad, g_one, g_mi, g_taps, g_mo, g_two, g_gate, g_up, g_down = finished

    def shared(item, axis=0):
        if spare == 1:
            return item
        return lax.psum_scatter(
            item, axes, scatter_dimension=axis, axis_index_groups=groups, tiled=True
        )

    return (
        block_out.reshape(row_count, seq_here, width),
        input_grad.reshape(row_count, seq_here, width),
        shared(g_one.reshape(rows)),
        shared(g_mi),
        shared(g_taps, 1),
        shared(g_mo),
        shared(g_two.reshape(rows)),
        shared(g_gate),
        shared(g_up),
        shared(g_down),
    )


def solution(mesh):
    fsdp_count = mesh.shape["fsdp"]
    device_count = mesh.shape["dp"] * fsdp_count
    return jax.shard_map(
        functools.partial(per_device, fsdp_count, device_count),
        mesh=mesh,
        in_specs=(
            P("dp", "fsdp", None),
            P("dp", None),
            P("dp", "fsdp"),
            P("dp", "fsdp", None),
            P(("dp", "fsdp")),
            P(("dp", "fsdp"), None),
            P(None, ("dp", "fsdp")),
            P(("dp", "fsdp"), None),
            P(("dp", "fsdp")),
            P(("dp", "fsdp"), None),
            P(("dp", "fsdp"), None),
            P(("dp", "fsdp"), None),
        ),
        out_specs=(
            P("dp", "fsdp", None),
            P("dp", "fsdp", None),
            P(("dp", "fsdp")),
            P(("dp", "fsdp"), None),
            P(None, ("dp", "fsdp")),
            P(("dp", "fsdp"), None),
            P(("dp", "fsdp")),
            P(("dp", "fsdp"), None),
            P(("dp", "fsdp"), None),
            P(("dp", "fsdp"), None),
        ),
        check_vma=False,
    )
```

```python
import functools
import math

import jax
import jax.numpy as jnp
from jax import lax
from jax.experimental import pallas as pl
from jax.experimental.pallas import tpu as pltpu
from jax.sharding import PartitionSpec as P

EPSILON = 1e-05
MESH = pl.DeviceIdType.MESH
F32 = jnp.float32
BF16 = jnp.bfloat16
PLACES = 32


def nn(a, b):
    return jnp.dot(a, b, preferred_element_type=F32)


def nt(a, b):
    return lax.dot_general(a, b, (((1,), (1,)), ((), ())), preferred_element_type=F32)


def tn(a, b):
    return lax.dot_general(a, b, (((0,), (0,)), ((), ())), preferred_element_type=F32)


def kernel(
    fsdp_count,
    copies_of_place,
    factor,
    tokens_hbm,
    cotangent,
    document,
    loss_mask,
    gain_one,
    gain_two,
    taps,
    mixer_in_hbm,
    mixer_out,
    gate_hbm,
    up_hbm,
    down,
    block_out,
    input_sum,
    small_out,
    mi_sum,
    mo_sum,
    gu_sum,
    dn_sum,
    input_grad,
    tokens,
    mixer_in,
    gate,
    up,
    small_tile,
    small_all,
    small_grad,
    small_in,
    w_mi,
    w_mo,
    w_gu,
    w_dn,
    mi_stage,
    gu_stage,
    xs,
    flags,
    gs,
    hs,
    proj,
    ubuf,
    conv,
    ys,
    dps,
    x2,
    o_send,
    o_recv,
    pre,
    dm_buf,
    ms,
    dabs,
    acc,
    dhp,
    dh_a,
    dh_b,
    dh_x,
    dh_y,
    dos,
    r_gu_c,
    r_gu_0,
    r_gu_1,
    r_dn_c,
    r_dn_0,
    r_dn_1,
    r_mi_c,
    r_mi_y,
    r_mi_0,
    r_mi_1,
    r_mo_c,
    r_mo_y,
    r_mo_0,
    r_mo_1,
    rows_buf,
    send,
    recv,
    load_sem,
    store_sem,
    small_send,
    small_recv,
    back_send,
    back_recv,
    free_x,
    free_y,
):
    toks, width = tokens.shape
    dkbuf = pre
    rows = mixer_in.shape[0]
    half_width = width // 2
    units = w_dn.shape[0] * w_dn.shape[1] * w_dn.shape[2] * w_dn.shape[3]
    part = units // 3
    half = toks // 2
    step = 32

    dp, fs = lax.axis_index("dp"), lax.axis_index("fsdp")
    number = dp * fsdp_count + fs
    v = lax.div(number, copies_of_place)
    rep = lax.rem(number, copies_of_place)
    c = lax.rem(v, 2)
    x = lax.rem(lax.div(v, 2), 2)
    y = lax.rem(lax.div(v, 4), 2)
    z0 = lax.rem(lax.div(v, 8), 2)
    z1 = lax.div(v, 16)
    p = 2 * y + x
    px = 2 * y + (1 - x)
    py = 2 * (1 - y) + x
    pd = 2 * (1 - y) + (1 - x)

    def dev(place):
        whole = place * copies_of_place + rep
        return (lax.div(whole, fsdp_count), lax.rem(whole, fsdp_count))

    cn = dev(v + (1 - 2 * c))
    xn = dev(v + 2 * (1 - 2 * x))
    yn = dev(v + 4 * (1 - 2 * y))
    dn = dev(v + 2 * (1 - 2 * x) + 4 * (1 - 2 * y))
    z0n = dev(v + 8 * (1 - 2 * z0))
    z1n = dev(v + 16 * (1 - 2 * z1))
    following = (dp, lax.rem(fs + 1, fsdp_count))
    preceding = (dp, lax.rem(fs + fsdp_count - 1, fsdp_count))

    counter = [0]
    started = []

    def remote(src, dst, target):
        at = counter[0]
        counter[0] += 1
        return pltpu.make_async_remote_copy(
            src_ref=src, dst_ref=dst, send_sem=send.at[at], recv_sem=recv.at[at],
            device_id=target, device_id_type=MESH,
        )

    def go(copy):
        copy.start()
        started.append(copy)
        return copy

    def same(ref, target):
        return remote(ref, ref, target)

    def sent(copy):
        copy.wait_send()
        started[:] = [other for other in started if other is not copy]

    barrier = pltpu.get_barrier_semaphore()

    def greet(m, _):
        pl.semaphore_signal(
            barrier, inc=1, device_id=dev(lax.rem(v + m, PLACES)), device_id_type=MESH
        )
        return 0

    lax.fori_loop(1, PLACES, greet, 0)
    pl.semaphore_signal(barrier, inc=1, device_id=following, device_id_type=MESH)
    pl.semaphore_signal(barrier, inc=1, device_id=preceding, device_id_type=MESH)

    load_mixer = pltpu.make_async_copy(mixer_in_hbm, mixer_in, load_sem.at[3])
    load_tokens = pltpu.make_async_copy(tokens_hbm, tokens, load_sem.at[4])
    load_gate = pltpu.make_async_copy(gate_hbm, gate, load_sem.at[5])
    load_up = pltpu.make_async_copy(up_hbm, up, load_sem.at[6])
    load_mixer.start()
    load_out = pltpu.make_async_copy(mixer_out, w_mo.at[z1, z0, y, c], load_sem.at[0])
    load_down = pltpu.make_async_copy(down, w_dn.at[z1, z0, c], load_sem.at[1])
    load_cot = pltpu.make_async_copy(cotangent, gs.at[p], load_sem.at[2])
    load_out.start()
    load_down.start()
    load_cot.start()
    load_gate.start()
    load_up.start()
    load_tokens.start()

    lane = lax.broadcasted_iota(jnp.int32, (1, 128), 1)
    mine = lax.div(lane, 32) == lax.rem(v, 4)
    small_tile[...] = jnp.zeros_like(small_tile)

    def spread(values):
        wide = jnp.concatenate([values.astype(F32)] * 4, axis=1)
        return jnp.where(mine, wide, 0.0)

    small_tile[0:1, :] = spread(gain_one[...])
    small_tile[1:2, :] = spread(gain_two[...])
    small_tile[2:5, :] = spread(taps[...])

    lanes128 = lax.broadcasted_iota(jnp.int32, (rows, 128), 1)
    low = lanes128 < 64
    load_mixer.wait()
    for b in range(3):
        for q in range(width // 256):
            at = b * width + 256 * q
            even = mixer_in[:, at : at + 128].astype(F32)
            odd = mixer_in[:, at + 128 : at + 256].astype(F32)
            to = b * half_width + 128 * q
            mi_stage[0, :, to : to + 128] = jnp.where(low, even, pltpu.roll(odd, 64, 1)).astype(BF16)
            mi_stage[1, :, to : to + 128] = jnp.where(low, pltpu.roll(even, 64, 1), odd).astype(BF16)
    w_mi[z1, z0, y, x, c] = mi_stage[x]
    small_all[v] = small_tile[...]

    pl.semaphore_wait(barrier, PLACES + 1)

    def small_copy(src, dst, m, sems=(small_send, small_recv)):
        return pltpu.make_async_remote_copy(
            src_ref=src, dst_ref=dst, send_sem=sems[0].at[m], recv_sem=sems[1].at[m],
            device_id=dev(lax.rem(v + m, PLACES)), device_id_type=MESH,
        )

    def small_start(m, _):
        small_copy(small_tile, small_all.at[v], m).start()
        return 0

    mi_swap = go(remote(mi_stage.at[1 - x], w_mi.at[z1, z0, y, x, c], xn))
    lax.fori_loop(1, PLACES, small_start, 0)
    tok_swap = go(remote(tokens_hbm, xs.at[x], xn))

    def mo_at(a, b, yy, cc):
        return w_mo.at[a, b, yy, cc]

    def mi_at(a, b, yy, cc):
        return w_mi.at[a, b, yy, :, cc]

    every = slice(None)

    def mix_gather(at):
        return dict(
            s1=same(at(z1, z0, y, c), z1n),
            s2=same(at(z1, z0, y, c), z0n),
            s3=same(at(1 - z1, z0, y, c), z0n),
            y0=same(at(z1, z0, y, c), yn),
            y1=same(at(1 - z1, z0, y, c), yn),
            y2=same(at(z1, 1 - z0, y, c), yn),
            y3=same(at(1 - z1, 1 - z0, y, c), yn),
            ca=same(at(every, every, y, c), cn),
            cb=same(at(every, every, 1 - y, c), cn),
        )

    wide = 3 * half_width

    def mi_half(h):
        columns = pl.ds(h * (wide // 2), wide // 2)
        return lambda a, b, yy, cc: w_mi.at[a, b, yy, :, cc, :, columns]

    mo_g = mix_gather(mo_at)
    mi_gs = [mix_gather(mi_half(0)), mix_gather(mi_half(1))]
    load_out.wait()
    go(mo_g["s1"])
    go(mo_g["s2"])
    mi_swap.wait_recv()
    for g in mi_gs:
        for name in ("s1", "s2", "y0"):
            go(g[name])

    offset = fs * toks
    ids = document[...].astype(F32) + 1.0
    mask_row = loss_mask[...].astype(F32)
    id_lane = lax.broadcasted_iota(jnp.int32, (step, ids.shape[1]), 1)
    id_row = lax.broadcasted_iota(jnp.int32, (step, ids.shape[1]), 0)
    ma_lane = lax.broadcasted_iota(jnp.int32, (step, toks), 1)
    ma_row = lax.broadcasted_iota(jnp.int32, (step, toks), 0)
    fl_lane = lax.broadcasted_iota(jnp.int32, (step, 128), 1)

    def flag_rows(i, _):
        base = i * step
        at = pl.ds(pl.multiple_of(base, step), step)

        def column(shift):
            hit = id_lane == id_row + (offset + base + shift)
            return jnp.sum(jnp.where(hit, ids, 0.0), axis=1, keepdims=True)

        centre = column(0)
        tile = jnp.zeros((step, 128), F32)
        for k, shift in enumerate((-1, -2, 1, 2)):
            tile = jnp.where(
                jnp.logical_and(fl_lane == k, column(shift) == centre), 1.0, tile
            )
        flags[x, at, :] = tile.astype(BF16)
        keep = jnp.sum(
            jnp.where(ma_lane == ma_row + base, mask_row, 0.0), axis=1, keepdims=True
        )
        gs[p, at, :] = (gs[p, at, :].astype(F32) * keep).astype(BF16)
        return 0

    run = units // 4

    def pick(ref, at_p):
        whole = ref[...].astype(F32)
        return jnp.concatenate(
            [whole[:, run * (4 * z + at_p) : run * (4 * z + at_p) + run] for z in range(4)], axis=1
        ).astype(BF16)

    def forward(g, arrived, names):
        g[arrived].wait_recv()
        for name in names:
            go(g[name])

    def z_gather(at):
        return dict(
            s1=same(at(z1, z0, c), z1n),
            s2=same(at(z1, z0, c), z0n),
            s3=same(at(1 - z1, z0, c), z0n),
            core=same(at(every, every, c), cn),
        )

    dn_g = z_gather(lambda a, b, cc: w_dn.at[a, b, cc])
    gu_g = [z_gather(lambda a, b, cc, j=j: w_gu.at[j, a, b, :, cc]) for j in range(3)]

    def z_start(g):
        go(g["s1"])
        go(g["s2"])

    def z_forward(g):
        forward(g, "s1", ("s3",))

    def z_core(g):
        g["s2"].wait_recv()
        g["s3"].wait_recv()
        go(g["core"])

    def plane_gather(buf, halves):
        lo, hi = pl.ds(0, half), pl.ds(half, half)
        return dict(
            x0=same(buf.at[p, lo], xn),
            y1=same(buf.at[p, hi], yn),
            x1=same(buf.at[p, hi], xn),
            y0=same(buf.at[p, lo], yn),
            fx=same(buf.at[px, lo] if halves else buf.at[px], yn),
            **(dict(fy=same(buf.at[py, hi], xn)) if halves else {}),
        )

    def plane_forward(g):
        forward(g, "x0", ("fx",))
        forward(g, "y1", ("fy",))

    gs_g, hs_g = plane_gather(gs, False), plane_gather(hs, True)

    load_cot.wait()
    lax.fori_loop(0, toks // step, flag_rows, 0)
    flag_swap = go(same(flags.at[x], xn))
    load_gate.wait()
    load_up.wait()
    for at_p in range(4):
        picked_gate, picked_up = pick(gate, at_p), pick(up, at_p)
        for j in range(3):
            gu_stage[at_p, j, :, 0:part] = picked_gate[:, j * part : j * part + part]
            gu_stage[at_p, j, :, part:] = picked_up[:, j * part : j * part + part]
    load_tokens.wait()
    xs[x] = tokens[...]
    for j in range(3):
        w_gu[j, z1, z0, p, c] = gu_stage[p, j]

    go(mo_g["y0"])
    forward(mo_g, "s1", ("s3", "y1"))
    forward(mo_g, "s2", ("y2",))
    for g in mi_gs:
        forward(g, "s1", ("s3", "y1"))
        forward(g, "s2", ("y2",))
    gu_swap = [
        remote(gu_stage.at[px], w_gu.at[:, z1, z0, p, c], xn),
        remote(gu_stage.at[py], w_gu.at[:, z1, z0, p, c], yn),
        remote(gu_stage.at[pd], w_gu.at[:, z1, z0, p, c], dn),
    ]
    go(gu_swap[2])
    go(gu_swap[0])
    go(gs_g["x0"])
    go(gs_g["x1"])

    def small_wait(m, _):
        copy = small_copy(small_tile, small_all.at[v], m)
        copy.wait()
        return 0

    lax.fori_loop(1, PLACES, small_wait, 0)
    natural = []
    for q in range(8):
        natural.append(
            small_all[4 * q] + small_all[4 * q + 1] + small_all[4 * q + 2] + small_all[4 * q + 3]
        )
    for q in range(8):
        rows_buf[:, 128 * q : 128 * q + 128] = natural[q]
    low8 = lax.broadcasted_iota(jnp.int32, (8, 128), 1) < 64
    is_one = x == 1
    for q in range(4):
        even, odd = natural[2 * q], natural[2 * q + 1]
        first = jnp.where(low8, even, pltpu.roll(odd, 64, 1))
        second = jnp.where(low8, pltpu.roll(even, 64, 1), odd)
        rows_buf[:, width + 128 * q : width + 128 * q + 128] = jnp.where(is_one, second, first)
    g1 = rows_buf[0:1, 0:width]
    g2 = rows_buf[1:2, 0:width]
    tap0 = rows_buf[2:3, width : width + half_width]
    tap1 = rows_buf[3:4, width : width + half_width]
    tap2 = rows_buf[4:5, width : width + half_width]

    def inverse_rms(values):
        return lax.rsqrt(jnp.mean(values * values, axis=1, keepdims=True) + EPSILON)

    def loop(count, body):
        def wrapped(i, _):
            body(pl.ds(pl.multiple_of(i * step, step), step))
            return 0

        lax.fori_loop(0, count // step, wrapped, 0)

    def hidden_one(s):
        def body(at):
            values = xs[s, at, :].astype(F32)
            xs[s, at, :] = (values * inverse_rms(values) * g1).astype(BF16)

        loop(toks, body)

    for g in mi_gs:
        forward(g, "s3", ("y3",))
        go(g["ca"])
    forward(mo_g, "s3", ("y3",))
    go(mo_g["ca"])
    go(gu_swap[1])
    load_down.wait()
    z_start(dn_g)
    hidden_one(x)
    tok_swap.wait_recv()
    hidden_one(1 - x)
    for g in mi_gs:
        for name in ("y0", "y1", "y2", "y3"):
            g[name].wait_recv()
        go(g["cb"])
    go(gs_g["y1"])
    go(gs_g["y0"])
    for g in mi_gs:
        g["ca"].wait_recv()
        g["cb"].wait_recv()
    h1 = xs[...].reshape(2 * toks, width)
    proj[...] = nn(h1, w_mi[...].reshape(width, wide)).reshape(2, toks, wide)

    for s in range(2):
        def body(at, s=s):
            ubuf[s, pl.ds(pl.multiple_of(at.start + 8, 8), step), :] = (
                proj[s, at, 0:half_width] * proj[s, at, 2 * half_width :]
            )

        loop(toks, body)
    halo = go(remote(ubuf.at[:, pl.ds(toks, 8), :], ubuf.at[:, pl.ds(0, 8), :], following))
    z_forward(dn_g)
    for copy in gu_swap:
        copy.wait_recv()
    z_start(gu_g[0])
    z_start(gu_g[1])
    for name in ("y0", "y1", "y2", "y3"):
        mo_g[name].wait_recv()
    go(mo_g["cb"])
    flag_swap.wait_recv()
    halo.wait_recv()
    for s in range(2):
        for i in range(toks // step):
            a = i * step
            fl = flags[s, a : a + step, :].astype(F32)
            value = (
                tap2 * ubuf[s, a + 8 : a + 8 + step, :]
                + tap1 * (fl[:, 0:1] * ubuf[s, a + 7 : a + 7 + step, :])
                + tap0 * (fl[:, 1:2] * ubuf[s, a + 6 : a + 6 + step, :])
            )
            conv[s, a : a + step, :] = value
            ys[s, a : a + step, :] = (
                proj[s, a : a + step, half_width : 2 * half_width] * value
            ).astype(BF16)
    mo_g["ca"].wait_recv()
    mo_g["cb"].wait_recv()
    mo_flat = w_mo[...].reshape(half_width, width)
    o_send[...] = nn(ys[1 - x], mo_flat).astype(BF16)
    o_swap = go(remote(o_send, o_recv, xn))
    x2[...] = nn(ys[x], mo_flat)

    forward(gs_g, "x0", ())
    forward(gs_g, "x1", ("fx",))
    z_core(dn_g)
    for copy in gu_swap:
        sent(copy)
    sent(mi_swap)

    def second_body(at):
        values = tokens[at, :].astype(F32) + x2[at, :] + o_recv[at, :].astype(F32)
        x2[at, :] = values
        hs[p, at, :] = (values * inverse_rms(values) * g2).astype(BF16)

    o_swap.wait_recv()
    loop(toks, second_body)
    for name in ("x0", "y1", "x1", "y0"):
        go(hs_g[name])
    z_forward(gu_g[0])
    z_forward(gu_g[1])
    z_start(gu_g[2])
    plane_forward(hs_g)
    z_core(gu_g[0])

    ya, yb = 2 * y, 2 * (1 - y)

    def plane_pair(g, names):
        for name in names:
            g[name].wait_recv()

    def pair_rows(ref, base):
        return ref[pl.ds(base, 2)].reshape(2 * toks, width)

    def feed(j, base):
        w = w_gu[j].reshape(width, 2 * part)
        pre[:, 0:toks, :] = nn(pair_rows(hs, base), w).reshape(2, toks, 2 * part)
        down_rows = w_dn[...].reshape(units, width)[j * part : j * part + part]
        dm_buf[...] = nt(pair_rows(gs, base), down_rows)

        def body(i, _):
            at = pl.ds(pl.multiple_of(i * step, step), step)
            slot = base + lax.div(i, toks // step)
            inner = pl.ds(pl.multiple_of(lax.rem(i, toks // step) * step, step), step)
            which = lax.div(i, toks // step)
            a = pre[which, inner, 0:part]
            b = pre[which, inner, part:]
            d = dm_buf[at, :]
            sg = jax.nn.sigmoid(a)
            silu = a * sg
            ms[slot, inner, j * part : j * part + part] = (silu * b).astype(BF16)
            chunk = lax.rem(i, toks // step)
            at = (lax.div(chunk, 4), lax.rem(lax.div(chunk, 2), 2), lax.rem(chunk, 2))
            dabs[(j, lax.div(base, 2), which, *at, every, slice(0, part))] = (
                d * b * sg * (1.0 + a * (1.0 - sg))
            ).astype(BF16)
            dabs[(j, lax.div(base, 2), which, *at, every, slice(part, 2 * part))] = (
                d * silu
            ).astype(BF16)
            return 0

        lax.fori_loop(0, 2 * toks // step, body, 0)
        back = nt(dabs[j, lax.div(base, 2)].reshape(2 * toks, 2 * part), w)
        back = back.reshape(2, toks, width)
        if j == 0:
            acc[pl.ds(base, 2)] = back
        elif j == 1:
            acc[pl.ds(base, 2)] += back
        else:
            total = acc[pl.ds(base, 2)] + back
            acc[pl.ds(base, 2)] = total
            dhp[pl.ds(base, 2)] = total.astype(BF16)

    def gu_weight_grad(j):
        w_gu[j] = (
            tn(hs[...].reshape(4 * toks, width), dabs[j].reshape(4 * toks, 2 * part))
            .astype(BF16)
            .reshape(w_gu.shape[1:])
        )

    def plane_scatter(buf, r_a, r_b, r_x, r_y):
        lo, hi = pl.ds(0, half), pl.ds(half, half)
        return dict(
            a=remote(buf.at[pd, lo], r_a, xn),
            b=remote(buf.at[pd, hi], r_b, yn),
            x0=remote(buf.at[px, lo], r_x.at[lo], xn),
            y1=remote(buf.at[py, hi], r_y.at[hi], yn),
            x1=remote(buf.at[px, hi], r_x.at[hi], xn),
            y0=remote(buf.at[py, lo], r_y.at[lo], yn),
        )

    def add_rows(buf, slot, start, other):
        def body(at):
            into = pl.ds(pl.multiple_of(at.start + start, step), step)
            buf[slot, into, :] = (
                buf[slot, into, :].astype(F32) + other[at, :].astype(F32)
            ).astype(BF16)

        loop(half, body)

    def scatter_rest(g, buf, r_a, r_b):
        g["b"].wait_recv()
        add_rows(buf, px, half, r_b)
        go(g["x1"])
        g["a"].wait_recv()
        add_rows(buf, py, 0, r_a)
        go(g["y0"])

    def z_reduce(at, r_c, r_0, r_1):
        return dict(
            core=remote(at(every, every, 1 - c), r_c, cn),
            z0=remote(at(every, 1 - z0, c), r_0, z0n),
            z1=remote(at(1 - z1, z0, c), r_1, z1n),
        )

    gu_r = [
        z_reduce(lambda a, b, cc, j=j: w_gu.at[j, a, b, :, cc], r_gu_c.at[j % 2], r_gu_0.at[j], r_gu_1.at[j])
        for j in range(3)
    ]
    dn_r = z_reduce(lambda a, b, cc: w_dn.at[a, b, cc], r_dn_c, r_dn_0, r_dn_1)

    def plus(one, two):
        return (one.astype(F32) + two.astype(F32)).astype(BF16)

    def gu_after_core(j):
        gu_r[j]["core"].wait_recv()
        for a in range(2):
            for b in range(2):
                w_gu[j, a, b, :, c] = plus(w_gu[j, a, b, :, c], r_gu_c[j % 2, a, b])
        go(gu_r[j]["z0"])

    def gu_after_z0(j):
        gu_r[j]["z0"].wait_recv()
        for a in range(2):
            w_gu[j, a, z0, :, c] = plus(w_gu[j, a, z0, :, c], r_gu_0[j, a])
        go(gu_r[j]["z1"])

    gu_back = []

    def gu_sum_z1(j):
        gu_r[j]["z1"].wait_recv()
        w_gu[j, z1, z0, :, c] = plus(w_gu[j, z1, z0, :, c], r_gu_1[j])
        gu_stage[p, j] = w_gu[j, z1, z0, p, c]

    def gu_return(j):
        for place, target in ((px, xn), (py, yn), (pd, dn)):
            gu_back.append(go(remote(w_gu.at[j, z1, z0, place, c], gu_stage.at[p, j], target)))

    def gathered(g):
        for name in ("s1", "s2", "s3", "core"):
            sent(g[name])

    dn_g["core"].wait_recv()
    plane_pair(hs_g, ("x1",))
    gu_g[0]["core"].wait_recv()
    feed(0, ya)
    z_core(gu_g[1])
    plane_pair(gs_g, ("y0", "y1", "fx"))
    plane_pair(hs_g, ("y0", "fx", "fy"))
    feed(0, yb)
    z_forward(gu_g[2])
    gathered(gu_g[0])
    gu_weight_grad(0)
    go(gu_r[0]["core"])
    gu_after_core(0)
    gu_g[1]["core"].wait_recv()
    feed(1, yb)
    z_core(gu_g[2])
    feed(1, ya)
    gu_g[2]["core"].wait_recv()
    feed(2, yb)
    dh_g = plane_scatter(dhp, dh_a, dh_b, dh_x, dh_y)
    go(dh_g["a"])
    go(dh_g["b"])
    go(dh_g["y1"])
    gu_after_z0(0)
    feed(2, ya)
    go(dh_g["x0"])
    gathered(gu_g[1])
    gu_weight_grad(1)
    go(gu_r[1]["core"])
    gathered(gu_g[2])
    gu_weight_grad(2)
    gu_after_core(1)
    go(gu_r[2]["core"])
    scatter_rest(dh_g, dhp, dh_a, dh_b)

    for name in ("x0", "x1", "y0", "y1", "fx", "fy"):
        sent(hs_g[name])
    dn_flat = w_dn[...].reshape(units, width)
    for base in (ya, yb):
        m = ms[pl.ds(base, 2)].reshape(2 * toks, units)
        hs[pl.ds(base, 2)] = nn(m, dn_flat).astype(BF16).reshape(2, toks, width)
    gu_after_core(2)
    gathered(dn_g)
    w_dn[...] = (
        tn(ms[...].reshape(4 * toks, units), gs[...].reshape(4 * toks, width))
        .astype(BF16)
        .reshape(w_dn.shape)
    )
    go(dn_r["core"])
    dn_r["core"].wait_recv()
    for a in range(2):
        for b in range(2):
            w_dn[a, b, c] = plus(w_dn[a, b, c], r_dn_c[a, b])
    go(dn_r["z0"])

    for name in ("x0", "x1", "y0", "y1"):
        dh_g[name].wait_recv()
    small_grad[...] = jnp.zeros_like(small_grad)

    def norm_two(at):
        dh = acc[p, at, :] + dh_x[at, :].astype(F32) + dh_y[at, :].astype(F32)
        values = x2[at, :]
        inverse = inverse_rms(values)
        normed = values * inverse
        small_grad[1:2, :] += jnp.sum(dh * normed, axis=0, keepdims=True)
        q = dh * g2
        grad = gs[p, at, :].astype(F32) + inverse * (
            q - normed * jnp.mean(q * normed, axis=1, keepdims=True)
        )
        input_grad[at, :] = grad
        dos[x, at, :] = grad.astype(BF16)

    loop(toks, norm_two)
    do_swap = go(same(dos.at[x], xn))
    lo, hi = pl.ds(0, half), pl.ds(half, half)
    ou_g = plane_scatter(hs, dhp.at[py, lo], dhp.at[px, hi], dhp.at[p], dhp.at[p])
    for copy in dh_g.values():
        sent(copy)
    pl.semaphore_signal(free_x, inc=1, device_id=xn, device_id_type=MESH)
    pl.semaphore_signal(free_y, inc=1, device_id=yn, device_id_type=MESH)
    pl.semaphore_wait(free_x, 1)
    pl.semaphore_wait(free_y, 1)
    for name in ("b", "y1", "a"):
        go(ou_g[name])

    mo_flat = w_mo[...].reshape(half_width, width)

    def split_dy(s):
        def body(at):
            dy = dkbuf[s, at, 0:half_width]
            dps[s, at, half_width : 2 * half_width] = (dy * conv[s, at, :]).astype(BF16)
            dkbuf[s, at, 0:half_width] = dy * proj[s, at, half_width : 2 * half_width]

        loop(toks, body)

    dkbuf[x, 0:toks, 0:half_width] = nt(dos[x], mo_flat)
    split_dy(x)
    gu_after_z0(1)
    gu_sum_z1(0)
    gu_return(0)
    gu_after_z0(2)
    do_swap.wait_recv()
    dkbuf[1 - x, 0:toks, 0:half_width] = nt(dos[1 - x], mo_flat)
    split_dy(1 - x)
    dk_halo = go(
        remote(
            dkbuf.at[:, pl.ds(0, 8), pl.ds(0, half_width)],
            dkbuf.at[:, pl.ds(toks, 8), pl.ds(0, half_width)],
            preceding,
        )
    )
    for g in (mo_g, *mi_gs):
        for copy in g.values():
            sent(copy)
    w_mo[...] = (
        tn(ys[...].reshape(2 * toks, half_width), dos[...].reshape(2 * toks, width))
        .astype(BF16)
        .reshape(w_mo.shape)
    )

    def mix_reduce(at, r_c, r_y, r_0, r_1):
        return dict(
            ca=remote(at(every, every, 1 - y, 1 - c), r_c.at[:, :, 1 - y], cn),
            cb=remote(at(every, every, y, 1 - c), r_c.at[:, :, y], cn),
            y3=remote(at(1 - z1, 1 - z0, 1 - y, c), r_y.at[1 - z1, 1 - z0], yn),
            y2=remote(at(z1, 1 - z0, 1 - y, c), r_y.at[z1, 1 - z0], yn),
            y1=remote(at(1 - z1, z0, 1 - y, c), r_y.at[1 - z1, z0], yn),
            y0=remote(at(z1, z0, 1 - y, c), r_y.at[z1, z0], yn),
            s3=remote(at(1 - z1, 1 - z0, y, c), r_0.at[1 - z1], z0n),
            s2=remote(at(z1, 1 - z0, y, c), r_0.at[z1], z0n),
            s1=remote(at(1 - z1, z0, y, c), r_1, z1n),
        )

    mo_r = mix_reduce(mo_at, r_mo_c, r_mo_y, r_mo_0, r_mo_1)
    mi_rs = [
        mix_reduce(
            lambda a, b, yy, cc, h=h: dabs.at[h, a, b, yy, :, cc],
            r_mi_c.at[h], r_mi_y.at[h], r_mi_0.at[h], r_mi_1.at[h],
        )
        for h in range(2)
    ]
    go(mo_r["ca"])
    go(mo_r["cb"])
    def mix_core(w, r_c, g, with_x):
        def add(yy):
            for a in range(2):
                for b in range(2):
                    if with_x:
                        w[a, b, yy, :, c] = plus(w[a, b, yy, :, c], r_c[a, b, yy])
                    else:
                        w[a, b, yy, c] = plus(w[a, b, yy, c], r_c[a, b, yy])

        g["ca"].wait_recv()
        add(1 - y)
        for name in ("y3", "y1", "y2", "y0"):
            go(g[name])
        g["cb"].wait_recv()
        add(y)

    dk_halo.wait_recv()
    ek = [jnp.zeros((1, half_width), F32) for _ in range(3)]
    for s in range(2):
        for i in range(toks // step):
            a = i * step
            fl = flags[s, a : a + step, :].astype(F32)
            dk = dkbuf[s, a : a + step, 0:half_width]
            ek[2] += jnp.sum(dk * ubuf[s, a + 8 : a + 8 + step, :], axis=0, keepdims=True)
            ek[1] += jnp.sum(
                dk * (fl[:, 0:1] * ubuf[s, a + 7 : a + 7 + step, :]), axis=0, keepdims=True
            )
            ek[0] += jnp.sum(
                dk * (fl[:, 1:2] * ubuf[s, a + 6 : a + 6 + step, :]), axis=0, keepdims=True
            )
            du = (
                tap2 * dk
                + tap1 * (fl[:, 2:3] * dkbuf[s, a + 1 : a + 1 + step, 0:half_width])
                + tap0 * (fl[:, 3:4] * dkbuf[s, a + 2 : a + 2 + step, 0:half_width])
            )
            dps[s, a : a + step, 0:half_width] = (
                du * proj[s, a : a + step, 2 * half_width :]
            ).astype(BF16)
            dps[s, a : a + step, 2 * half_width :] = (
                du * proj[s, a : a + step, 0:half_width]
            ).astype(BF16)
    for k in range(3):
        for q in range(4):
            chunk = jnp.broadcast_to(ek[k][:, 128 * q : 128 * q + 128], (8, 128))
            turned = pltpu.roll(chunk, 64, 1)
            even = jnp.where(is_one, jnp.where(low8, 0.0, turned), jnp.where(low8, chunk, 0.0))
            odd = jnp.where(is_one, jnp.where(low8, 0.0, chunk), jnp.where(low8, turned, 0.0))
            small_grad[2 + k : 3 + k, 256 * q : 256 * q + 128] = even[0:1]
            small_grad[2 + k : 3 + k, 256 * q + 128 : 256 * q + 256] = odd[0:1]

    for q in range(8):
        small_in[PLACES + q] = small_grad[:, 128 * q : 128 * q + 128]

    def small_back(m):
        target = lax.rem(v + m, PLACES)
        source = small_in.at[PLACES + lax.div(target, 4)]
        return small_copy(source, small_in.at[v], m, (back_send, back_recv))

    def small_back_start(m, _):
        small_back(m).start()
        return 0

    lax.fori_loop(1, PLACES, small_back_start, 0)
    small_in[v] = small_in[PLACES + lax.div(v, 4)]

    mix_core(w_mo, r_mo_c, mo_r, False)
    columns = 2 * part
    for h in range(2):
        dabs[h] = (
            tn(
                xs[...].reshape(2 * toks, width),
                dps[:, :, h * columns : (h + 1) * columns].reshape(2 * toks, columns),
            )
            .astype(BF16)
            .reshape(dabs.shape[1:])
        )
        go(mi_rs[h]["ca"])
        go(mi_rs[h]["cb"])
    mi_flat = w_mi[...].reshape(width, wide)
    sent(o_swap)
    o_send[...] = nt(dps[1 - x], mi_flat).astype(BF16)
    dh1_swap = go(remote(o_send, o_recv, xn))
    mix_core(dabs.at[0], r_mi_c.at[0], mi_rs[0], True)
    mix_core(dabs.at[1], r_mi_c.at[1], mi_rs[1], True)
    dn_r["z0"].wait_recv()
    for a in range(2):
        w_dn[a, z0, c] = plus(w_dn[a, z0, c], r_dn_0[a])
    go(dn_r["z1"])
    ou_g["a"].wait_recv()
    add_rows(hs, py, 0, dhp.at[pd, lo])
    go(ou_g["y0"])
    ou_g["b"].wait_recv()
    add_rows(hs, px, half, dhp.at[pd, hi])
    go(ou_g["x0"])
    go(ou_g["x1"])
    acc[p] = nt(dps[x], mi_flat)

    def mo_idx(a, b):
        return (a, b, y, c)

    def mi_idx(a, b):
        return (a, b, y, every, c)

    mo_parts = (w_mo, mo_idx, mo_r, r_mo_y, r_mo_0)
    mi_parts = [
        (dabs.at[h], mi_idx, mi_rs[h], r_mi_y.at[h], r_mi_0.at[h]) for h in range(2)
    ]

    def mix_three(w, idx, g, r_y, r_0):
        g["y3"].wait_recv()
        at = idx(1 - z1, 1 - z0)
        w[at] = plus(w[at], r_y[1 - z1, 1 - z0])
        go(g["s3"])

    def mix_one(w, idx, g, r_y, r_0):
        g["y1"].wait_recv()
        g["s3"].wait_recv()
        at = idx(1 - z1, z0)
        w[at] = plus(plus(w[at], r_y[1 - z1, z0]), r_0[1 - z1])
        go(g["s1"])

    def mix_two(w, idx, g, r_y, r_0):
        g["y2"].wait_recv()
        at = idx(z1, 1 - z0)
        w[at] = plus(w[at], r_y[z1, 1 - z0])
        go(g["s2"])

    def mix_last(w, idx, g, r_y, r_0):
        g["y0"].wait_recv()
        g["s2"].wait_recv()
        at = idx(z1, z0)
        w[at] = plus(plus(w[at], r_y[z1, z0]), r_0[z1])

    mix_three(*mo_parts)
    mix_three(*mi_parts[0])
    mix_three(*mi_parts[1])
    dh1_swap.wait_recv()

    def norm_one(at):
        dh = acc[p, at, :] + o_recv[at, :].astype(F32)
        values = tokens[at, :].astype(F32)
        inverse = inverse_rms(values)
        normed = values * inverse
        q = dh * g1
        input_grad[at, :] = input_grad[at, :] + inverse * (
            q - normed * jnp.mean(q * normed, axis=1, keepdims=True)
        )

    loop(toks, norm_one)

    stores = []

    def store(src, dst):
        copy = pltpu.make_async_copy(src, dst, store_sem.at[len(stores)])
        copy.start()
        stores.append(copy)

    store(input_grad, input_sum)
    gu_sum_z1(1)
    gu_return(1)

    mix_one(*mo_parts)
    mix_two(*mo_parts)
    mix_one(*mi_parts[0])
    mix_two(*mi_parts[0])
    mix_one(*mi_parts[1])
    mix_two(*mi_parts[1])
    gu_sum_z1(2)
    gu_return(2)
    for name in ("x0", "x1", "y0", "y1"):
        ou_g[name].wait_recv()

    def out_body(at):
        o_send[at, :] = (
            x2[at, :]
            + hs[p, at, :].astype(F32)
            + dhp[px, at, :].astype(F32)
            + dhp[py, at, :].astype(F32)
        ).astype(BF16)

    sent(dh1_swap)
    loop(toks, out_body)

    store(o_send, block_out)
    down_rows = w_dn.shape[3]
    def small_back_wait(m, _):
        small_back(m).wait()
        return 0

    lax.fori_loop(1, PLACES, small_back_wait, 0)
    total = small_in[0]
    for q in range(1, PLACES):
        total = total + small_in[q]
    total = total * factor
    small_out[...] = total

    mix_last(*mo_parts)
    dn_r["z1"].wait_recv()
    acc[3, 0:down_rows] = (w_dn[z1, z0, c].astype(F32) + r_dn_1[...].astype(F32)) * factor
    store(acc.at[3, pl.ds(0, down_rows)], dn_sum)
    mo_r["s1"].wait_recv()
    acc[2, 96 : 96 + rows] = (w_mo[z1, z0, y, c].astype(F32) + r_mo_1[...].astype(F32)) * factor
    store(acc.at[2, pl.ds(96, rows)], mo_sum)
    for copy in gu_back:
        copy.wait_recv()
    store(gu_stage, gu_sum)
    mi_back = []
    for h in range(2):
        mix_last(*mi_parts[h])
        mi_rs[h]["s1"].wait_recv()
        dabs[h, z1, z0, y, :, c] = plus(dabs[h, z1, z0, y, :, c], r_mi_1[h])
        into = pl.ds(h * columns, columns)
        mi_stage[x, :, into] = dabs[h, z1, z0, y, x, c]
        mi_back.append(go(remote(dabs.at[h, z1, z0, y, 1 - x, c], mi_stage.at[x, :, into], xn)))
    for copy in mi_back:
        copy.wait_recv()
    store(mi_stage, mi_sum)

    for copy in stores:
        copy.wait()
    for copy in list(started):
        sent(copy)


COPIES = 160


def finish(
    fsdp_count,
    copies_of_place,
    factor,
    block_sum,
    input_sum,
    small,
    mi_sum,
    mo_sum,
    gu_sum,
    dn_sum,
    mixer_in,
    gain_one,
    block_out,
    input_grad,
    gain_one_grad,
    mixer_in_grad,
    taps_grad,
    mixer_out_grad,
    gain_two_grad,
    gate_grad,
    up_grad,
    down_grad,
):
    input_grad[...] = input_sum[...]
    block_out[...] = block_sum[...]
    down_grad[...] = dn_sum[...]
    mixer_out_grad[...] = mo_sum[...]
    rows, ff = gate_grad.shape
    width = mixer_out_grad.shape[1]
    part, run, half_width = ff // 12, ff // 16, width // 2
    for ref, start in ((gate_grad, 0), (up_grad, part)):
        pieces = [
            jnp.concatenate(
                [gu_sum[at_p, j, :, start : start + part] for j in range(3)], axis=1
            ).astype(F32)
            * factor
            for at_p in range(4)
        ]
        ref[...] = jnp.concatenate(
            [pieces[q % 4][:, run * (q // 4) : run * (q // 4) + run] for q in range(16)], axis=1
        )
    low = lax.broadcasted_iota(jnp.int32, (rows, 128), 1) < 64
    by_row = jnp.zeros((rows, 128), F32)
    for b in range(3):
        for q in range(width // 256):
            at = b * half_width + 128 * q
            first = mi_sum[0, :, at : at + 128].astype(F32) * factor
            second = mi_sum[1, :, at : at + 128].astype(F32) * factor
            to = b * width + 256 * q
            even = jnp.where(low, first, pltpu.roll(second, 64, 1))
            odd = jnp.where(low, pltpu.roll(first, 64, 1), second)
            mixer_in_grad[:, to : to + 128] = even
            mixer_in_grad[:, to + 128 : to + 256] = odd
            by_row += even * mixer_in[:, to : to + 128].astype(F32)
            by_row += odd * mixer_in[:, to + 128 : to + 256].astype(F32)
    column = jnp.sum(by_row, axis=1, keepdims=True)
    every_row = gain_one.shape[1]
    step = pl.program_id(0)
    row_at = lax.broadcasted_iota(jnp.int32, (rows, every_row), 0) + step * rows
    col_at = lax.broadcasted_iota(jnp.int32, (rows, every_row), 1)
    turned = jnp.sum(jnp.where(row_at == col_at, column, 0.0), axis=0, keepdims=True)
    turned = turned / gain_one[...].astype(F32)
    number = lax.axis_index("dp") * fsdp_count + lax.axis_index("fsdp")
    quarter = lax.rem(lax.div(number, copies_of_place), 4)
    values = small[...]
    own = values[:, 0:every_row]
    for k in range(1, 4):
        own = jnp.where(quarter == k, values[:, k * every_row : (k + 1) * every_row], own)

    @pl.when(step == 0)
    def first_step():
        gain_one_grad[...] = turned

    @pl.when(step > 0)
    def later_step():
        gain_one_grad[...] += turned

    gain_two_grad[...] = own[1:2]
    taps_grad[...] = own[2:5]


def per_device(
    fsdp_count,
    device_count,
    tokens,
    document_index,
    loss_token_mask,
    cotangent,
    first_gain,
    mixer_in,
    conv_kernel,
    mixer_out,
    second_gain,
    gate_weight,
    up_weight,
    down_weight,
):
    row_count, seq_here, width = tokens.shape
    toks = row_count * seq_here
    spare = device_count // PLACES
    groups = [[place * spare + k for k in range(spare)] for place in range(PLACES)]
    axes = ("dp", "fsdp")

    def joined(shard, axis=0):
        if spare == 1:
            return shard
        return lax.all_gather(shard, axes, axis=axis, tiled=True, axis_index_groups=groups)

    first_gain, second_gain = joined(first_gain), joined(second_gain)
    conv_kernel = joined(conv_kernel, 1)
    mixer_in, mixer_out = joined(mixer_in), joined(mixer_out)
    gate_weight, up_weight, down_weight = joined(gate_weight), joined(up_weight), joined(down_weight)
    rows = mixer_in.shape[0]
    down_rows = down_weight.shape[0]
    ff = gate_weight.shape[1]
    part = ff // 12
    half_width = width // 2
    wide = 3 * half_width
    factor = 1.0 / math.sqrt(toks * device_count)

    def vm(shape, dtype=BF16):
        return pltpu.VMEM(shape, dtype)

    half = toks // 2
    scratch = [
        vm((toks, width), F32),
        vm((toks, width)),
        vm((rows, 3 * width)),
        vm((rows, ff)),
        vm((rows, ff)),
        vm((8, 128), F32),
        vm((PLACES, 8, 128), F32),
        vm((8, width), F32),
        vm((PLACES + 8, 8, 128), F32),
        vm((2, 2, 2, 2, 2, rows, wide)),
        vm((2, 2, 2, 2, rows, width)),
        vm((3, 2, 2, 4, 2, rows, 2 * part)),
        vm((2, 2, 2, down_rows, width)),
        vm((2, rows, wide)),
        vm((4, 3, rows, 2 * part)),
        vm((2, toks, width)),
        vm((2, toks, 128)),
        vm((4, toks, width)),
        vm((4, toks, width)),
        vm((2, toks, wide), F32),
        vm((2, toks + 8, half_width), F32),
        vm((2, toks, half_width), F32),
        vm((2, toks, half_width)),
        vm((2, toks, wide)),
        vm((toks, width), F32),
        vm((toks, width)),
        vm((toks, width)),
        vm((2, toks + 8, 2 * part), F32),
        vm((2 * toks, part), F32),
        vm((4, toks, 3 * part)),
        vm((3, 2, 2, 2, 2, 2, rows, 2 * part)),
        vm((4, toks, width), F32),
        vm((4, toks, width)),
        vm((half, width)),
        vm((half, width)),
        vm((toks, width)),
        vm((toks, width)),
        vm((2, toks, width)),
        vm((2, 2, 2, 4, rows, 2 * part)),
        vm((3, 2, 4, rows, 2 * part)),
        vm((3, 4, rows, 2 * part)),
        vm((2, 2, down_rows, width)),
        vm((2, down_rows, width)),
        vm((down_rows, width)),
        vm((2, 2, 2, 2, 2, rows, 2 * part)),
        vm((2, 2, 2, 2, rows, 2 * part)),
        vm((2, 2, 2, rows, 2 * part)),
        vm((2, 2, rows, 2 * part)),
        vm((2, 2, 2, rows, width)),
        vm((2, 2, rows, width)),
        vm((2, rows, width)),
        vm((rows, width)),
        vm((8, width + half_width), F32),
        pltpu.SemaphoreType.DMA((COPIES,)),
        pltpu.SemaphoreType.DMA((COPIES,)),
        pltpu.SemaphoreType.DMA((7,)),
        pltpu.SemaphoreType.DMA((20,)),
        pltpu.SemaphoreType.DMA((PLACES,)),
        pltpu.SemaphoreType.DMA((PLACES,)),
        pltpu.SemaphoreType.DMA((PLACES,)),
        pltpu.SemaphoreType.DMA((PLACES,)),
        pltpu.SemaphoreType.REGULAR,
        pltpu.SemaphoreType.REGULAR,
    ]
    outs = [
        jax.ShapeDtypeStruct((toks, width), BF16),
        jax.ShapeDtypeStruct((toks, width), F32),
        jax.ShapeDtypeStruct((8, 128), F32),
        jax.ShapeDtypeStruct((2, rows, wide), BF16),
        jax.ShapeDtypeStruct((rows, width), F32),
        jax.ShapeDtypeStruct((4, 3, rows, 2 * part), BF16),
        jax.ShapeDtypeStruct((down_rows, width), F32),
    ]
    vmem = pl.BlockSpec(memory_space=pltpu.VMEM)
    hbm = pl.BlockSpec(memory_space=pl.ANY)
    result = pl.pallas_call(
        functools.partial(kernel, fsdp_count, spare, factor),
        out_shape=outs,
        in_specs=[hbm] * 2 + [vmem] * 5 + [hbm] * 5,
        out_specs=[hbm] * 2 + [vmem] + [hbm] * 4,
        scratch_shapes=scratch,
        compiler_params=pltpu.CompilerParams(
            collective_id=0, has_side_effects=True, vmem_limit_bytes=60 << 20
        ),
    )(
        tokens.reshape(toks, width),
        cotangent.reshape(toks, width),
        document_index,
        loss_token_mask,
        first_gain.reshape(1, rows),
        second_gain.reshape(1, rows),
        conv_kernel,
        mixer_in,
        mixer_out,
        gate_weight,
        up_weight,
        down_weight,
    )
    def halved(count, columns):
        return pl.BlockSpec((count // 2, columns), lambda i: (i, 0))

    def whole(count, columns):
        return pl.BlockSpec((count, columns), lambda i: (0, 0))

    finished = pl.pallas_call(
        functools.partial(finish, fsdp_count, spare, factor),
        out_shape=[
            jax.ShapeDtypeStruct((toks, width), BF16),
            jax.ShapeDtypeStruct((toks, width), F32),
            jax.ShapeDtypeStruct((1, rows), F32),
            jax.ShapeDtypeStruct((rows, 3 * width), F32),
            jax.ShapeDtypeStruct((3, rows), F32),
            jax.ShapeDtypeStruct((rows, width), F32),
            jax.ShapeDtypeStruct((1, rows), F32),
            jax.ShapeDtypeStruct((rows, ff), F32),
            jax.ShapeDtypeStruct((rows, ff), F32),
            jax.ShapeDtypeStruct((down_rows, width), F32),
        ],
        grid=(2,),
        in_specs=[
            halved(toks, width),
            halved(toks, width),
            whole(8, 128),
            pl.BlockSpec((2, rows // 2, wide), lambda i: (0, i, 0)),
            halved(rows, width),
            pl.BlockSpec((4, 3, rows // 2, 2 * part), lambda i: (0, 0, i, 0)),
            halved(down_rows, width),
            halved(rows, 3 * width),
            whole(1, rows),
        ],
        out_specs=[
            halved(toks, width),
            halved(toks, width),
            whole(1, rows),
            halved(rows, 3 * width),
            whole(3, rows),
            halved(rows, width),
            whole(1, rows),
            halved(rows, ff),
            halved(rows, ff),
            halved(down_rows, width),
        ],
        compiler_params=pltpu.CompilerParams(vmem_limit_bytes=60 << 20),
    )(*result, mixer_in, first_gain.reshape(1, rows))
    block_out, input_grad, g_one, g_mi, g_taps, g_mo, g_two, g_gate, g_up, g_down = finished

    def shared(item, axis=0):
        if spare == 1:
            return item
        return lax.psum_scatter(
            item, axes, scatter_dimension=axis, axis_index_groups=groups, tiled=True
        )

    return (
        block_out.reshape(row_count, seq_here, width),
        input_grad.reshape(row_count, seq_here, width),
        shared(g_one.reshape(rows)),
        shared(g_mi),
        shared(g_taps, 1),
        shared(g_mo),
        shared(g_two.reshape(rows)),
        shared(g_gate),
        shared(g_up),
        shared(g_down),
    )


def solution(mesh):
    fsdp_count = mesh.shape["fsdp"]
    device_count = mesh.shape["dp"] * fsdp_count
    return jax.shard_map(
        functools.partial(per_device, fsdp_count, device_count),
        mesh=mesh,
        in_specs=(
            P("dp", "fsdp", None),
            P("dp", None),
            P("dp", "fsdp"),
            P("dp", "fsdp", None),
            P(("dp", "fsdp")),
            P(("dp", "fsdp"), None),
            P(None, ("dp", "fsdp")),
            P(("dp", "fsdp"), None),
            P(("dp", "fsdp")),
            P(("dp", "fsdp"), None),
            P(("dp", "fsdp"), None),
            P(("dp", "fsdp"), None),
        ),
        out_specs=(
            P("dp", "fsdp", None),
            P("dp", "fsdp", None),
            P(("dp", "fsdp")),
            P(("dp", "fsdp"), None),
            P(None, ("dp", "fsdp")),
            P(("dp", "fsdp"), None),
            P(("dp", "fsdp")),
            P(("dp", "fsdp"), None),
            P(("dp", "fsdp"), None),
            P(("dp", "fsdp"), None),
        ),
        check_vma=False,
    )
```

```python
import functools
import math

import jax
import jax.numpy as jnp
from jax import lax
from jax.experimental import pallas as pl
from jax.experimental.pallas import tpu as pltpu
from jax.sharding import PartitionSpec as P

EPSILON = 1e-05
MESH = pl.DeviceIdType.MESH
F32 = jnp.float32
BF16 = jnp.bfloat16
PLACES = 32


def nn(a, b):
    return jnp.dot(a, b, preferred_element_type=F32)


def nt(a, b):
    return lax.dot_general(a, b, (((1,), (1,)), ((), ())), preferred_element_type=F32)


def tn(a, b):
    return lax.dot_general(a, b, (((0,), (0,)), ((), ())), preferred_element_type=F32)


def kernel(
    fsdp_count,
    copies_of_place,
    factor,
    tokens_hbm,
    cotangent,
    document,
    loss_mask,
    gain_one,
    gain_two,
    taps,
    mixer_in_hbm,
    mixer_out,
    gate_hbm,
    up_hbm,
    down,
    block_out,
    input_sum,
    small_out,
    mi_sum,
    mo_sum,
    gu_sum,
    dn_sum,
    input_grad,
    tokens,
    mixer_in,
    gate,
    up,
    small_tile,
    small_all,
    small_grad,
    small_in,
    w_mi,
    w_mo,
    w_gu,
    w_dn,
    mi_stage,
    gu_stage,
    xs,
    flags,
    gs,
    hs,
    proj,
    ubuf,
    conv,
    ys,
    dps,
    x2,
    o_send,
    o_recv,
    pre,
    dm_buf,
    ms,
    dabs,
    acc,
    dhp,
    dh_a,
    dh_b,
    dh_x,
    dh_y,
    dos,
    r_gu_c,
    r_gu_0,
    r_gu_1,
    r_dn_c,
    r_dn_0,
    r_dn_1,
    r_mi_c,
    r_mi_y,
    r_mi_0,
    r_mi_1,
    r_mo_c,
    r_mo_y,
    r_mo_0,
    r_mo_1,
    rows_buf,
    send,
    recv,
    load_sem,
    store_sem,
    small_send,
    small_recv,
    back_send,
    back_recv,
    free_x,
    free_y,
):
    toks, width = tokens.shape
    dkbuf = pre
    rows = mixer_in.shape[0]
    half_width = width // 2
    units = w_dn.shape[0] * w_dn.shape[1] * w_dn.shape[2] * w_dn.shape[3]
    part = units // 3
    half = toks // 2
    step = 32

    dp, fs = lax.axis_index("dp"), lax.axis_index("fsdp")
    number = dp * fsdp_count + fs
    v = lax.div(number, copies_of_place)
    rep = lax.rem(number, copies_of_place)
    c = lax.rem(v, 2)
    x = lax.rem(lax.div(v, 2), 2)
    y = lax.rem(lax.div(v, 4), 2)
    z0 = lax.rem(lax.div(v, 8), 2)
    z1 = lax.div(v, 16)
    p = 2 * y + x
    px = 2 * y + (1 - x)
    py = 2 * (1 - y) + x
    pd = 2 * (1 - y) + (1 - x)

    def dev(place):
        whole = place * copies_of_place + rep
        return (lax.div(whole, fsdp_count), lax.rem(whole, fsdp_count))

    cn = dev(v + (1 - 2 * c))
    xn = dev(v + 2 * (1 - 2 * x))
    yn = dev(v + 4 * (1 - 2 * y))
    dn = dev(v + 2 * (1 - 2 * x) + 4 * (1 - 2 * y))
    z0n = dev(v + 8 * (1 - 2 * z0))
    z1n = dev(v + 16 * (1 - 2 * z1))
    following = (dp, lax.rem(fs + 1, fsdp_count))
    preceding = (dp, lax.rem(fs + fsdp_count - 1, fsdp_count))

    counter = [0]
    started = []

    def remote(src, dst, target):
        at = counter[0]
        counter[0] += 1
        return pltpu.make_async_remote_copy(
            src_ref=src, dst_ref=dst, send_sem=send.at[at], recv_sem=recv.at[at],
            device_id=target, device_id_type=MESH,
        )

    def go(copy):
        copy.start()
        started.append(copy)
        return copy

    def same(ref, target):
        return remote(ref, ref, target)

    def sent(copy):
        copy.wait_send()
        started[:] = [other for other in started if other is not copy]

    barrier = pltpu.get_barrier_semaphore()

    def greet(m, _):
        pl.semaphore_signal(
            barrier, inc=1, device_id=dev(lax.rem(v + m, PLACES)), device_id_type=MESH
        )
        return 0

    lax.fori_loop(1, PLACES, greet, 0)
    pl.semaphore_signal(barrier, inc=1, device_id=following, device_id_type=MESH)
    pl.semaphore_signal(barrier, inc=1, device_id=preceding, device_id_type=MESH)

    load_mixer = pltpu.make_async_copy(mixer_in_hbm, mixer_in, load_sem.at[3])
    load_tokens = pltpu.make_async_copy(tokens_hbm, tokens, load_sem.at[4])
    load_gate = pltpu.make_async_copy(gate_hbm, gate, load_sem.at[5])
    load_up = pltpu.make_async_copy(up_hbm, up, load_sem.at[6])
    load_mixer.start()
    load_out = pltpu.make_async_copy(mixer_out, w_mo.at[z1, z0, y, c], load_sem.at[0])
    load_down = pltpu.make_async_copy(down, w_dn.at[z1, z0, c], load_sem.at[1])
    load_cot = pltpu.make_async_copy(cotangent, gs.at[p], load_sem.at[2])
    load_out.start()
    load_down.start()
    load_cot.start()
    load_gate.start()
    load_up.start()
    load_tokens.start()

    lane = lax.broadcasted_iota(jnp.int32, (1, 128), 1)
    mine = lax.div(lane, 32) == lax.rem(v, 4)
    small_tile[...] = jnp.zeros_like(small_tile)

    def spread(values):
        wide = jnp.concatenate([values.astype(F32)] * 4, axis=1)
        return jnp.where(mine, wide, 0.0)

    small_tile[0:1, :] = spread(gain_one[...])
    small_tile[1:2, :] = spread(gain_two[...])
    small_tile[2:5, :] = spread(taps[...])

    lanes128 = lax.broadcasted_iota(jnp.int32, (rows, 128), 1)
    low = lanes128 < 64
    load_mixer.wait()
    for b in range(3):
        for q in range(width // 256):
            at = b * width + 256 * q
            even = mixer_in[:, at : at + 128].astype(F32)
            odd = mixer_in[:, at + 128 : at + 256].astype(F32)
            to = b * half_width + 128 * q
            mi_stage[0, :, to : to + 128] = jnp.where(low, even, pltpu.roll(odd, 64, 1)).astype(BF16)
            mi_stage[1, :, to : to + 128] = jnp.where(low, pltpu.roll(even, 64, 1), odd).astype(BF16)
    w_mi[z1, z0, y, x, c] = mi_stage[x]
    small_all[v] = small_tile[...]

    pl.semaphore_wait(barrier, PLACES + 1)

    def small_copy(src, dst, m, sems=(small_send, small_recv)):
        return pltpu.make_async_remote_copy(
            src_ref=src, dst_ref=dst, send_sem=sems[0].at[m], recv_sem=sems[1].at[m],
            device_id=dev(lax.rem(v + m, PLACES)), device_id_type=MESH,
        )

    def small_start(m, _):
        small_copy(small_tile, small_all.at[v], m).start()
        return 0

    mi_swap = go(remote(mi_stage.at[1 - x], w_mi.at[z1, z0, y, x, c], xn))
    lax.fori_loop(1, PLACES, small_start, 0)
    tok_swap = go(remote(tokens_hbm, xs.at[x], xn))

    def mo_at(a, b, yy, cc):
        return w_mo.at[a, b, yy, cc]

    def mi_at(a, b, yy, cc):
        return w_mi.at[a, b, yy, :, cc]

    every = slice(None)

    def mix_gather(at):
        return dict(
            s1=same(at(z1, z0, y, c), z1n),
            s2=same(at(z1, z0, y, c), z0n),
            s3=same(at(1 - z1, z0, y, c), z0n),
            y0=same(at(z1, z0, y, c), yn),
            y1=same(at(1 - z1, z0, y, c), yn),
            y2=same(at(z1, 1 - z0, y, c), yn),
            y3=same(at(1 - z1, 1 - z0, y, c), yn),
            ca=same(at(every, every, y, c), cn),
            cb=same(at(every, every, 1 - y, c), cn),
        )

    wide = 3 * half_width

    def mi_half(h):
        columns = pl.ds(h * (wide // 2), wide // 2)
        return lambda a, b, yy, cc: w_mi.at[a, b, yy, :, cc, :, columns]

    mo_g = mix_gather(mo_at)
    mi_gs = [mix_gather(mi_half(0)), mix_gather(mi_half(1))]
    load_out.wait()
    go(mo_g["s1"])
    go(mo_g["s2"])
    mi_swap.wait_recv()
    for g in mi_gs:
        for name in ("s1", "s2", "y0"):
            go(g[name])

    offset = fs * toks
    ids = document[...].astype(F32) + 1.0
    mask_row = loss_mask[...].astype(F32)
    id_lane = lax.broadcasted_iota(jnp.int32, (step, ids.shape[1]), 1)
    id_row = lax.broadcasted_iota(jnp.int32, (step, ids.shape[1]), 0)
    ma_lane = lax.broadcasted_iota(jnp.int32, (step, toks), 1)
    ma_row = lax.broadcasted_iota(jnp.int32, (step, toks), 0)
    fl_lane = lax.broadcasted_iota(jnp.int32, (step, 128), 1)

    def flag_rows(i, _):
        base = i * step
        at = pl.ds(pl.multiple_of(base, step), step)

        def column(shift):
            hit = id_lane == id_row + (offset + base + shift)
            return jnp.sum(jnp.where(hit, ids, 0.0), axis=1, keepdims=True)

        centre = column(0)
        tile = jnp.zeros((step, 128), F32)
        for k, shift in enumerate((-1, -2, 1, 2)):
            tile = jnp.where(
                jnp.logical_and(fl_lane == k, column(shift) == centre), 1.0, tile
            )
        flags[x, at, :] = tile.astype(BF16)
        keep = jnp.sum(
            jnp.where(ma_lane == ma_row + base, mask_row, 0.0), axis=1, keepdims=True
        )
        gs[p, at, :] = (gs[p, at, :].astype(F32) * keep).astype(BF16)
        return 0

    run = units // 4

    def pick(ref, at_p):
        whole = ref[...].astype(F32)
        return jnp.concatenate(
            [whole[:, run * (4 * z + at_p) : run * (4 * z + at_p) + run] for z in range(4)], axis=1
        ).astype(BF16)

    def forward(g, arrived, names):
        g[arrived].wait_recv()
        for name in names:
            go(g[name])

    def z_gather(at):
        return dict(
            s1=same(at(z1, z0, c), z1n),
            s2=same(at(z1, z0, c), z0n),
            s3=same(at(1 - z1, z0, c), z0n),
            core=same(at(every, every, c), cn),
        )

    dn_g = z_gather(lambda a, b, cc: w_dn.at[a, b, cc])
    gu_g = [z_gather(lambda a, b, cc, j=j: w_gu.at[j, a, b, :, cc]) for j in range(3)]

    def z_start(g):
        go(g["s1"])
        go(g["s2"])

    def z_forward(g):
        forward(g, "s1", ("s3",))

    def z_core(g):
        g["s2"].wait_recv()
        g["s3"].wait_recv()
        go(g["core"])

    def plane_gather(buf, halves):
        lo, hi = pl.ds(0, half), pl.ds(half, half)
        return dict(
            x0=same(buf.at[p, lo], xn),
            y1=same(buf.at[p, hi], yn),
            x1=same(buf.at[p, hi], xn),
            y0=same(buf.at[p, lo], yn),
            fx=same(buf.at[px, lo] if halves else buf.at[px], yn),
            **(dict(fy=same(buf.at[py, hi], xn)) if halves else {}),
        )

    def plane_forward(g):
        forward(g, "x0", ("fx",))
        forward(g, "y1", ("fy",))

    gs_g, hs_g = plane_gather(gs, False), plane_gather(hs, True)

    load_cot.wait()
    lax.fori_loop(0, toks // step, flag_rows, 0)
    flag_swap = go(same(flags.at[x], xn))
    load_gate.wait()
    load_up.wait()
    for at_p in range(4):
        picked_gate, picked_up = pick(gate, at_p), pick(up, at_p)
        for j in range(3):
            gu_stage[at_p, j, :, 0:part] = picked_gate[:, j * part : j * part + part]
            gu_stage[at_p, j, :, part:] = picked_up[:, j * part : j * part + part]
    load_tokens.wait()
    xs[x] = tokens[...]
    for j in range(3):
        w_gu[j, z1, z0, p, c] = gu_stage[p, j]

    go(mo_g["y0"])
    forward(mo_g, "s1", ("s3", "y1"))
    forward(mo_g, "s2", ("y2",))
    for g in mi_gs:
        forward(g, "s1", ("s3", "y1"))
        forward(g, "s2", ("y2",))
    gu_swap = [
        remote(gu_stage.at[px], w_gu.at[:, z1, z0, p, c], xn),
        remote(gu_stage.at[py], w_gu.at[:, z1, z0, p, c], yn),
        remote(gu_stage.at[pd], w_gu.at[:, z1, z0, p, c], dn),
    ]
    go(gu_swap[2])
    go(gu_swap[0])
    go(gs_g["x0"])
    go(gs_g["x1"])

    def small_wait(m, _):
        copy = small_copy(small_tile, small_all.at[v], m)
        copy.wait()
        return 0

    lax.fori_loop(1, PLACES, small_wait, 0)
    natural = []
    for q in range(8):
        natural.append(
            small_all[4 * q] + small_all[4 * q + 1] + small_all[4 * q + 2] + small_all[4 * q + 3]
        )
    for q in range(8):
        rows_buf[:, 128 * q : 128 * q + 128] = natural[q]
    low8 = lax.broadcasted_iota(jnp.int32, (8, 128), 1) < 64
    is_one = x == 1
    for q in range(4):
        even, odd = natural[2 * q], natural[2 * q + 1]
        first = jnp.where(low8, even, pltpu.roll(odd, 64, 1))
        second = jnp.where(low8, pltpu.roll(even, 64, 1), odd)
        rows_buf[:, width + 128 * q : width + 128 * q + 128] = jnp.where(is_one, second, first)
    g1 = rows_buf[0:1, 0:width]
    g2 = rows_buf[1:2, 0:width]
    tap0 = rows_buf[2:3, width : width + half_width]
    tap1 = rows_buf[3:4, width : width + half_width]
    tap2 = rows_buf[4:5, width : width + half_width]

    def inverse_rms(values):
        return lax.rsqrt(jnp.mean(values * values, axis=1, keepdims=True) + EPSILON)

    def loop(count, body):
        def wrapped(i, _):
            body(pl.ds(pl.multiple_of(i * step, step), step))
            return 0

        lax.fori_loop(0, count // step, wrapped, 0)

    def hidden_one(s):
        def body(at):
            values = xs[s, at, :].astype(F32)
            xs[s, at, :] = (values * inverse_rms(values) * g1).astype(BF16)

        loop(toks, body)

    for g in mi_gs:
        forward(g, "s3", ("y3",))
        go(g["ca"])
    forward(mo_g, "s3", ("y3",))
    go(mo_g["ca"])
    go(gu_swap[1])
    load_down.wait()
    z_start(dn_g)
    hidden_one(x)
    tok_swap.wait_recv()
    hidden_one(1 - x)
    for g in mi_gs:
        for name in ("y0", "y1", "y2", "y3"):
            g[name].wait_recv()
        go(g["cb"])
    go(gs_g["y1"])
    go(gs_g["y0"])
    for g in mi_gs:
        g["ca"].wait_recv()
        g["cb"].wait_recv()
    h1 = xs[...].reshape(2 * toks, width)
    proj[...] = nn(h1, w_mi[...].reshape(width, wide)).reshape(2, toks, wide)

    for s in range(2):
        def body(at, s=s):
            ubuf[s, pl.ds(pl.multiple_of(at.start + 8, 8), step), :] = (
                proj[s, at, 0:half_width] * proj[s, at, 2 * half_width :]
            )

        loop(toks, body)
    halo = go(remote(ubuf.at[:, pl.ds(toks, 8), :], ubuf.at[:, pl.ds(0, 8), :], following))
    z_forward(dn_g)
    for copy in gu_swap:
        copy.wait_recv()
    z_start(gu_g[0])
    z_start(gu_g[1])
    for name in ("y0", "y1", "y2", "y3"):
        mo_g[name].wait_recv()
    go(mo_g["cb"])
    flag_swap.wait_recv()
    halo.wait_recv()
    for s in range(2):
        for i in range(toks // step):
            a = i * step
            fl = flags[s, a : a + step, :].astype(F32)
            value = (
                tap2 * ubuf[s, a + 8 : a + 8 + step, :]
                + tap1 * (fl[:, 0:1] * ubuf[s, a + 7 : a + 7 + step, :])
                + tap0 * (fl[:, 1:2] * ubuf[s, a + 6 : a + 6 + step, :])
            )
            conv[s, a : a + step, :] = value
            ys[s, a : a + step, :] = (
                proj[s, a : a + step, half_width : 2 * half_width] * value
            ).astype(BF16)
    mo_g["ca"].wait_recv()
    mo_g["cb"].wait_recv()
    mo_flat = w_mo[...].reshape(half_width, width)
    o_send[...] = nn(ys[1 - x], mo_flat).astype(BF16)
    o_swap = go(remote(o_send, o_recv, xn))
    x2[...] = nn(ys[x], mo_flat)

    forward(gs_g, "x0", ())
    forward(gs_g, "x1", ("fx",))
    z_core(dn_g)
    for copy in gu_swap:
        sent(copy)
    sent(mi_swap)

    def second_body(at):
        values = tokens[at, :].astype(F32) + x2[at, :] + o_recv[at, :].astype(F32)
        x2[at, :] = values
        hs[p, at, :] = (values * inverse_rms(values) * g2).astype(BF16)

    o_swap.wait_recv()
    loop(toks, second_body)
    for name in ("x0", "y1", "x1", "y0"):
        go(hs_g[name])
    z_forward(gu_g[0])
    z_forward(gu_g[1])
    z_start(gu_g[2])
    plane_forward(hs_g)
    z_core(gu_g[0])

    ya, yb = 2 * y, 2 * (1 - y)

    def plane_pair(g, names):
        for name in names:
            g[name].wait_recv()

    def pair_rows(ref, base):
        return ref[pl.ds(base, 2)].reshape(2 * toks, width)

    def feed(j, base):
        w = w_gu[j].reshape(width, 2 * part)
        pre[:, 0:toks, :] = nn(pair_rows(hs, base), w).reshape(2, toks, 2 * part)
        down_rows = w_dn[...].reshape(units, width)[j * part : j * part + part]
        dm_buf[...] = nt(pair_rows(gs, base), down_rows)

        def body(i, _):
            at = pl.ds(pl.multiple_of(i * step, step), step)
            slot = base + lax.div(i, toks // step)
            inner = pl.ds(pl.multiple_of(lax.rem(i, toks // step) * step, step), step)
            which = lax.div(i, toks // step)
            a = pre[which, inner, 0:part]
            b = pre[which, inner, part:]
            d = dm_buf[at, :]
            sg = jax.nn.sigmoid(a)
            silu = a * sg
            ms[slot, inner, j * part : j * part + part] = (silu * b).astype(BF16)
            chunk = lax.rem(i, toks // step)
            at = (lax.div(chunk, 4), lax.rem(lax.div(chunk, 2), 2), lax.rem(chunk, 2))
            dabs[(j, lax.div(base, 2), which, *at, every, slice(0, part))] = (
                d * b * sg * (1.0 + a * (1.0 - sg))
            ).astype(BF16)
            dabs[(j, lax.div(base, 2), which, *at, every, slice(part, 2 * part))] = (
                d * silu
            ).astype(BF16)
            return 0

        lax.fori_loop(0, 2 * toks // step, body, 0)
        back = nt(dabs[j, lax.div(base, 2)].reshape(2 * toks, 2 * part), w)
        back = back.reshape(2, toks, width)
        if j == 0:
            acc[pl.ds(base, 2)] = back
        elif j == 1:
            acc[pl.ds(base, 2)] += back
        else:
            total = acc[pl.ds(base, 2)] + back
            acc[pl.ds(base, 2)] = total
            dhp[pl.ds(base, 2)] = total.astype(BF16)

    def gu_weight_grad(j):
        w_gu[j] = (
            tn(hs[...].reshape(4 * toks, width), dabs[j].reshape(4 * toks, 2 * part))
            .astype(BF16)
            .reshape(w_gu.shape[1:])
        )

    def plane_scatter(buf, r_a, r_b, r_x, r_y):
        lo, hi = pl.ds(0, half), pl.ds(half, half)
        return dict(
            a=remote(buf.at[pd, lo], r_a, xn),
            b=remote(buf.at[pd, hi], r_b, yn),
            x0=remote(buf.at[px, lo], r_x.at[lo], xn),
            y1=remote(buf.at[py, hi], r_y.at[hi], yn),
            x1=remote(buf.at[px, hi], r_x.at[hi], xn),
            y0=remote(buf.at[py, lo], r_y.at[lo], yn),
        )

    def add_rows(buf, slot, start, other):
        def body(at):
            into = pl.ds(pl.multiple_of(at.start + start, step), step)
            buf[slot, into, :] = (
                buf[slot, into, :].astype(F32) + other[at, :].astype(F32)
            ).astype(BF16)

        loop(half, body)

    def scatter_rest(g, buf, r_a, r_b):
        g["b"].wait_recv()
        add_rows(buf, px, half, r_b)
        go(g["x1"])
        g["a"].wait_recv()
        add_rows(buf, py, 0, r_a)
        go(g["y0"])

    def z_reduce(at, r_c, r_0, r_1):
        return dict(
            core=remote(at(every, every, 1 - c), r_c, cn),
            z0=remote(at(every, 1 - z0, c), r_0, z0n),
            z1=remote(at(1 - z1, z0, c), r_1, z1n),
        )

    gu_r = [
        z_reduce(lambda a, b, cc, j=j: w_gu.at[j, a, b, :, cc], r_gu_c.at[j % 2], r_gu_0.at[j], r_gu_1.at[j])
        for j in range(3)
    ]
    dn_r = z_reduce(lambda a, b, cc: w_dn.at[a, b, cc], r_dn_c, r_dn_0, r_dn_1)

    def plus(one, two):
        return (one.astype(F32) + two.astype(F32)).astype(BF16)

    def gu_after_core(j):
        gu_r[j]["core"].wait_recv()
        for a in range(2):
            for b in range(2):
                w_gu[j, a, b, :, c] = plus(w_gu[j, a, b, :, c], r_gu_c[j % 2, a, b])
        go(gu_r[j]["z0"])

    def gu_after_z0(j):
        gu_r[j]["z0"].wait_recv()
        for a in range(2):
            w_gu[j, a, z0, :, c] = plus(w_gu[j, a, z0, :, c], r_gu_0[j, a])
        go(gu_r[j]["z1"])

    gu_back = []

    def gu_sum_z1(j):
        gu_r[j]["z1"].wait_recv()
        w_gu[j, z1, z0, :, c] = plus(w_gu[j, z1, z0, :, c], r_gu_1[j])
        gu_stage[p, j] = w_gu[j, z1, z0, p, c]

    def gu_return(j):
        for place, target in ((px, xn), (py, yn), (pd, dn)):
            gu_back.append(go(remote(w_gu.at[j, z1, z0, place, c], gu_stage.at[p, j], target)))

    def gathered(g):
        for name in ("s1", "s2", "s3", "core"):
            sent(g[name])

    dn_g["core"].wait_recv()
    plane_pair(hs_g, ("x1",))
    gu_g[0]["core"].wait_recv()
    feed(0, ya)
    z_core(gu_g[1])
    plane_pair(gs_g, ("y0", "y1", "fx"))
    plane_pair(hs_g, ("y0", "fx", "fy"))
    feed(0, yb)
    z_forward(gu_g[2])
    gathered(gu_g[0])
    gu_weight_grad(0)
    go(gu_r[0]["core"])
    gu_after_core(0)
    gu_g[1]["core"].wait_recv()
    feed(1, yb)
    z_core(gu_g[2])
    feed(1, ya)
    gu_g[2]["core"].wait_recv()
    feed(2, yb)
    dh_g = plane_scatter(dhp, dh_a, dh_b, dh_x, dh_y)
    go(dh_g["a"])
    go(dh_g["b"])
    go(dh_g["y1"])
    gu_after_z0(0)
    feed(2, ya)
    go(dh_g["x0"])
    gathered(gu_g[1])
    gu_weight_grad(1)
    go(gu_r[1]["core"])
    gathered(gu_g[2])
    gu_weight_grad(2)
    gu_after_core(1)
    go(gu_r[2]["core"])
    scatter_rest(dh_g, dhp, dh_a, dh_b)

    for name in ("x0", "x1", "y0", "y1", "fx", "fy"):
        sent(hs_g[name])
    dn_flat = w_dn[...].reshape(units, width)
    for base in (ya, yb):
        m = ms[pl.ds(base, 2)].reshape(2 * toks, units)
        hs[pl.ds(base, 2)] = nn(m, dn_flat).astype(BF16).reshape(2, toks, width)
    gu_after_core(2)
    gathered(dn_g)
    w_dn[...] = (
        tn(ms[...].reshape(4 * toks, units), gs[...].reshape(4 * toks, width))
        .astype(BF16)
        .reshape(w_dn.shape)
    )
    go(dn_r["core"])
    dn_r["core"].wait_recv()
    for a in range(2):
        for b in range(2):
            w_dn[a, b, c] = plus(w_dn[a, b, c], r_dn_c[a, b])
    go(dn_r["z0"])

    for name in ("x0", "x1", "y0", "y1"):
        dh_g[name].wait_recv()
    small_grad[...] = jnp.zeros_like(small_grad)

    def norm_two(at):
        dh = acc[p, at, :] + dh_x[at, :].astype(F32) + dh_y[at, :].astype(F32)
        values = x2[at, :]
        inverse = inverse_rms(values)
        normed = values * inverse
        small_grad[1:2, :] += jnp.sum(dh * normed, axis=0, keepdims=True)
        q = dh * g2
        grad = gs[p, at, :].astype(F32) + inverse * (
            q - normed * jnp.mean(q * normed, axis=1, keepdims=True)
        )
        input_grad[at, :] = grad
        dos[x, at, :] = grad.astype(BF16)

    loop(toks, norm_two)
    do_swap = go(same(dos.at[x], xn))
    lo, hi = pl.ds(0, half), pl.ds(half, half)
    ou_g = plane_scatter(hs, dhp.at[py, lo], dhp.at[px, hi], dhp.at[p], dhp.at[p])
    for copy in dh_g.values():
        sent(copy)
    pl.semaphore_signal(free_x, inc=1, device_id=xn, device_id_type=MESH)
    pl.semaphore_signal(free_y, inc=1, device_id=yn, device_id_type=MESH)
    pl.semaphore_wait(free_x, 1)
    pl.semaphore_wait(free_y, 1)
    for name in ("b", "y1", "a"):
        go(ou_g[name])

    mo_flat = w_mo[...].reshape(half_width, width)

    def split_dy(s):
        def body(at):
            dy = dkbuf[s, at, 0:half_width]
            dps[s, at, half_width : 2 * half_width] = (dy * conv[s, at, :]).astype(BF16)
            dkbuf[s, at, 0:half_width] = dy * proj[s, at, half_width : 2 * half_width]

        loop(toks, body)

    dkbuf[x, 0:toks, 0:half_width] = nt(dos[x], mo_flat)
    split_dy(x)
    gu_after_z0(1)
    gu_sum_z1(0)
    gu_return(0)
    gu_after_z0(2)
    do_swap.wait_recv()
    dkbuf[1 - x, 0:toks, 0:half_width] = nt(dos[1 - x], mo_flat)
    split_dy(1 - x)
    dk_halo = go(
        remote(
            dkbuf.at[:, pl.ds(0, 8), pl.ds(0, half_width)],
            dkbuf.at[:, pl.ds(toks, 8), pl.ds(0, half_width)],
            preceding,
        )
    )
    for g in (mo_g, *mi_gs):
        for copy in g.values():
            sent(copy)
    w_mo[...] = (
        tn(ys[...].reshape(2 * toks, half_width), dos[...].reshape(2 * toks, width))
        .astype(BF16)
        .reshape(w_mo.shape)
    )

    def mix_reduce(at, r_c, r_y, r_0, r_1):
        return dict(
            ca=remote(at(every, every, 1 - y, 1 - c), r_c.at[:, :, 1 - y], cn),
            cb=remote(at(every, every, y, 1 - c), r_c.at[:, :, y], cn),
            y3=remote(at(1 - z1, 1 - z0, 1 - y, c), r_y.at[1 - z1, 1 - z0], yn),
            y2=remote(at(z1, 1 - z0, 1 - y, c), r_y.at[z1, 1 - z0], yn),
            y1=remote(at(1 - z1, z0, 1 - y, c), r_y.at[1 - z1, z0], yn),
            y0=remote(at(z1, z0, 1 - y, c), r_y.at[z1, z0], yn),
            s3=remote(at(1 - z1, 1 - z0, y, c), r_0.at[1 - z1], z0n),
            s2=remote(at(z1, 1 - z0, y, c), r_0.at[z1], z0n),
            s1=remote(at(1 - z1, z0, y, c), r_1, z1n),
        )

    mo_r = mix_reduce(mo_at, r_mo_c, r_mo_y, r_mo_0, r_mo_1)
    mi_rs = [
        mix_reduce(
            lambda a, b, yy, cc, h=h: dabs.at[h, a, b, yy, :, cc],
            r_mi_c.at[h], r_mi_y.at[h], r_mi_0.at[h], r_mi_1.at[h],
        )
        for h in range(2)
    ]
    go(mo_r["ca"])
    go(mo_r["cb"])
    def mix_core(w, r_c, g, with_x):
        def add(yy):
            for a in range(2):
                for b in range(2):
                    if with_x:
                        w[a, b, yy, :, c] = plus(w[a, b, yy, :, c], r_c[a, b, yy])
                    else:
                        w[a, b, yy, c] = plus(w[a, b, yy, c], r_c[a, b, yy])

        g["ca"].wait_recv()
        add(1 - y)
        for name in ("y3", "y1", "y2", "y0"):
            go(g[name])
        g["cb"].wait_recv()
        add(y)

    dk_halo.wait_recv()
    ek = [jnp.zeros((1, half_width), F32) for _ in range(3)]
    for s in range(2):
        for i in range(toks // step):
            a = i * step
            fl = flags[s, a : a + step, :].astype(F32)
            dk = dkbuf[s, a : a + step, 0:half_width]
            ek[2] += jnp.sum(dk * ubuf[s, a + 8 : a + 8 + step, :], axis=0, keepdims=True)
            ek[1] += jnp.sum(
                dk * (fl[:, 0:1] * ubuf[s, a + 7 : a + 7 + step, :]), axis=0, keepdims=True
            )
            ek[0] += jnp.sum(
                dk * (fl[:, 1:2] * ubuf[s, a + 6 : a + 6 + step, :]), axis=0, keepdims=True
            )
            du = (
                tap2 * dk
                + tap1 * (fl[:, 2:3] * dkbuf[s, a + 1 : a + 1 + step, 0:half_width])
                + tap0 * (fl[:, 3:4] * dkbuf[s, a + 2 : a + 2 + step, 0:half_width])
            )
            dps[s, a : a + step, 0:half_width] = (
                du * proj[s, a : a + step, 2 * half_width :]
            ).astype(BF16)
            dps[s, a : a + step, 2 * half_width :] = (
                du * proj[s, a : a + step, 0:half_width]
            ).astype(BF16)
    for k in range(3):
        for q in range(4):
            chunk = jnp.broadcast_to(ek[k][:, 128 * q : 128 * q + 128], (8, 128))
            turned = pltpu.roll(chunk, 64, 1)
            even = jnp.where(is_one, jnp.where(low8, 0.0, turned), jnp.where(low8, chunk, 0.0))
            odd = jnp.where(is_one, jnp.where(low8, 0.0, chunk), jnp.where(low8, turned, 0.0))
            small_grad[2 + k : 3 + k, 256 * q : 256 * q + 128] = even[0:1]
            small_grad[2 + k : 3 + k, 256 * q + 128 : 256 * q + 256] = odd[0:1]

    for q in range(8):
        small_in[PLACES + q] = small_grad[:, 128 * q : 128 * q + 128]

    def small_back(m):
        target = lax.rem(v + m, PLACES)
        source = small_in.at[PLACES + lax.div(target, 4)]
        return small_copy(source, small_in.at[v], m, (back_send, back_recv))

    def small_back_start(m, _):
        small_back(m).start()
        return 0

    lax.fori_loop(1, PLACES, small_back_start, 0)
    small_in[v] = small_in[PLACES + lax.div(v, 4)]

    mix_core(w_mo, r_mo_c, mo_r, False)
    columns = 2 * part
    for h in range(2):
        dabs[h] = (
            tn(
                xs[...].reshape(2 * toks, width),
                dps[:, :, h * columns : (h + 1) * columns].reshape(2 * toks, columns),
            )
            .astype(BF16)
            .reshape(dabs.shape[1:])
        )
        go(mi_rs[h]["ca"])
        go(mi_rs[h]["cb"])
    mi_flat = w_mi[...].reshape(width, wide)
    sent(o_swap)
    o_send[...] = nt(dps[1 - x], mi_flat).astype(BF16)
    dh1_swap = go(remote(o_send, o_recv, xn))
    mix_core(dabs.at[0], r_mi_c.at[0], mi_rs[0], True)
    mix_core(dabs.at[1], r_mi_c.at[1], mi_rs[1], True)
    dn_r["z0"].wait_recv()
    for a in range(2):
        w_dn[a, z0, c] = plus(w_dn[a, z0, c], r_dn_0[a])
    go(dn_r["z1"])
    ou_g["a"].wait_recv()
    add_rows(hs, py, 0, dhp.at[pd, lo])
    go(ou_g["y0"])
    ou_g["b"].wait_recv()
    add_rows(hs, px, half, dhp.at[pd, hi])
    go(ou_g["x0"])
    go(ou_g["x1"])
    acc[p] = nt(dps[x], mi_flat)

    def mo_idx(a, b):
        return (a, b, y, c)

    def mi_idx(a, b):
        return (a, b, y, every, c)

    mo_parts = (w_mo, mo_idx, mo_r, r_mo_y, r_mo_0)
    mi_parts = [
        (dabs.at[h], mi_idx, mi_rs[h], r_mi_y.at[h], r_mi_0.at[h]) for h in range(2)
    ]

    def mix_three(w, idx, g, r_y, r_0):
        g["y3"].wait_recv()
        at = idx(1 - z1, 1 - z0)
        w[at] = plus(w[at], r_y[1 - z1, 1 - z0])
        go(g["s3"])

    def mix_one(w, idx, g, r_y, r_0):
        g["y1"].wait_recv()
        g["s3"].wait_recv()
        at = idx(1 - z1, z0)
        w[at] = plus(plus(w[at], r_y[1 - z1, z0]), r_0[1 - z1])
        go(g["s1"])

    def mix_two(w, idx, g, r_y, r_0):
        g["y2"].wait_recv()
        at = idx(z1, 1 - z0)
        w[at] = plus(w[at], r_y[z1, 1 - z0])
        go(g["s2"])

    def mix_last(w, idx, g, r_y, r_0):
        g["y0"].wait_recv()
        g["s2"].wait_recv()
        at = idx(z1, z0)
        w[at] = plus(plus(w[at], r_y[z1, z0]), r_0[z1])

    mix_three(*mo_parts)
    mix_three(*mi_parts[0])
    mix_three(*mi_parts[1])
    dh1_swap.wait_recv()

    def norm_one(at):
        dh = acc[p, at, :] + o_recv[at, :].astype(F32)
        values = tokens[at, :].astype(F32)
        inverse = inverse_rms(values)
        normed = values * inverse
        q = dh * g1
        input_grad[at, :] = input_grad[at, :] + inverse * (
            q - normed * jnp.mean(q * normed, axis=1, keepdims=True)
        )

    loop(toks, norm_one)

    stores = []

    def store(src, dst):
        copy = pltpu.make_async_copy(src, dst, store_sem.at[len(stores)])
        copy.start()
        stores.append(copy)

    store(input_grad, input_sum)
    gu_sum_z1(1)
    gu_return(1)

    mix_one(*mo_parts)
    mix_two(*mo_parts)
    mix_one(*mi_parts[0])
    mix_two(*mi_parts[0])
    mix_one(*mi_parts[1])
    mix_two(*mi_parts[1])
    gu_sum_z1(2)
    gu_return(2)
    for name in ("x0", "x1", "y0", "y1"):
        ou_g[name].wait_recv()

    def out_body(at):
        o_send[at, :] = (
            x2[at, :]
            + hs[p, at, :].astype(F32)
            + dhp[px, at, :].astype(F32)
            + dhp[py, at, :].astype(F32)
        ).astype(BF16)

    sent(dh1_swap)
    loop(toks, out_body)

    store(o_send, block_out)
    down_rows = w_dn.shape[3]
    def small_back_wait(m, _):
        small_back(m).wait()
        return 0

    lax.fori_loop(1, PLACES, small_back_wait, 0)
    total = small_in[0]
    for q in range(1, PLACES):
        total = total + small_in[q]
    total = total * factor
    small_out[...] = total

    mix_last(*mo_parts)
    dn_r["z1"].wait_recv()
    acc[3, 0:down_rows] = (w_dn[z1, z0, c].astype(F32) + r_dn_1[...].astype(F32)) * factor
    store(acc.at[3, pl.ds(0, down_rows)], dn_sum)
    mo_r["s1"].wait_recv()
    acc[2, 96 : 96 + rows] = (w_mo[z1, z0, y, c].astype(F32) + r_mo_1[...].astype(F32)) * factor
    store(acc.at[2, pl.ds(96, rows)], mo_sum)
    mi_back = []
    for h in range(2):
        mix_last(*mi_parts[h])
        mi_rs[h]["s1"].wait_recv()
        dabs[h, z1, z0, y, :, c] = plus(dabs[h, z1, z0, y, :, c], r_mi_1[h])
        into = pl.ds(h * columns, columns)
        mi_stage[x, :, into] = dabs[h, z1, z0, y, x, c]
        mi_back.append(go(remote(dabs.at[h, z1, z0, y, 1 - x, c], mi_stage.at[x, :, into], xn)))
    for copy in gu_back:
        copy.wait_recv()
    store(gu_stage, gu_sum)
    for copy in mi_back:
        copy.wait_recv()
    store(mi_stage, mi_sum)

    for copy in stores:
        copy.wait()
    for copy in list(started):
        sent(copy)


COPIES = 160


def finish(
    fsdp_count,
    copies_of_place,
    factor,
    block_sum,
    input_sum,
    small,
    mi_sum,
    mo_sum,
    gu_sum,
    dn_sum,
    mixer_in,
    gain_one,
    block_out,
    input_grad,
    gain_one_grad,
    mixer_in_grad,
    taps_grad,
    mixer_out_grad,
    gain_two_grad,
    gate_grad,
    up_grad,
    down_grad,
):
    input_grad[...] = input_sum[...]
    block_out[...] = block_sum[...]
    down_grad[...] = dn_sum[...]
    mixer_out_grad[...] = mo_sum[...]
    rows, ff = gate_grad.shape
    width = mixer_out_grad.shape[1]
    part, run, half_width = ff // 12, ff // 16, width // 2
    for ref, start in ((gate_grad, 0), (up_grad, part)):
        pieces = [
            jnp.concatenate(
                [gu_sum[at_p, j, :, start : start + part] for j in range(3)], axis=1
            ).astype(F32)
            * factor
            for at_p in range(4)
        ]
        ref[...] = jnp.concatenate(
            [pieces[q % 4][:, run * (q // 4) : run * (q // 4) + run] for q in range(16)], axis=1
        )
    low = lax.broadcasted_iota(jnp.int32, (rows, 128), 1) < 64
    by_row = jnp.zeros((rows, 128), F32)
    for b in range(3):
        for q in range(width // 256):
            at = b * half_width + 128 * q
            first = mi_sum[0, :, at : at + 128].astype(F32) * factor
            second = mi_sum[1, :, at : at + 128].astype(F32) * factor
            to = b * width + 256 * q
            even = jnp.where(low, first, pltpu.roll(second, 64, 1))
            odd = jnp.where(low, pltpu.roll(first, 64, 1), second)
            mixer_in_grad[:, to : to + 128] = even
            mixer_in_grad[:, to + 128 : to + 256] = odd
            by_row += even * mixer_in[:, to : to + 128].astype(F32)
            by_row += odd * mixer_in[:, to + 128 : to + 256].astype(F32)
    column = jnp.sum(by_row, axis=1, keepdims=True)
    every_row = gain_one.shape[1]
    step = pl.program_id(0)
    row_at = lax.broadcasted_iota(jnp.int32, (rows, every_row), 0) + step * rows
    col_at = lax.broadcasted_iota(jnp.int32, (rows, every_row), 1)
    turned = jnp.sum(jnp.where(row_at == col_at, column, 0.0), axis=0, keepdims=True)
    turned = turned / gain_one[...].astype(F32)
    number = lax.axis_index("dp") * fsdp_count + lax.axis_index("fsdp")
    quarter = lax.rem(lax.div(number, copies_of_place), 4)
    values = small[...]
    own = values[:, 0:every_row]
    for k in range(1, 4):
        own = jnp.where(quarter == k, values[:, k * every_row : (k + 1) * every_row], own)

    @pl.when(step == 0)
    def first_step():
        gain_one_grad[...] = turned

    @pl.when(step > 0)
    def later_step():
        gain_one_grad[...] += turned

    gain_two_grad[...] = own[1:2]
    taps_grad[...] = own[2:5]


def per_device(
    fsdp_count,
    device_count,
    tokens,
    document_index,
    loss_token_mask,
    cotangent,
    first_gain,
    mixer_in,
    conv_kernel,
    mixer_out,
    second_gain,
    gate_weight,
    up_weight,
    down_weight,
):
    row_count, seq_here, width = tokens.shape
    toks = row_count * seq_here
    spare = device_count // PLACES
    groups = [[place * spare + k for k in range(spare)] for place in range(PLACES)]
    axes = ("dp", "fsdp")

    def joined(shard, axis=0):
        if spare == 1:
            return shard
        return lax.all_gather(shard, axes, axis=axis, tiled=True, axis_index_groups=groups)

    first_gain, second_gain = joined(first_gain), joined(second_gain)
    conv_kernel = joined(conv_kernel, 1)
    mixer_in, mixer_out = joined(mixer_in), joined(mixer_out)
    gate_weight, up_weight, down_weight = joined(gate_weight), joined(up_weight), joined(down_weight)
    rows = mixer_in.shape[0]
    down_rows = down_weight.shape[0]
    ff = gate_weight.shape[1]
    part = ff // 12
    half_width = width // 2
    wide = 3 * half_width
    factor = 1.0 / math.sqrt(toks * device_count)

    def vm(shape, dtype=BF16):
        return pltpu.VMEM(shape, dtype)

    half = toks // 2
    scratch = [
        vm((toks, width), F32),
        vm((toks, width)),
        vm((rows, 3 * width)),
        vm((rows, ff)),
        vm((rows, ff)),
        vm((8, 128), F32),
        vm((PLACES, 8, 128), F32),
        vm((8, width), F32),
        vm((PLACES + 8, 8, 128), F32),
        vm((2, 2, 2, 2, 2, rows, wide)),
        vm((2, 2, 2, 2, rows, width)),
        vm((3, 2, 2, 4, 2, rows, 2 * part)),
        vm((2, 2, 2, down_rows, width)),
        vm((2, rows, wide)),
        vm((4, 3, rows, 2 * part)),
        vm((2, toks, width)),
        vm((2, toks, 128)),
        vm((4, toks, width)),
        vm((4, toks, width)),
        vm((2, toks, wide), F32),
        vm((2, toks + 8, half_width), F32),
        vm((2, toks, half_width), F32),
        vm((2, toks, half_width)),
        vm((2, toks, wide)),
        vm((toks, width), F32),
        vm((toks, width)),
        vm((toks, width)),
        vm((2, toks + 8, 2 * part), F32),
        vm((2 * toks, part), F32),
        vm((4, toks, 3 * part)),
        vm((3, 2, 2, 2, 2, 2, rows, 2 * part)),
        vm((4, toks, width), F32),
        vm((4, toks, width)),
        vm((half, width)),
        vm((half, width)),
        vm((toks, width)),
        vm((toks, width)),
        vm((2, toks, width)),
        vm((2, 2, 2, 4, rows, 2 * part)),
        vm((3, 2, 4, rows, 2 * part)),
        vm((3, 4, rows, 2 * part)),
        vm((2, 2, down_rows, width)),
        vm((2, down_rows, width)),
        vm((down_rows, width)),
        vm((2, 2, 2, 2, 2, rows, 2 * part)),
        vm((2, 2, 2, 2, rows, 2 * part)),
        vm((2, 2, 2, rows, 2 * part)),
        vm((2, 2, rows, 2 * part)),
        vm((2, 2, 2, rows, width)),
        vm((2, 2, rows, width)),
        vm((2, rows, width)),
        vm((rows, width)),
        vm((8, width + half_width), F32),
        pltpu.SemaphoreType.DMA((COPIES,)),
        pltpu.SemaphoreType.DMA((COPIES,)),
        pltpu.SemaphoreType.DMA((7,)),
        pltpu.SemaphoreType.DMA((20,)),
        pltpu.SemaphoreType.DMA((PLACES,)),
        pltpu.SemaphoreType.DMA((PLACES,)),
        pltpu.SemaphoreType.DMA((PLACES,)),
        pltpu.SemaphoreType.DMA((PLACES,)),
        pltpu.SemaphoreType.REGULAR,
        pltpu.SemaphoreType.REGULAR,
    ]
    outs = [
        jax.ShapeDtypeStruct((toks, width), BF16),
        jax.ShapeDtypeStruct((toks, width), F32),
        jax.ShapeDtypeStruct((8, 128), F32),
        jax.ShapeDtypeStruct((2, rows, wide), BF16),
        jax.ShapeDtypeStruct((rows, width), F32),
        jax.ShapeDtypeStruct((4, 3, rows, 2 * part), BF16),
        jax.ShapeDtypeStruct((down_rows, width), F32),
    ]
    vmem = pl.BlockSpec(memory_space=pltpu.VMEM)
    hbm = pl.BlockSpec(memory_space=pl.ANY)
    result = pl.pallas_call(
        functools.partial(kernel, fsdp_count, spare, factor),
        out_shape=outs,
        in_specs=[hbm] * 2 + [vmem] * 5 + [hbm] * 5,
        out_specs=[hbm] * 2 + [vmem] + [hbm] * 4,
        scratch_shapes=scratch,
        compiler_params=pltpu.CompilerParams(
            collective_id=0, has_side_effects=True, vmem_limit_bytes=60 << 20
        ),
    )(
        tokens.reshape(toks, width),
        cotangent.reshape(toks, width),
        document_index,
        loss_token_mask,
        first_gain.reshape(1, rows),
        second_gain.reshape(1, rows),
        conv_kernel,
        mixer_in,
        mixer_out,
        gate_weight,
        up_weight,
        down_weight,
    )
    def halved(count, columns):
        return pl.BlockSpec((count // 2, columns), lambda i: (i, 0))

    def whole(count, columns):
        return pl.BlockSpec((count, columns), lambda i: (0, 0))

    finished = pl.pallas_call(
        functools.partial(finish, fsdp_count, spare, factor),
        out_shape=[
            jax.ShapeDtypeStruct((toks, width), BF16),
            jax.ShapeDtypeStruct((toks, width), F32),
            jax.ShapeDtypeStruct((1, rows), F32),
            jax.ShapeDtypeStruct((rows, 3 * width), F32),
            jax.ShapeDtypeStruct((3, rows), F32),
            jax.ShapeDtypeStruct((rows, width), F32),
            jax.ShapeDtypeStruct((1, rows), F32),
            jax.ShapeDtypeStruct((rows, ff), F32),
            jax.ShapeDtypeStruct((rows, ff), F32),
            jax.ShapeDtypeStruct((down_rows, width), F32),
        ],
        grid=(2,),
        in_specs=[
            halved(toks, width),
            halved(toks, width),
            whole(8, 128),
            pl.BlockSpec((2, rows // 2, wide), lambda i: (0, i, 0)),
            halved(rows, width),
            pl.BlockSpec((4, 3, rows // 2, 2 * part), lambda i: (0, 0, i, 0)),
            halved(down_rows, width),
            halved(rows, 3 * width),
            whole(1, rows),
        ],
        out_specs=[
            halved(toks, width),
            halved(toks, width),
            whole(1, rows),
            halved(rows, 3 * width),
            whole(3, rows),
            halved(rows, width),
            whole(1, rows),
            halved(rows, ff),
            halved(rows, ff),
            halved(down_rows, width),
        ],
        compiler_params=pltpu.CompilerParams(vmem_limit_bytes=60 << 20),
    )(*result, mixer_in, first_gain.reshape(1, rows))
    block_out, input_grad, g_one, g_mi, g_taps, g_mo, g_two, g_gate, g_up, g_down = finished

    def shared(item, axis=0):
        if spare == 1:
            return item
        return lax.psum_scatter(
            item, axes, scatter_dimension=axis, axis_index_groups=groups, tiled=True
        )

    return (
        block_out.reshape(row_count, seq_here, width),
        input_grad.reshape(row_count, seq_here, width),
        shared(g_one.reshape(rows)),
        shared(g_mi),
        shared(g_taps, 1),
        shared(g_mo),
        shared(g_two.reshape(rows)),
        shared(g_gate),
        shared(g_up),
        shared(g_down),
    )


def solution(mesh):
    fsdp_count = mesh.shape["fsdp"]
    device_count = mesh.shape["dp"] * fsdp_count
    return jax.shard_map(
        functools.partial(per_device, fsdp_count, device_count),
        mesh=mesh,
        in_specs=(
            P("dp", "fsdp", None),
            P("dp", None),
            P("dp", "fsdp"),
            P("dp", "fsdp", None),
            P(("dp", "fsdp")),
            P(("dp", "fsdp"), None),
            P(None, ("dp", "fsdp")),
            P(("dp", "fsdp"), None),
            P(("dp", "fsdp")),
            P(("dp", "fsdp"), None),
            P(("dp", "fsdp"), None),
            P(("dp", "fsdp"), None),
        ),
        out_specs=(
            P("dp", "fsdp", None),
            P("dp", "fsdp", None),
            P(("dp", "fsdp")),
            P(("dp", "fsdp"), None),
            P(None, ("dp", "fsdp")),
            P(("dp", "fsdp"), None),
            P(("dp", "fsdp")),
            P(("dp", "fsdp"), None),
            P(("dp", "fsdp"), None),
            P(("dp", "fsdp"), None),
        ),
        check_vma=False,
    )
```
